32 devices in a mesh: dp: 4 (over y, core), ctx: 8 (over z, x).
Axes of the slice: x: 2, y: 2, z: 4, core: 2. Of those that a mesh axis runs over, the one named last changes fastest.
Arguments:
- inputs: bfloat16 [4, 1024, 2048], P('dp', 'ctx'), may hold values from -6 to 6
- positions: int32 [4, 1024], P('dp', 'ctx'), may hold values from 0 to 3070, as said below
- seq_ids: int32 [4, 1024], P('dp', 'ctx'), may hold values from 0 to 2, as said below
- ln_gain: bfloat16 [2048], P('dp'), may hold values from 0.5 to 1.5
- ln_bias: bfloat16 [2048], P('dp'), may hold values from -0.625 to 0.625
- w_qkv: bfloat16 [2048, 6144], P('dp'), may hold values from -0.125 to 0.125
- b_qkv: bfloat16 [6144], P('dp'), may hold values from -0.1875 to 0.1875
- w_dense: bfloat16 [2048, 2048], P('dp'), may hold values from -1 to 1
- b_dense: bfloat16 [2048], P('dp'), may hold values from -0.625 to 0.625
- w_fc1: bfloat16 [2048, 8192], P('dp'), may hold values from -0.125 to 0.125
- b_fc1: bfloat16 [8192], P('dp'), may hold values from -0.625 to 0.625
- w_fc2: bfloat16 [8192, 2048], P('dp'), may hold values from -0.0625 to 0.0625
- b_fc2: bfloat16 [2048], P('dp'), may hold values from -0.625 to 0.625
- cotangent: bfloat16 [4, 1024, 2048], P('dp', 'ctx'), may hold values from -6 to 6
Outputs:
- outputs: bfloat16 [4, 1024, 2048], P('dp', 'ctx')
- input_grad: bfloat16 [4, 1024, 2048], P('dp', 'ctx')
- ln_gain_grad: float32 [2048], P(('dp', 'ctx'))
- ln_bias_grad: float32 [2048], P(('dp', 'ctx'))
- w_qkv_grad: float32 [2048, 6144], P(('dp', 'ctx'))
- b_qkv_grad: float32 [6144], P(('dp', 'ctx'))
- w_dense_grad: float32 [2048, 2048], P(('dp', 'ctx'))
- b_dense_grad: float32 [2048], P(('dp', 'ctx'))
- w_fc1_grad: float32 [2048, 8192], P(('dp', 'ctx'))
- b_fc1_grad: float32 [8192], P(('dp', 'ctx'))
- w_fc2_grad: float32 [8192, 2048], P(('dp', 'ctx'))
- b_fc2_grad: float32 [2048], P(('dp', 'ctx'))
The draws below stay inside these ranges and needn't reach their ends.
Inputs may be any that keep to these rules, and one draw needn't show every extreme that they name: `seq_ids`: each stream holds the documents 0, 1, 2 in this order, each non-empty; documents 0 and 2 have fewer than 128 tokens. Within a document positions rise by one from token to token; document 1 starts at position 0; document 0 ends at position 3070, document 2 at or below it.
All inputs are finite; a program needn't handle non-finite values.
Results may differ from the reference program's by a relative error of at most 0.0095.
Values may be sent and summed in bfloat16 or wider, within the bound.
A program may use at most 448 MiB of HBM per device.

```python
import math
import jax
import jax.numpy as jnp
from jax import lax

D = 2048
FF = 8192
HEAD_DIM = 64
ROT = 32
TOK_DEV = 128
STREAM = 1024
SEQS = 4


def document_bounds(key):
    first_key, last_key = jax.random.split(key)
    head_len = jax.random.randint(first_key, (SEQS, 1), 1, TOK_DEV)
    tail_len = jax.random.randint(last_key, (SEQS, 1), 1, TOK_DEV)
    stream_index = jnp.arange(STREAM, dtype=jnp.int32)[None, :]
    doc_ids = (stream_index >= head_len).astype(jnp.int32) + (stream_index >= STREAM - tail_len).astype(jnp.int32)
    doc_starts = jnp.concatenate([jnp.zeros_like(head_len), head_len, STREAM - tail_len], axis=1)
    return (doc_ids, doc_starts, head_len, tail_len)


def draw_seq_ids(key, part):
    doc_ids, doc_starts, head_len, tail_len = document_bounds(key)
    return doc_ids


def draw_positions(key, part):
    doc_ids, doc_starts, head_len, tail_len = document_bounds(key)
    key = jax.random.fold_in(key, 11)
    first_offset = STREAM + 2047 - head_len
    last_offset = jax.random.randint(key, (SEQS, 1), 0, STREAM + 2048 - tail_len)
    offsets = jnp.concatenate([first_offset, jnp.zeros_like(head_len), last_offset], axis=1)
    shifts = offsets - doc_starts
    picked = jnp.take_along_axis(shifts, doc_ids, axis=1)
    return jnp.arange(STREAM, dtype=jnp.int32)[None, :] + picked


def shard_levels(stream_key, shape, pieces, low, largest):
    def one(position, parts):
        heights = jax.random.uniform(jax.random.fold_in(jax.random.fold_in(stream_key, 6), position), (parts,), jnp.float32, low / len(pieces), largest / len(pieces))
        return jnp.repeat(jnp.exp(heights), shape[position] // parts).reshape((-1,) + (1,) * (len(shape) - position - 1))

    factor_of = one(*pieces[0])
    for cut in pieces[1:]:
        factor_of = factor_of * one(*cut)
    return factor_of


def centred(stream_key, dims, scale, bound, pieces=(), held_as=jnp.bfloat16):
    gain = shard_levels(stream_key, dims, pieces, -0.22, 0.18) if pieces else 1.0
    values = jax.random.normal(stream_key, dims, jnp.float32) * scale * gain
    return jnp.minimum(jnp.maximum(values, -bound), bound).astype(held_as)


def setup_inputs(seed: int = 0) -> dict:
    streams_of = jax.random.split(jax.random.key(seed), 15)
    inputs = centred(streams_of[0], (SEQS, STREAM, D), 1.0, 6.0, ((0, 4), (1, 8)))
    positions = draw_positions(jax.random.fold_in(streams_of[14], 71), 0)
    seq_ids = draw_seq_ids(jax.random.fold_in(streams_of[14], 71), 0)
    ln_gain = jnp.clip(1.0 + 0.1 * jax.random.normal(streams_of[3], (D,), jnp.float32), 0.5, 1.5).astype(jnp.bfloat16)
    ln_bias = centred(streams_of[4], (D,), 0.1, 0.625, ((0, 4),))
    w_qkv = centred(streams_of[5], (D, 3 * D), D ** -0.5, 0.125, ((0, 4),))
    b_qkv = centred(streams_of[6], (3 * D,), 0.03, 0.1875, ((0, 4),))
    w_dense = centred(streams_of[7], (D, D), (D // 64) ** -0.5, 1.0, ((0, 4),))
    b_dense = centred(streams_of[8], (D,), 0.1, 0.625, ((0, 4),))
    w_fc1 = centred(streams_of[9], (D, FF), D ** -0.5, 0.125, ((0, 4),))
    b_fc1 = centred(streams_of[10], (FF,), 0.1, 0.625, ((0, 4),))
    w_fc2 = centred(streams_of[11], (FF, D), FF ** -0.5, 0.0625, ((0, 4),))
    b_fc2 = centred(streams_of[12], (D,), 0.1, 0.625, ((0, 4),))
    cotangent = centred(streams_of[13], (SEQS, STREAM, D), 1.0, 6.0, ((0, 4), (1, 8)))
    return {"inputs": inputs, "positions": positions, "seq_ids": seq_ids, "ln_gain": ln_gain, "ln_bias": ln_bias, "w_qkv": w_qkv, "b_qkv": b_qkv, "w_dense": w_dense, "b_dense": b_dense, "w_fc1": w_fc1, "b_fc1": b_fc1, "w_fc2": w_fc2, "b_fc2": b_fc2, "cotangent": cotangent}


EPS = 1e-05
MASKED = -1e+30
SCALE = 0.125
BASE = 10000.0
PRECISE = lax.Precision.HIGHEST

@jax.custom_vjp
def low(v):
    return lax.optimization_barrier(v.astype(jnp.bfloat16)).astype(jnp.float32)

@jax.custom_vjp
def low_back(v):
    return v

def low_keep(v):
    return (low(v), None)

def low_pass(kept, grad):
    return (grad,)

def back_keep(v):
    return (v, None)

def back_low(kept, grad):
    return (low(grad),)
low.defvjp(low_keep, low_pass)
low_back.defvjp(back_keep, back_low)

def rotate(values, angle_pos):
    row_count = values.shape[0]
    head_count = values.shape[1] // HEAD_DIM
    half_rot = ROT // 2
    split_heads = values.reshape(row_count, head_count, HEAD_DIM)
    freqs = BASE ** (-(jnp.arange(half_rot, dtype=jnp.float32) * 2.0) / ROT)
    angles = angle_pos[:, None] * freqs[None, :]
    cosine = jnp.cos(angles)[:, None, :]
    sine = jnp.sin(angles)[:, None, :]
    first_half = split_heads[:, :, :half_rot]
    second_half = split_heads[:, :, half_rot:ROT]
    turned = jnp.concatenate([first_half * cosine - second_half * sine, second_half * cosine + first_half * sine, split_heads[:, :, ROT:]], axis=2)
    return turned.reshape(row_count, head_count * HEAD_DIM)

def visible(query_index, query_seg, key_index, key_seg):
    return (key_index[None, :] <= query_index[:, None]) & (key_seg[None, :] == query_seg[:, None])

def layer(resid, ln_gain, ln_bias, w_qkv, b_qkv, w_dense, b_dense, w_fc1, b_fc1, w_fc2, b_fc2, angle_pos, seg_row):
    length = resid.shape[0]
    width = resid.shape[1]
    head_count = width // HEAD_DIM
    center = resid - lax.optimization_barrier(jnp.mean(resid, axis=1, keepdims=True))
    spread = lax.optimization_barrier(jnp.mean(center * center, axis=1, keepdims=True))
    normed = low(center * lax.rsqrt(spread + EPS) * ln_gain + ln_bias)
    joint = low_back(jnp.dot(normed, w_qkv, precision=PRECISE) + b_qkv)
    queries = low(rotate(joint[:, :width], angle_pos))
    key_heads = low(rotate(joint[:, width:2 * width], angle_pos)).reshape(length, head_count, HEAD_DIM)
    value_heads = low(joint[:, 2 * width:]).reshape(length, head_count, HEAD_DIM)
    block = math.gcd(length, 512)
    block_count = length // block
    full_index = jnp.arange(length, dtype=jnp.int32)

    def attend(block_args):
        block_query, block_index, block_seg = block_args
        scores = low_back(jnp.einsum('qhd,khd->hqk', block_query.reshape(block, head_count, HEAD_DIM), key_heads, precision=PRECISE) * SCALE)
        allowed = visible(block_index, block_seg, full_index, seg_row)
        weights = jax.nn.softmax(jnp.where(allowed[None], scores, MASKED), axis=2)
        probs = low(weights)
        return jnp.einsum('hqk,khd->qhd', probs, value_heads, precision=PRECISE).reshape(block, width)
    attended = lax.map(jax.checkpoint(attend), (queries.reshape(block_count, block, width), full_index.reshape(block_count, block), seg_row.reshape(block_count, block)))
    mixed = low_back(low(attended.reshape(length, width)))
    attn_out = jnp.dot(mixed, w_dense, precision=PRECISE) + b_dense
    inner = low_back(jnp.dot(normed, w_fc1, precision=PRECISE) + b_fc1)
    active = low(jax.nn.gelu(inner, approximate=True))
    mlp_out = jnp.dot(active, w_fc2, precision=PRECISE) + b_fc2
    return resid + attn_out + mlp_out

def reference(inputs, positions, seq_ids, ln_gain, ln_bias, w_qkv, b_qkv, w_dense, b_dense, w_fc1, b_fc1, w_fc2, b_fc2, cotangent):
    params = (ln_gain.astype(jnp.float32), ln_bias.astype(jnp.float32), w_qkv.astype(jnp.float32), b_qkv.astype(jnp.float32), w_dense.astype(jnp.float32), b_dense.astype(jnp.float32), w_fc1.astype(jnp.float32), b_fc1.astype(jnp.float32), w_fc2.astype(jnp.float32), b_fc2.astype(jnp.float32))

    def one_stream(carry, items):
        stream_in, stream_pos, stream_seg, stream_cot = items
        angle_pos = stream_pos.astype(jnp.float32)

        def forward(resid, *weights_in):
            return layer(resid, *weights_in, angle_pos, stream_seg)
        result, back = jax.vjp(forward, stream_in.astype(jnp.float32), *params)
        grads = back(stream_cot.astype(jnp.float32))
        summed = tuple((total + piece for total, piece in zip(carry, grads[1:])))
        return (summed, (result.astype(jnp.bfloat16), grads[0].astype(jnp.bfloat16)))
    start_sums = tuple((jnp.zeros(param.shape, jnp.float32) for param in params))
    totals, (outputs, input_grad) = lax.scan(one_stream, start_sums, (inputs, positions, seq_ids, cotangent))
    return (outputs, input_grad, totals[0], totals[1], totals[2], totals[3], totals[4], totals[5], totals[6], totals[7], totals[8], totals[9])
```

```python
import math

import jax
import jax.numpy as jnp
import numpy as np
from jax import lax
from jax.experimental import pallas as pl
from jax.experimental.pallas import tpu as pltpu
from jax.sharding import PartitionSpec as P

HEAD_DIM = 64
ROT = 32


EPS = 1e-05
MASKED = -1e30
SCALE = 0.125
BASE = 10000.0


def layer_norm(values, gain_vec, shift_vec):
    center = values - jnp.mean(values, axis=1, keepdims=True)
    spread = jnp.mean(center * center, axis=1, keepdims=True)
    return center * lax.rsqrt(spread + EPS) * gain_vec + shift_vec


def gelu_tanh(values):
    return jax.nn.gelu(values, approximate=True)


def rotate(values, angle_pos):
    row_count = values.shape[0]
    head_count = values.shape[1] // HEAD_DIM
    half_rot = ROT // 2
    split_heads = values.reshape(row_count, head_count, HEAD_DIM)
    freqs = BASE ** (-(jnp.arange(half_rot, dtype=jnp.float32) * 2.0) / ROT)
    angles = angle_pos[:, None] * freqs[None, :]
    cosine = jnp.cos(angles)[:, None, :]
    sine = jnp.sin(angles)[:, None, :]
    first_half = split_heads[:, :, :half_rot]
    second_half = split_heads[:, :, half_rot:ROT]
    turned = jnp.concatenate(
        [
            first_half * cosine - second_half * sine,
            second_half * cosine + first_half * sine,
            split_heads[:, :, ROT:],
        ],
        axis=2,
    )
    return turned.reshape(row_count, head_count * HEAD_DIM)


def visible(query_index, query_seg, key_index, key_seg):
    causal = key_index[None, :] <= query_index[:, None]
    return causal[None] & (key_seg[:, None, :] == query_seg[:, :, None])


def split_cols(values, low_col, high_col):
    return values[:, :, low_col:high_col].reshape(
        values.shape[0], values.shape[1], (high_col - low_col) // HEAD_DIM, HEAD_DIM
    )


def head_scores(query_heads, key_heads, allowed):
    raw = (
        jnp.einsum("sqhd,skhd->shqk", query_heads, key_heads, preferred_element_type=jnp.float32)
        * SCALE
    )
    return jnp.where(allowed[:, None], raw, MASKED)


def unchanged(state):
    return state


def per_device(
    inputs,
    positions,
    seq_ids,
    ln_gain,
    ln_bias,
    w_qkv,
    b_qkv,
    w_dense,
    b_dense,
    w_fc1,
    b_fc1,
    w_fc2,
    b_fc2,
    cotangent,
):
    (
        gain_all,
        shift_all,
        qkv_all,
        qkv_offset,
        dense_all,
        dense_offset,
        fc1_all,
        fc1_offset,
        fc2_all,
        fc2_offset,
    ) = (
        lax.all_gather(ln_gain, "dp", axis=0, tiled=True),
        lax.all_gather(ln_bias, "dp", axis=0, tiled=True),
        lax.all_gather(w_qkv, "dp", axis=0, tiled=True),
        lax.all_gather(b_qkv, "dp", axis=0, tiled=True),
        lax.all_gather(w_dense, "dp", axis=0, tiled=True),
        lax.all_gather(b_dense, "dp", axis=0, tiled=True),
        lax.all_gather(w_fc1, "dp", axis=0, tiled=True),
        lax.all_gather(b_fc1, "dp", axis=0, tiled=True),
        lax.all_gather(w_fc2, "dp", axis=0, tiled=True),
        lax.all_gather(b_fc2, "dp", axis=0, tiled=True),
    )
    stream_count = inputs.shape[0]
    row_count = inputs.shape[1]
    width = inputs.shape[2]
    flat_rows = stream_count * row_count
    resid = inputs.reshape(flat_rows, width).astype(jnp.float32)
    head_count = width // HEAD_DIM
    group_heads = math.gcd(head_count, 8)
    group_cols = group_heads * HEAD_DIM
    group_count = head_count // group_heads
    angle_pos = positions.reshape(flat_rows).astype(jnp.float32)
    own_seg = seq_ids.astype(jnp.bfloat16)
    row_start = lax.axis_index("ctx") * row_count
    own_index = row_start + jnp.arange(row_count, dtype=jnp.int32)
    normed, norm_back = jax.vjp(
        layer_norm, resid, gain_all.astype(jnp.float32), shift_all.astype(jnp.float32)
    )
    hidden = normed.astype(jnp.bfloat16)
    joint = jnp.dot(hidden, qkv_all, preferred_element_type=jnp.float32) + qkv_offset.astype(
        jnp.float32
    )
    queries = (
        rotate(joint[:, :width], angle_pos)
        .astype(jnp.bfloat16)
        .reshape(stream_count, row_count, width)
    )
    keys_own = (
        rotate(joint[:, width : 2 * width], angle_pos)
        .astype(jnp.bfloat16)
        .reshape(stream_count, row_count, width)
    )
    values_own = joint[:, 2 * width :].astype(jnp.bfloat16).reshape(stream_count, row_count, width)
    start_state = (
        jnp.full((stream_count, head_count, row_count), MASKED, jnp.float32),
        jnp.zeros((stream_count, head_count, row_count), jnp.float32),
        jnp.zeros((stream_count, row_count, width), jnp.float32),
    )
    key_part = lax.all_gather(keys_own, "ctx", axis=1, tiled=True)
    value_part = lax.all_gather(values_own, "ctx", axis=1, tiled=True)
    seg_part = lax.all_gather(own_seg, "ctx", axis=1, tiled=True)
    key_count = key_part.shape[1]
    allowed = visible(own_index, own_seg, jnp.arange(key_count, dtype=jnp.int32), seg_part)

    def forward_compute(state):
        peak_in, total_in, accum_in = state
        peak_list, total_list, accum_list = ([], [], [])
        for group_index in range(group_count):
            low_col = group_index * group_cols
            high_col = low_col + group_cols
            low_head = group_index * group_heads
            high_head = low_head + group_heads
            scores = head_scores(
                split_cols(queries, low_col, high_col),
                split_cols(key_part, low_col, high_col),
                allowed,
            )
            old_peak = peak_in[:, low_head:high_head]
            new_peak = jnp.maximum(old_peak, jnp.max(scores, axis=3))
            weights = jnp.where(allowed[:, None], jnp.exp(scores - new_peak[:, :, :, None]), 0.0)
            total_list.append(jnp.sum(weights, axis=3))
            gathered_vals = jnp.einsum(
                "shqk,skhd->sqhd",
                weights.astype(jnp.bfloat16),
                split_cols(value_part, low_col, high_col),
                preferred_element_type=jnp.float32,
            )
            accum_list.append(gathered_vals.reshape(stream_count, row_count, group_cols))
            peak_list.append(new_peak)
        return (
            jnp.concatenate(peak_list, 1),
            jnp.concatenate(total_list, 1),
            jnp.concatenate(accum_list, 2),
        )

    result_state = lax.cond(
        jnp.int32(0) < row_start + row_count, forward_compute, unchanged, start_state
    )
    peak, total, accum = result_state
    attended = (
        accum.reshape(stream_count, row_count, head_count, HEAD_DIM)
        / jnp.transpose(total, (0, 2, 1))[:, :, :, None]
    ).reshape(stream_count, row_count, width)
    log_total = jnp.transpose(peak + jnp.log(total), (0, 2, 1))
    mixed = attended.astype(jnp.bfloat16).reshape(flat_rows, width)
    inner = jnp.dot(hidden, fc1_all, preferred_element_type=jnp.float32) + fc1_offset.astype(
        jnp.float32
    )
    active, gelu_back = jax.vjp(gelu_tanh, inner)
    active_low = active.astype(jnp.bfloat16)
    summed = (
        resid
        + jnp.dot(mixed, dense_all, preferred_element_type=jnp.float32)
        + dense_offset.astype(jnp.float32)
    )
    summed = (
        summed
        + jnp.dot(active_low, fc2_all, preferred_element_type=jnp.float32)
        + fc2_offset.astype(jnp.float32)
    )
    outputs = summed.astype(jnp.bfloat16).reshape(stream_count, row_count, width)
    upstream = cotangent.reshape(flat_rows, width)
    upstream_f = upstream.astype(jnp.float32)
    bias_term = jnp.sum(upstream_f, axis=0)
    fc2_term = jnp.einsum("tf,td->fd", active_low, upstream, preferred_element_type=jnp.float32)
    fc2_sum = lax.psum_scatter(fc2_term, ("dp", "ctx"), scatter_dimension=0, tiled=True)
    fc2_sum, upstream = lax.optimization_barrier((fc2_sum, upstream))
    act_grad = jnp.einsum("td,fd->tf", upstream, fc2_all, preferred_element_type=jnp.float32)
    inner_grad = gelu_back(act_grad)[0].astype(jnp.bfloat16)
    fc1_term = jnp.einsum("td,tf->df", hidden, inner_grad, preferred_element_type=jnp.float32)
    fc1_bias_term = jnp.sum(inner_grad.astype(jnp.float32), axis=0)
    fc1_sum = lax.psum_scatter(fc1_term, ("dp", "ctx"), scatter_dimension=0, tiled=True)
    fc1_sum, mixed, upstream, upstream_f, fc1_bias_term, inner_grad, hidden = lax.optimization_barrier(
        (fc1_sum, mixed, upstream, upstream_f, fc1_bias_term, inner_grad, hidden)
    )
    fc1_bias_sum, bias_sum = (
        lax.psum_scatter(fc1_bias_term, ("dp", "ctx"), scatter_dimension=0, tiled=True),
        lax.psum_scatter(bias_term, ("dp", "ctx"), scatter_dimension=0, tiled=True),
    )
    dense_term = jnp.einsum("td,te->de", mixed, upstream, preferred_element_type=jnp.float32)
    dense_sum = lax.psum_scatter(dense_term, ("dp", "ctx"), scatter_dimension=0, tiled=True)
    dense_sum, upstream, dense_all = lax.optimization_barrier((dense_sum, upstream, dense_all))
    mixed_grad = (
        jnp.einsum("te,de->td", upstream, dense_all, preferred_element_type=jnp.float32)
        .astype(jnp.bfloat16)
        .reshape(stream_count, row_count, width)
    )
    delta = jnp.sum(
        (mixed_grad.astype(jnp.float32) * attended).reshape(
            stream_count, row_count, head_count, HEAD_DIM
        ),
        axis=3,
    )
    zero_block = jnp.zeros((stream_count, row_count, width), jnp.float32)
    query_key_part = lax.all_gather(keys_own, "ctx", axis=1, tiled=True)
    query_value_part = lax.all_gather(values_own, "ctx", axis=1, tiled=True)
    seg_part = lax.all_gather(own_seg, "ctx", axis=1, tiled=True)
    key_count = query_key_part.shape[1]
    query_allowed = visible(own_index, own_seg, jnp.arange(key_count, dtype=jnp.int32), seg_part)

    def query_compute(grad_in):
        step_list = []
        for group_index in range(group_count):
            low_col = group_index * group_cols
            high_col = low_col + group_cols
            low_head = group_index * group_heads
            high_head = low_head + group_heads
            scores = head_scores(
                split_cols(queries, low_col, high_col),
                split_cols(query_key_part, low_col, high_col),
                query_allowed,
            )
            lse_here = jnp.transpose(log_total[:, :, low_head:high_head], (0, 2, 1))[:, :, :, None]
            delta_here = jnp.transpose(delta[:, :, low_head:high_head], (0, 2, 1))[:, :, :, None]
            probs = jnp.where(query_allowed[:, None], jnp.exp(scores - lse_here), 0.0)
            prob_grad = jnp.einsum(
                "sqhd,skhd->shqk",
                split_cols(mixed_grad, low_col, high_col),
                split_cols(query_value_part, low_col, high_col),
                preferred_element_type=jnp.float32,
            )
            score_grad = (probs * (prob_grad - delta_here)).astype(jnp.bfloat16)
            query_step = (
                jnp.einsum(
                    "shqk,skhd->sqhd",
                    score_grad,
                    split_cols(query_key_part, low_col, high_col),
                    preferred_element_type=jnp.float32,
                )
                * SCALE
            )
            step_list.append(query_step.reshape(stream_count, row_count, group_cols))
        return grad_in + jnp.concatenate(step_list, 2)

    result_grad = lax.cond(
        jnp.int32(0) < row_start + row_count, query_compute, unchanged, zero_block
    )
    log_total_all, delta_all = (
        lax.all_gather(log_total, "ctx", axis=1, tiled=True),
        lax.all_gather(delta, "ctx", axis=1, tiled=True),
    )
    start = jnp.int32(0)
    query_part = lax.all_gather(queries, "ctx", axis=1, tiled=True)
    grad_part = lax.all_gather(mixed_grad, "ctx", axis=1, tiled=True)
    seg_part = lax.all_gather(own_seg, "ctx", axis=1, tiled=True)
    query_count = query_part.shape[1]
    query_index = jnp.arange(query_count, dtype=jnp.int32)
    key_allowed = visible(query_index, seg_part, own_index, own_seg)
    lse_part = lax.dynamic_slice_in_dim(log_total_all, start, query_count, 1)

    def key_compute(state):
        key_in, value_in = state
        key_list, value_list = ([], [])
        for group_index in range(group_count):
            low_col = group_index * group_cols
            high_col = low_col + group_cols
            low_head = group_index * group_heads
            high_head = low_head + group_heads
            scores = head_scores(
                split_cols(query_part, low_col, high_col),
                split_cols(keys_own, low_col, high_col),
                key_allowed,
            )
            lse_here = jnp.transpose(lse_part[:, :, low_head:high_head], (0, 2, 1))[:, :, :, None]
            delta_here = jnp.transpose(delta_all[:, :, low_head:high_head], (0, 2, 1))[
                :, :, :, None
            ]
            probs = jnp.where(key_allowed[:, None], jnp.exp(scores - lse_here), 0.0)
            grad_heads = split_cols(grad_part, low_col, high_col)
            value_step = jnp.einsum(
                "shqk,sqhd->skhd",
                probs.astype(jnp.bfloat16),
                grad_heads,
                preferred_element_type=jnp.float32,
            )
            prob_grad = jnp.einsum(
                "sqhd,skhd->shqk",
                grad_heads,
                split_cols(values_own, low_col, high_col),
                preferred_element_type=jnp.float32,
            )
            score_grad = (probs * (prob_grad - delta_here)).astype(jnp.bfloat16)
            key_step = (
                jnp.einsum(
                    "shqk,sqhd->skhd",
                    score_grad,
                    split_cols(query_part, low_col, high_col),
                    preferred_element_type=jnp.float32,
                )
                * SCALE
            )
            key_list.append(key_step.reshape(stream_count, row_count, group_cols))
            value_list.append(value_step.reshape(stream_count, row_count, group_cols))
        return (key_in + jnp.concatenate(key_list, 2), value_in + jnp.concatenate(value_list, 2))

    result_pair = lax.cond(
        start + query_count > row_start, key_compute, unchanged, (zero_block, zero_block)
    )
    key_grad, value_grad = result_pair
    joint_grad = jnp.concatenate(
        [
            rotate(result_grad.reshape(flat_rows, width), -angle_pos),
            rotate(key_grad.reshape(flat_rows, width), -angle_pos),
            value_grad.reshape(flat_rows, width),
        ],
        axis=1,
    ).astype(jnp.bfloat16)
    qkv_term = jnp.einsum("td,te->de", hidden, joint_grad, preferred_element_type=jnp.float32)
    qkv_bias_term = jnp.sum(joint_grad.astype(jnp.float32), axis=0)
    hidden_grad = jnp.einsum("te,de->td", joint_grad, qkv_all, preferred_element_type=jnp.float32)
    hidden_grad = hidden_grad + jnp.einsum(
        "tf,df->td", inner_grad, fc1_all, preferred_element_type=jnp.float32
    )
    resid_grad, gain_term, shift_term = norm_back(hidden_grad)
    input_grad = (
        (upstream_f + resid_grad).astype(jnp.bfloat16).reshape(stream_count, row_count, width)
    )
    gain_sum, shift_sum, qkv_sum, qkv_bias_sum = (
        lax.psum_scatter(gain_term, ("dp", "ctx"), scatter_dimension=0, tiled=True),
        lax.psum_scatter(shift_term, ("dp", "ctx"), scatter_dimension=0, tiled=True),
        lax.psum_scatter(qkv_term, ("dp", "ctx"), scatter_dimension=0, tiled=True),
        lax.psum_scatter(qkv_bias_term, ("dp", "ctx"), scatter_dimension=0, tiled=True),
    )
    return (
        outputs,
        input_grad,
        gain_sum,
        shift_sum,
        qkv_sum,
        qkv_bias_sum,
        dense_sum,
        bias_sum,
        fc1_sum,
        fc1_bias_sum,
        fc2_sum,
        bias_sum,
    )


BF = jnp.bfloat16
F32 = jnp.float32
BLK = 128
PAIR = 256
NC = 8
ND = 4
TOK = NC * BLK
HEADS_C = 4
MESH_ID = pl.DeviceIdType.MESH
GELU_A = 0.044715
GELU_K = math.sqrt(2.0 / math.pi)

R_N, R_G, R_M, R_V = 0, 8, 16, 24
R_WY, R_WC, R_WF = 28, 32, 36
R_X = (40, 44)
R_Z = (48, 53)
R_C, R_Y = 58, 66
R_A1, R_AQ, R_PC, R_PD = 70, 78, 86, 94
N_RECV = 98
N_SEND = 112
FREQS = [float(np.float32(BASE) ** np.float32(-2.0 * i / ROT)) for i in range(ROT // 2)]


def dot_nn(a, b):
    return lax.dot_general(a, b, (((1,), (0,)), ((), ())), preferred_element_type=F32)


def dot_nt(a, b):
    return lax.dot_general(a, b, (((1,), (1,)), ((), ())), preferred_element_type=F32)


def transposed(v):
    return jnp.transpose(v)


def swap_turned(v):
    lane = lax.broadcasted_iota(jnp.int32, v.shape, 1) % HEAD_DIM
    return jnp.where(lane < 16, pltpu.roll(v, 112, 1), pltpu.roll(v, 16, 1))


def as_rows(v):
    return jnp.concatenate([v[:, i * 128 : (i + 1) * 128] for i in range(v.shape[1] // 128)], 0)


def as_row(v):
    return jnp.concatenate([v[i : i + 1] for i in range(v.shape[0])], 1)


def own_lanes(row, width, index, count):
    total = jnp.zeros((1, width), F32)
    for i in range(count):
        total = total + jnp.where(index == i, row[:, i * width : (i + 1) * width], 0.0)
    return total


def layer_kernel(
    x_ref,
    g_ref,
    seg_ref,
    pos_ref,
    gain_ref,
    shift_ref,
    bd_ref,
    b2_ref,
    bq_ref,
    b1_ref,
    wq_ref,
    w1_ref,
    w2_ref,
    wd_ref,
    out_ref,
    xgrad_ref,
    small_ref,
    w2s_ref,
    wds_ref,
    a1_ref,
    aq_ref,
    nb,
    gb,
    wq,
    w1,
    w2,
    wd,
    vbuf,
    mbuf,
    ctab,
    stab,
    qstart,
    qh,
    kh,
    vh,
    k_t,
    v_t,
    o_t,
    lse,
    delta,
    mixed,
    act,
    ig,
    d_out,
    jg,
    dka,
    dva,
    svec,
    outp,
    rx,
    rz,
    acc,
    cw,
    cq,
    cd,
    a1,
    aq,
    pkc,
    pkd,
    tb,
    ssem,
    rsem,
    lsem,
    xfree,
    zfree,
    cfree,
    yfree,
):
    dp = lax.axis_index("dp")
    c = lax.axis_index("ctx")
    core = dp % 2
    y = dp // 2
    xx = c % 2
    z = c // 2
    cx = z * 2 + (1 - xx)
    mid = (z == 1) | (z == 2)
    end = (z == 0) | (z == 3)
    far = jnp.where(z < 2, 1, 0)
    zp = [z, z + 1 - 2 * (z % 2), 1 + far, 3 * far]
    dp_core = y * 2 + (1 - core)
    dp_y = (1 - y) * 2 + core
    dp_diag = (1 - y) * 2 + (1 - core)
    to_x = (dp, cx)
    to_outer = (dp, zp[1] * 2 + xx)
    to_inner = (dp, jnp.where(mid, 3 - z, zp[1]) * 2 + xx)
    to_core = (dp_core, c)
    to_y = (dp_y, c)
    dp_peers = [dp_core, dp_y, dp_diag]
    ctx_peers = [(c + o) % NC for o in range(1, NC)]
    pending = []
    counter = [0]

    def rows_of(i, n):
        return pl.ds(pl.multiple_of(i * n, n), n)

    def send(src, dst, ridx, dev, sidx=None):
        if sidx is None:
            sidx = counter[0]
            counter[0] += 1
        copy = pltpu.make_async_remote_copy(
            src_ref=src,
            dst_ref=dst,
            send_sem=ssem.at[sidx],
            recv_sem=rsem.at[ridx],
            device_id=dev,
            device_id_type=MESH_ID,
        )
        copy.start()
        return copy

    def new_send():
        counter[0] += 1
        return counter[0] - 1

    def got(dst, ridx):
        pltpu.make_async_remote_copy(
            src_ref=dst,
            dst_ref=dst,
            send_sem=ssem.at[0],
            recv_sem=rsem.at[ridx],
            device_id=to_x,
            device_id_type=MESH_ID,
        ).wait_recv()

    def sent(src, sidx):
        pltpu.make_async_remote_copy(
            src_ref=src,
            dst_ref=src,
            send_sem=ssem.at[sidx],
            recv_sem=rsem.at[0],
            device_id=to_x,
            device_id_type=MESH_ID,
        ).wait_send()

    def signal(sem, dev):
        pl.semaphore_signal(sem, inc=1, device_id=dev, device_id_type=MESH_ID)

    barrier = pltpu.get_barrier_semaphore()
    for p in dp_peers:
        signal(barrier, (p, c))
    for p in ctx_peers:
        signal(barrier, (dp, p))
    pl.semaphore_wait(barrier, len(dp_peers) + len(ctx_peers))

    pair_cols = outp.at[pl.ds(0, 512)]
    for i in range(12):
        pltpu.make_async_copy(
            wq_ref.at[:, pl.ds(pl.multiple_of(i * 512 + z * 128, 128), 128)],
            pair_cols.at[:, pl.ds(i * 128, 128)],
            lsem.at[0],
        ).start()

    def row_of(ref):
        return ref[...].astype(F32).reshape(1, ref.shape[0])

    bq_all = row_of(bq_ref)
    bq_own = [own_lanes(bq_all[:, j * 512 : (j + 1) * 512], 64, c, NC) for j in range(3)]
    b1_own = own_lanes(row_of(b1_ref), 256, c, NC)
    wide = [row_of(r) for r in (gain_ref, shift_ref, bd_ref, b2_ref)]
    wide += [jnp.concatenate(bq_own + [jnp.zeros((1, 320), F32)], 1)]
    wide += [jnp.concatenate([b1_own, jnp.zeros((1, 256), F32)], 1)]
    vbuf[dp] = jnp.concatenate(wide + [jnp.zeros((10, 512), F32)], 0).astype(BF)
    mbuf[c] = jnp.concatenate([seg_ref[...], pos_ref[...], jnp.zeros((6, BLK), jnp.int32)], 0)
    for p in dp_peers:
        pending.append(send(vbuf.at[dp], vbuf.at[dp], R_V + dp, (p, c)))
    for p in ctx_peers:
        pending.append(send(mbuf.at[c], mbuf.at[c], R_M + c, (dp, p)))

    def pieces(t, slot):
        if t == 0:
            return [(wq.at[rows_of(slot, 512)], wq.at[rows_of(slot, 512)])]
        if t == 1:
            return [
                (
                    w1_ref.at[:, pl.ds(pl.multiple_of(q * 2048 + c * 256, 256), 256)],
                    w1.at[rows_of(slot, 512), pl.ds(q * 256, 256)],
                )
                for q in range(ND)
            ]
        if t == 2:
            return [
                (
                    w2_ref.at[rows_of(c, 256), pl.ds(half * 1024, 1024)],
                    w2.at[pl.ds(pl.multiple_of(half * 1024 + slot * 256, 256), 256)],
                )
                for half in range(2)
            ]
        return [(wd_ref.at[rows_of(c, 64)], wd.at[rows_of(slot, 64)])]

    def whole(t):
        return [wq.at[pl.ds(0, 512)], w1.at[pl.ds(0, 512)], w2.at[pl.ds(0, 512)], wd.at[pl.ds(0, 64)]][t]

    wsent = []

    def weight_send(t):
        sy, sc = new_send(), new_send()
        for src, dst in pieces(t, dp):
            send(src, dst, R_WY + t, to_y, sy)
        for src, dst in pieces(t, dp):
            send(src, dst, R_WC + t, to_core, sc)
        if t > 0:
            for src, dst in pieces(t, dp):
                pltpu.make_async_copy(src, dst, lsem.at[t]).start()
        wsent.extend([(t, sy), (t, sc)])

    def pick_heads():
        pltpu.make_async_copy(wq_ref.at[:, pl.ds(0, 1536)], pair_cols.at[:, pl.ds(0, 1536)], lsem.at[0]).wait()
        low_half = lax.broadcasted_iota(jnp.int32, (512, 128), 1) < 64
        for i in range(6):
            a = outp[0:512, i * 256 : i * 256 + 128].astype(F32)
            b = outp[0:512, i * 256 + 128 : i * 256 + 256].astype(F32)
            left = jnp.where(xx == 1, pltpu.roll(a, 64, 1), a)
            right = jnp.where(xx == 0, pltpu.roll(b, 64, 1), b)
            wq[rows_of(dp, 512), i * 128 : (i + 1) * 128] = jnp.where(low_half, left, right).astype(BF)

    pick_heads()
    for t in range(4):
        weight_send(t)

    def weight_forward(t):
        got(whole(t), R_WY + t)
        sf = new_send()
        for _, dst in pieces(t, dp_y):
            send(dst, dst, R_WF + t, to_core, sf)
        wsent.append((t, sf))

    def weight_ready(t):
        got(whole(t), R_WC + t)
        got(whole(t), R_WF + t)
        if t > 0:
            pltpu.make_async_copy(whole(t), whole(t), lsem.at[t]).wait()

    for p in dp_peers:
        got(vbuf.at[p], R_V + p)
    slots = [vbuf[s].astype(F32) for s in range(ND)]

    def vec_row(i):
        return jnp.concatenate([slots[s][i : i + 1] for s in range(ND)], 1)

    gain = vec_row(0)
    shift = vec_row(1)
    out_bias = vec_row(2) + vec_row(3)
    bias_q = jnp.concatenate([slots[i // 3][4:5, (i % 3) * 64 : (i % 3 + 1) * 64] for i in range(12)], 1)
    bias_1 = jnp.concatenate([slots[s][5:6, :256] for s in range(ND)], 1)

    def norm_parts():
        xv = x_ref[...].astype(F32)
        center = xv - jnp.mean(xv, axis=1, keepdims=True)
        inv = lax.rsqrt(jnp.mean(center * center, axis=1, keepdims=True) + EPS)
        return center * inv, inv

    xhat, _ = norm_parts()
    nb[rows_of(c, BLK), :] = (xhat * gain + shift).astype(BF)
    gb[rows_of(c, BLK), :] = g_ref[...]

    def blk(buf, cc):
        return buf.at[rows_of(cc, BLK)]

    relays = []

    def relay(buf, base, cc, dev):
        s = new_send()

        @pl.when(mid)
        def _():
            send(blk(buf, cc), blk(buf, cc), base + cc, dev, s)

        relays.append(s)

    def own_x(buf, base):
        pending.append(send(blk(buf, c), blk(buf, c), base + c, to_x))

    def own_z(buf, base):
        pending.append(send(blk(buf, c), blk(buf, c), base + c, to_outer))
        relay(buf, base, c, to_inner)

    def arrive(buf, base, k):
        cc = zp[k] * 2 + xx
        got(blk(buf, cc), base + cc)
        relay(buf, base, cc, to_inner if k == 1 else to_outer)
        pending.append(send(blk(buf, cc), blk(buf, cc), base + cc, to_x))

    def from_x(buf, base, k):
        cc = zp[k] * 2 + (1 - xx)
        got(blk(buf, cc), base + cc)

    own_x(nb, R_N)
    own_z(nb, R_N)

    for p in ctx_peers:
        got(mbuf.at[p], R_M + p)
    seg = jnp.concatenate([mbuf[i, 0:1, :] for i in range(NC)], 1)
    pos = jnp.concatenate([mbuf[i, 1:2, :] for i in range(NC)], 1).astype(F32)
    first_len = jnp.sum((seg == 0).astype(jnp.int32).astype(F32), axis=1, keepdims=True).astype(jnp.int32)
    last_start = jnp.sum((seg <= 1).astype(jnp.int32).astype(F32), axis=1, keepdims=True).astype(jnp.int32)
    qstart[...] = jnp.where(seg == 0, 0, jnp.where(seg == 1, first_len, last_start))
    lane = lax.broadcasted_iota(jnp.int32, (16, PAIR), 0)
    freqs = jnp.zeros((16, PAIR), F32)
    for i, value in enumerate(FREQS):
        freqs = jnp.where(lane == i, value, freqs)
    for i in range(4):
        angles = freqs * pos[:, i * PAIR : (i + 1) * PAIR]
        cos_h, sin_h = jnp.cos(angles), jnp.sin(angles)
        ones, zeros = jnp.ones((32, PAIR), F32), jnp.zeros((32, PAIR), F32)
        ctab[i * PAIR : (i + 1) * PAIR, :] = jnp.transpose(
            jnp.concatenate([cos_h, cos_h, ones, cos_h, cos_h, ones], 0)
        )
        stab[i * PAIR : (i + 1) * PAIR, :] = jnp.transpose(
            jnp.concatenate([-sin_h, sin_h, zeros, -sin_h, sin_h, zeros], 0)
        )

    def turn(v, rows, sign):
        cos_t, sin_t = ctab[rows, :], stab[rows, :]
        halves = []
        for i in range(v.shape[1] // 128):
            part = v[:, i * 128 : (i + 1) * 128]
            halves.append(part * cos_t + sign * (swap_turned(part) * sin_t))
        return jnp.concatenate(halves, 1) if len(halves) > 1 else halves[0]

    def project(pair):
        rows = rows_of(pair, PAIR)
        xv = nb[rows, :]
        for part in range(3):
            cols = slice(part * 256, (part + 1) * 256)
            val = dot_nn(xv, wq[:, cols]) + bias_q[:, cols]
            if part < 2:
                val = turn(val, rows, 1.0)
            low = val.astype(BF)
            dest = (qh, kh, vh)[part]
            for h in range(HEADS_C):
                dest[h, rows, :] = low[:, h * 64 : (h + 1) * 64]
            if part > 0:
                (k_t, v_t)[part - 1][:, rows] = jnp.transpose(low)

    def project_ff(pair):
        rows = rows_of(pair, PAIR)
        xv = nb[rows, :]
        for f in range(4):
            cols = slice(f * 256, (f + 1) * 256)
            u = dot_nn(xv, w1[:, cols]) + bias_1[:, cols]
            uu = u * u
            th = jnp.tanh(GELU_K * (u + GELU_A * (uu * u)))
            half = 0.5 * (1.0 + th)
            act[rows, cols] = (u * half).astype(BF)
            slope = half + 0.5 * u * (1.0 - th * th) * (GELU_K * (1.0 + 3.0 * GELU_A * uu))
            ig[rows, cols] = slope.astype(BF)

    arrive(nb, R_N, 1)
    weight_forward(0)
    arrive(nb, R_N, 2)
    weight_ready(0)
    from_x(nb, R_N, 0)
    project(zp[0])
    arrive(nb, R_N, 3)
    own_x(gb, R_G)
    own_z(gb, R_G)
    from_x(nb, R_N, 1)
    project(zp[1])
    weight_forward(1)
    from_x(nb, R_N, 2)
    project(zp[2])
    weight_ready(1)
    project_ff(zp[0])
    arrive(gb, R_G, 1)
    project_ff(zp[1])
    from_x(nb, R_N, 3)
    project(zp[3])
    project_ff(zp[2])
    arrive(gb, R_G, 2)
    project_ff(zp[3])
    weight_forward(2)

    def masked(s, i, kv):
        ji = lax.broadcasted_iota(jnp.int32, (kv, PAIR), 0)
        qi = lax.broadcasted_iota(jnp.int32, (1, PAIR), 1) + i * PAIR
        ok = (ji <= qi) & (ji >= qstart[:, i * PAIR : (i + 1) * PAIR])
        return ok, jnp.where(ok, s * SCALE, MASKED)

    def head_rows(h):
        return pl.ds(pl.multiple_of(h * 64, 64), 64)

    def attend(h, carry):
        for i in range(4):
            kv = (i + 1) * PAIR
            cols = slice(i * PAIR, (i + 1) * PAIR)
            _, s = masked(dot_nt(kh[h, 0:kv, :], qh[h, cols, :]), i, kv)
            m = jnp.max(s, axis=0, keepdims=True)
            p = jnp.exp(s - m)
            total = jnp.sum(p, axis=0, keepdims=True)
            probs = (p * (1.0 / total)).astype(BF)
            o_t[head_rows(h), cols] = dot_nn(v_t[head_rows(h), 0:kv], probs)
            lse[h, :, cols] = m + jnp.log(total)
        return carry

    lax.fori_loop(0, HEADS_C, attend, 0)
    for i in range(4):
        cols = slice(i * PAIR, (i + 1) * PAIR)
        mixed[cols, :] = jnp.transpose(o_t[:, cols]).astype(BF)

    arrive(gb, R_G, 3)
    weight_forward(3)
    weight_ready(2)
    weight_ready(3)

    x_sent = [[None] * 4, [None] * 4]
    z_sent = [[None] * 4, [None] * 4]
    src_of = (outp, gb)

    def reduce_x(op, k):
        cc = zp[k] * 2 + (1 - xx)
        if op == 1:
            pl.semaphore_wait(xfree.at[k], 1)
        x_sent[op][k] = send(blk(src_of[op], cc), rx.at[k], R_X[op] + k, to_x)

    def z_send(op, k, slot, dev, s):
        if op == 1:
            pl.semaphore_wait(zfree.at[slot], 1)
        send(rx.at[k], rz.at[slot], R_Z[op] + slot, dev, s)

    def reduce_z(op, k):
        got(rx.at[k], R_X[op] + k)
        own = src_of[op][rows_of(zp[k] * 2 + xx, BLK), :].astype(F32)
        s = z_sent[op][k] = new_send()
        slot_in = {3: 0, 2: 1, 1: 3}[k]

        @pl.when(end)
        def _():
            rx[k] = (rx[k].astype(F32) + own).astype(BF)
            z_send(op, k, 3 - k, to_outer, s)

        @pl.when(mid)
        def _():
            got(rz.at[slot_in], R_Z[op] + slot_in)
            rx[k] = (rx[k].astype(F32) + own + rz[slot_in].astype(F32)).astype(BF)
            if op == 0:
                signal(zfree.at[slot_in], to_inner if k == 1 else to_outer)
            z_send(op, k, 0 if k == 1 else 6 - k, to_outer if k == 1 else to_inner, s)

    def reduced(op, total):
        @pl.when(end)
        def _():
            got(rz.at[0], R_Z[op])
            acc[...] = total + rz[0].astype(F32)
            if op == 0:
                signal(zfree.at[0], to_outer)

        @pl.when(mid)
        def _():
            got(rz.at[2], R_Z[op] + 2)
            got(rz.at[4], R_Z[op] + 4)
            acc[...] = total + rz[2].astype(F32) + rz[4].astype(F32)
            if op == 0:
                signal(zfree.at[2], to_outer)
                signal(zfree.at[4], to_inner)

        return acc[...]

    def partial_out(pair):
        rows = rows_of(pair, PAIR)
        mv, av = mixed[rows, :], act[rows, :]
        for n in range(8):
            cols = slice(n * 256, (n + 1) * 256)
            half, off = n // 4, (n % 4) * 256
            val = dot_nn(mv, wd[:, cols]) + dot_nn(av, w2[half * 1024 : (half + 1) * 1024, off : off + 256])
            outp[rows, cols] = val.astype(BF)

    for k in (3, 2, 1, 0):
        partial_out(zp[k])
        reduce_x(0, k)

    svec[...] = jnp.zeros_like(svec)

    def backward_in(pair):
        rows = rows_of(pair, PAIR)
        ga, gc = gb[rows, 0:1024], gb[rows, 1024:2048]
        svec[0:1, :] += jnp.sum(gb[rows, :].astype(F32), axis=0, keepdims=True)
        for f in range(4):
            cols = slice(f * 256, (f + 1) * 256)
            val = dot_nt(ga, w2[f * 256 : (f + 1) * 256, :]) + dot_nt(gc, w2[1024 + f * 256 : 1024 + (f + 1) * 256, :])
            low = (val * ig[rows, cols].astype(F32)).astype(BF)
            ig[rows, cols] = low
            svec[1:2, cols] += jnp.sum(low.astype(F32), axis=0, keepdims=True)
        mg = (dot_nt(ga, wd[:, 0:1024]) + dot_nt(gc, wd[:, 1024:2048])).astype(BF)
        for h in range(HEADS_C):
            d_out[h, rows, :] = mg[:, h * 64 : (h + 1) * 64]
        prod = jnp.transpose(mg.astype(F32)) * o_t[:, rows]
        for h in range(HEADS_C):
            delta[h, :, rows] = jnp.sum(prod[h * 64 : (h + 1) * 64], axis=0, keepdims=True)

    for k in range(4):
        from_x(gb, R_G, k)
        backward_in(zp[k])

    for t, s in wsent:
        sent(whole(t), s)
    for s in pending:
        s.wait_send()
    pending.clear()

    @pl.when(mid)
    def _():
        for s in relays:
            sent(blk(gb, 0), s)

    for f in range(4):
        tb[...] = transposed(act[:, f * 256 : (f + 1) * 256])

        def grad2(n, carry):
            off = pl.multiple_of((n % 4) * 256, 256)
            val = dot_nn(tb[...], gb[:, pl.ds(pl.multiple_of(n * 256, 256), 256)])
            w2[pl.ds(pl.multiple_of((n // 4) * 1024 + f * 256, 256), 256), pl.ds(off, 256)] = val.astype(BF)
            return carry

        lax.fori_loop(0, 8, grad2, 0)
    tb[...] = transposed(mixed[...])

    def gradd(n, carry):
        cols = pl.ds(pl.multiple_of(n * 256, 256), 256)
        wd[:, cols] = dot_nn(tb[...], gb[:, cols]).astype(BF)
        return carry

    lax.fori_loop(0, 8, gradd, 0)

    def quarter(t, q):
        if t == 2:
            return [w2.at[pl.ds(pl.multiple_of(half * 1024 + q * 256, 256), 256)] for half in range(2)]
        if t == 3:
            return [wd.at[rows_of(q, 64)]]
        return [(wq, w1)[t].at[rows_of(q, 512)]]

    def core_slot(t, yy):
        if t == 0:
            return [cq.at[yy]]
        if t == 1:
            return [cw.at[yy]]
        if t == 2:
            return [cw.at[yy, pl.ds(half * 256, 256)] for half in range(2)]
        return [cd.at[yy]]

    core_sent, y_sent = {}, {}

    def core_send(t):
        ids = []
        for yy in range(2):
            s = new_send()
            for src, dst in zip(quarter(t, yy * 2 + (1 - core)), core_slot(t, yy)):
                send(src, dst, R_C + t * 2 + yy, to_core, s)
            ids.append(s)
        core_sent[t] = ids

    def slot_whole(t, yy):
        return (cq, cw, cw, cd)[t].at[yy]

    def landing(t):
        return quarter(t, 1 - core)

    def y_send(t):
        for s in core_sent[t]:
            sent(slot_whole(t, 0), s)
        signal(yfree.at[t], to_y)
        for yy in range(2):
            got(slot_whole(t, yy), R_C + t * 2 + yy)
            for own, other in zip(quarter(t, yy * 2 + core), core_slot(t, yy)):
                own[...] = (own[...].astype(F32) + other[...].astype(F32)).astype(BF)
        if t == 2:
            signal(cfree.at[0], to_core)
        pl.semaphore_wait(yfree.at[t], 1)
        s = new_send()
        for src, dst in zip(quarter(t, (1 - y) * 2 + core), landing(t)):
            send(src, dst, R_Y + t, to_y, s)
        y_sent[t] = s

    def total(t):
        got(whole(t), R_Y + t)
        for own, other in zip(quarter(t, y * 2 + core), landing(t)):
            own[...] = (own[...].astype(F32) + other[...].astype(F32)).astype(BF)

    core_send(2)
    core_send(3)
    reduce_z(0, 3)

    def partial_ff(pair):
        rows = rows_of(pair, PAIR)
        iv = ig[rows, :]
        for n in range(8):
            cols = slice(n * 256, (n + 1) * 256)
            gb[rows, cols] = dot_nt(iv, w1[cols, :]).astype(BF)

    def partial_attn(pair):
        rows = rows_of(pair, PAIR)
        jv = jg[rows, :]
        svec[1:2, 1024:1792] += jnp.sum(jv.astype(F32), axis=0, keepdims=True)
        for n in range(8):
            cols = slice(n * 256, (n + 1) * 256)
            gb[rows, cols] = (dot_nt(jv, wq[cols, :]) + gb[rows, cols].astype(F32)).astype(BF)

    def input_grad_weights(t, q):
        for half in range(2):
            span = pl.ds(pl.multiple_of(q * 512 + half * 256, 256), 256)
            tb[...] = transposed(nb[:, span])

            def grad(n, carry):
                cols = pl.ds(pl.multiple_of(n * 256, 256), 256)
                (wq, w1)[t][span, cols] = dot_nn(tb[...], (jg, ig)[t][:, cols]).astype(BF)
                return carry

            lax.fori_loop(0, (3, 4)[t], grad, 0)

    for k in range(4):
        partial_ff(zp[k])
    y_send(2)
    y_send(3)
    reduce_z(0, 2)
    for yy in range(2):
        input_grad_weights(1, yy * 2 + (1 - core))
    pl.semaphore_wait(cfree.at[0], 1)
    core_send(1)
    for yy in range(2):
        input_grad_weights(1, yy * 2 + core)

    def attend_back(hp, carry):
        for j in range(2):
            h = hp * 2 + j
            for i in (3, 2, 1, 0):
                kv = (i + 1) * PAIR
                cols = slice(i * PAIR, (i + 1) * PAIR)
                ok, s = masked(dot_nt(kh[h, 0:kv, :], qh[h, cols, :]), i, kv)
                p = jnp.where(ok, jnp.exp(s - lse[h, :, cols]), 0.0)
                dp_t = dot_nt(vh[h, 0:kv, :], d_out[h, cols, :])
                ds = (p * (dp_t - delta[h, :, cols])).astype(BF)
                dv = dot_nn(p.astype(BF), d_out[h, cols, :])
                dk = dot_nn(ds, qh[h, cols, :])
                if i == 3:
                    dva[j, 0:kv, :] = dv
                    dka[j, 0:kv, :] = dk
                else:
                    dva[j, 0:kv, :] += dv
                    dka[j, 0:kv, :] += dk
                o_t[head_rows(h), cols] = dot_nn(k_t[head_rows(h), 0:kv], ds)
        for i in range(4):
            rows = slice(i * PAIR, (i + 1) * PAIR)
            kk = jnp.concatenate([dka[0, rows, :], dka[1, rows, :]], 1) * SCALE
            vv = jnp.concatenate([dva[0, rows, :], dva[1, rows, :]], 1)
            jg[rows, pl.ds(pl.multiple_of(256 + hp * 128, 128), 128)] = turn(kk, rows, -1.0).astype(BF)
            jg[rows, pl.ds(pl.multiple_of(512 + hp * 128, 128), 128)] = vv.astype(BF)
        return carry

    lax.fori_loop(0, 2, attend_back, 0)
    for i in range(4):
        rows = slice(i * PAIR, (i + 1) * PAIR)
        jg[rows, 0:256] = turn(jnp.transpose(o_t[:, rows]) * SCALE, rows, -1.0).astype(BF)

    y_send(1)
    reduce_z(0, 1)

    got(rx.at[0], R_X[0])
    x_sent[0][0].wait_send()
    outp[rows_of(cx, BLK), :] = rx[0]
    signal(xfree.at[0], to_x)

    for k in (3, 2):
        partial_attn(zp[k])
        sent(rx.at[k], z_sent[0][k])
        signal(xfree.at[k], to_x)
        reduce_x(1, k)
    partial_attn(zp[1])
    partial_attn(zp[0])
    for yy in range(2):
        input_grad_weights(0, yy * 2 + (1 - core))
    core_send(0)
    sent(rx.at[1], z_sent[0][1])
    signal(xfree.at[1], to_x)
    reduce_x(1, 1)
    reduce_x(1, 0)
    for yy in range(2):
        input_grad_weights(0, yy * 2 + core)
    y_send(0)

    total_o = outp[rows_of(cx, BLK), :].astype(F32) + outp[rows_of(c, BLK), :].astype(F32)
    out_ref[...] = (x_ref[...].astype(F32) + out_bias + reduced(0, total_o)).astype(BF)
    reduce_z(1, 3)

    outs = []

    def out_copy(src, dst):
        copy = pltpu.make_async_copy(src, dst, lsem.at[4 + len(outs)])
        copy.start()
        outs.append(copy)

    total(2)
    for half in range(2):
        out_copy(quarter(2, y * 2 + core)[half], w2s_ref.at[:, pl.ds(half * 1024, 1024)])
    total(3)
    out_copy(quarter(3, y * 2 + core)[0], wds_ref)
    reduce_z(1, 2)

    def exchange(t, buf, base):
        total(t)
        first = (y * 2 + core) * 8
        buf[c] = (wq, w1)[t][rows_of(first + c, 64), :]
        for p in ctx_peers:
            pending.append(send((wq, w1)[t].at[rows_of(first + p, 64)], buf.at[c], base + c, (dp, p)))

    exchange(1, a1, R_A1)
    reduce_z(1, 1)

    got(rx.at[0], R_X[1])
    ng = reduced(1, rx[0].astype(F32) + gb[rows_of(c, BLK), :].astype(F32))
    xhat, inv = norm_parts()
    e = ng * gain
    m1 = jnp.mean(e, axis=1, keepdims=True)
    m2 = jnp.mean(e * xhat, axis=1, keepdims=True)
    xgrad_ref[...] = (g_ref[...].astype(F32) + (e - m1 - xhat * m2) * inv).astype(BF)
    pkc[c, 0:16, :] = as_rows(jnp.sum(ng * xhat, axis=0, keepdims=True))
    pkc[c, 16:32, :] = as_rows(jnp.sum(ng, axis=0, keepdims=True))
    pkc[c, 32:40, :] = as_rows(svec[1:2, 1024:2048])
    for p in ctx_peers:
        pending.append(send(pkc.at[c], pkc.at[c], R_PC + c, (dp, p)))
    exchange(0, aq, R_AQ)

    for p in ctx_peers:
        got(pkc.at[p], R_PC + p)
    norm_sum = pkc[0, 0:32, :]
    for i in range(1, NC):
        norm_sum = norm_sum + pkc[i, 0:32, :]
    pkd[dp, 0:32, :] = norm_sum
    for i in range(NC):
        pkd[dp, 32 + i * 8 : 40 + i * 8, :] = pkc[i, 32:40, :]
    pkd[dp, 96:112, :] = as_rows(svec[0:1, :])
    pkd[dp, 112:120, :] = as_rows(svec[1:2, 0:1024])
    for p in dp_peers:
        pending.append(send(pkd.at[dp], pkd.at[dp], R_PD + dp, (p, c)))

    for p in ctx_peers:
        got(a1.at[p], R_A1 + p)
    out_copy(a1, a1_ref)
    for p in dp_peers:
        got(pkd.at[p], R_PD + p)
    small_ref[...] = pkd[0] + pkd[1] + pkd[2] + pkd[3]
    for p in ctx_peers:
        got(aq.at[p], R_AQ + p)
    out_copy(aq, aq_ref)

    for s in pending:
        s.wait_send()
    for k in (3, 2, 1):
        x_sent[0][k].wait_send()
    for k in range(4):
        x_sent[1][k].wait_send()
    for k in (3, 2, 1):
        sent(rx.at[k], z_sent[1][k])
    for t in range(4):
        sent(whole(t), y_sent[t])
    for copy in outs:
        copy.wait()


def finish_kernel(
    out_in,
    xgrad_in,
    small,
    w2s,
    wds,
    a1,
    aq,
    out_ref,
    xgrad_ref,
    gain_ref,
    shift_ref,
    wqg_ref,
    bqg_ref,
    wdg_ref,
    bd_ref,
    w1g_ref,
    b1_ref,
    w2g_ref,
    b2_ref,
):
    dp = lax.axis_index("dp")
    c = lax.axis_index("ctx")
    me = dp * NC + c
    out_ref[...] = out_in[...]
    xgrad_ref[...] = xgrad_in[...]
    w2g_ref[...] = w2s[...].astype(F32)
    wdg_ref[...] = wds[...].astype(F32)
    for q in range(ND):
        for i in range(NC):
            w1g_ref[:, q * 2048 + i * 256 : q * 2048 + (i + 1) * 256] = a1[i, :, q * 256 : (q + 1) * 256].astype(F32)
    for o in range(12):
        for i in range(NC // 2):
            both = [aq[2 * i + j, :, o * 64 : (o + 1) * 64].astype(F32) for j in range(2)]
            wqg_ref[:, o * 512 + i * 128 : o * 512 + (i + 1) * 128] = jnp.concatenate(both, 1)

    def own_64(first):
        row = small[pl.ds(first + me // 2, 1), :]
        return jnp.where(me % 2 == 0, row[:, 0:64], row[:, 64:128]).reshape(64)

    gain_ref[...] = own_64(0)
    shift_ref[...] = own_64(16)
    summed = own_64(96)
    bd_ref[...] = summed
    b2_ref[...] = summed
    rows = small[pl.ds(112 + dp * 2, 2), :]
    b1_ref[...] = jnp.concatenate([rows[0:1], rows[1:2]], 1).reshape(256)

    picked = []
    for j in range(3):
        head = me * 3 + j
        o, i = head // NC, head % NC
        row = small[pl.ds(32 + i * 8 + o // 2, 1), :]
        picked.append(jnp.where(o % 2 == 0, row[:, 0:64], row[:, 64:128]))
    bqg_ref[...] = jnp.concatenate(picked, 1).reshape(192)


def fast_device(inputs, positions, seq_ids, ln_gain, ln_bias, w_qkv, b_qkv, w_dense, b_dense, w_fc1, b_fc1, w_fc2, b_fc2, cotangent):
    width = inputs.shape[2]
    vm = pl.BlockSpec(memory_space=pltpu.VMEM)
    hbm = pl.BlockSpec(memory_space=pl.ANY)
    dma = pltpu.SemaphoreType.DMA
    reg = pltpu.SemaphoreType.REGULAR
    sd = jax.ShapeDtypeStruct
    parts = pl.pallas_call(
        layer_kernel,
        out_shape=(
            sd((BLK, width), BF),
            sd((BLK, width), BF),
            sd((120, 128), F32),
            sd((256, 2048), BF),
            sd((64, 2048), BF),
            sd((NC, 64, 1024), BF),
            sd((NC, 64, 768), BF),
        ),
        in_specs=[vm] * 10 + [hbm] * 4,
        out_specs=(vm, vm, vm, hbm, hbm, hbm, hbm),
        scratch_shapes=[
            pltpu.VMEM((TOK, 2048), BF),
            pltpu.VMEM((TOK, 2048), BF),
            pltpu.VMEM((2048, 768), BF),
            pltpu.VMEM((2048, 1024), BF),
            pltpu.VMEM((2048, 1024), BF),
            pltpu.VMEM((256, 2048), BF),
            pltpu.VMEM((ND, 16, 512), BF),
            pltpu.VMEM((NC, 8, BLK), jnp.int32),
            pltpu.VMEM((TOK, 128), F32),
            pltpu.VMEM((TOK, 128), F32),
            pltpu.VMEM((1, TOK), jnp.int32),
            pltpu.VMEM((4, TOK, 64), BF),
            pltpu.VMEM((4, TOK, 64), BF),
            pltpu.VMEM((4, TOK, 64), BF),
            pltpu.VMEM((256, TOK), BF),
            pltpu.VMEM((256, TOK), BF),
            pltpu.VMEM((256, TOK), F32),
            pltpu.VMEM((4, 1, TOK), F32),
            pltpu.VMEM((4, 1, TOK), F32),
            pltpu.VMEM((TOK, 256), BF),
            pltpu.VMEM((TOK, 1024), BF),
            pltpu.VMEM((TOK, 1024), BF),
            pltpu.VMEM((4, TOK, 64), BF),
            pltpu.VMEM((TOK, 768), BF),
            pltpu.VMEM((2, TOK, 64), F32),
            pltpu.VMEM((2, TOK, 64), F32),
            pltpu.VMEM((8, 2048), F32),
            pltpu.VMEM((TOK, 2048), BF),
            pltpu.VMEM((4, BLK, 2048), BF),
            pltpu.VMEM((5, BLK, 2048), BF),
            pltpu.VMEM((BLK, 2048), F32),
            pltpu.VMEM((2, 512, 1024), BF),
            pltpu.VMEM((2, 512, 768), BF),
            pltpu.VMEM((2, 64, 2048), BF),
            pltpu.VMEM((NC, 64, 1024), BF),
            pltpu.VMEM((NC, 64, 768), BF),
            pltpu.VMEM((NC, 40, 128), F32),
            pltpu.VMEM((ND, 120, 128), F32),
            pltpu.VMEM((256, TOK), BF),
            dma((N_SEND,)),
            dma((N_RECV,)),
            dma((9,)),
            reg((4,)),
            reg((5,)),
            reg((1,)),
            reg((4,)),
        ],
        compiler_params=pltpu.CompilerParams(
            collective_id=0, has_side_effects=True, vmem_limit_bytes=63 * 1024 * 1024
        ),
        name="layer",
    )(
        inputs[0], cotangent[0], seq_ids, positions, ln_gain, ln_bias, b_dense, b_fc2, b_qkv, b_fc1, w_qkv, w_fc1, w_fc2, w_dense
    )
    done = pl.pallas_call(
        finish_kernel,
        out_shape=(
            sd((BLK, width), BF),
            sd((BLK, width), BF),
            sd((64,), F32),
            sd((64,), F32),
            sd((64, 6144), F32),
            sd((192,), F32),
            sd((64, 2048), F32),
            sd((64,), F32),
            sd((64, 8192), F32),
            sd((256,), F32),
            sd((256, 2048), F32),
            sd((64,), F32),
        ),
        in_specs=[vm] * 7,
        out_specs=(vm,) * 12,
        compiler_params=pltpu.CompilerParams(vmem_limit_bytes=32 * 1024 * 1024),
        name="finish",
    )(*parts)
    return (done[0][None], done[1][None]) + tuple(done[2:])


def solution(mesh):
    placed = (
        P("dp", "ctx", None),
        P("dp", "ctx"),
        P("dp", "ctx"),
        P("dp"),
        P("dp"),
        P("dp", None),
        P("dp"),
        P("dp", None),
        P("dp"),
        P("dp", None),
        P("dp"),
        P("dp", None),
        P("dp"),
        P("dp", "ctx", None),
    )
    fits = mesh.shape["dp"] == ND and mesh.shape["ctx"] == NC
    return jax.shard_map(
        fast_device if fits else per_device,
        mesh=mesh,
        in_specs=placed,
        out_specs=(
            P("dp", "ctx", None),
            P("dp", "ctx", None),
            P(("dp", "ctx")),
            P(("dp", "ctx")),
            P(("dp", "ctx"), None),
            P(("dp", "ctx")),
            P(("dp", "ctx"), None),
            P(("dp", "ctx")),
            P(("dp", "ctx"), None),
            P(("dp", "ctx")),
            P(("dp", "ctx"), None),
            P(("dp", "ctx")),
        ),
        check_vma=False,
    )
```

```python
import math

import jax
import jax.numpy as jnp
import numpy as np
from jax import lax
from jax.experimental import pallas as pl
from jax.experimental.pallas import tpu as pltpu
from jax.sharding import PartitionSpec as P

HEAD_DIM = 64
ROT = 32


EPS = 1e-05
MASKED = -1e30
SCALE = 0.125
BASE = 10000.0


def layer_norm(values, gain_vec, shift_vec):
    center = values - jnp.mean(values, axis=1, keepdims=True)
    spread = jnp.mean(center * center, axis=1, keepdims=True)
    return center * lax.rsqrt(spread + EPS) * gain_vec + shift_vec


def gelu_tanh(values):
    return jax.nn.gelu(values, approximate=True)


def rotate(values, angle_pos):
    row_count = values.shape[0]
    head_count = values.shape[1] // HEAD_DIM
    half_rot = ROT // 2
    split_heads = values.reshape(row_count, head_count, HEAD_DIM)
    freqs = BASE ** (-(jnp.arange(half_rot, dtype=jnp.float32) * 2.0) / ROT)
    angles = angle_pos[:, None] * freqs[None, :]
    cosine = jnp.cos(angles)[:, None, :]
    sine = jnp.sin(angles)[:, None, :]
    first_half = split_heads[:, :, :half_rot]
    second_half = split_heads[:, :, half_rot:ROT]
    turned = jnp.concatenate(
        [
            first_half * cosine - second_half * sine,
            second_half * cosine + first_half * sine,
            split_heads[:, :, ROT:],
        ],
        axis=2,
    )
    return turned.reshape(row_count, head_count * HEAD_DIM)


def visible(query_index, query_seg, key_index, key_seg):
    causal = key_index[None, :] <= query_index[:, None]
    return causal[None] & (key_seg[:, None, :] == query_seg[:, :, None])


def split_cols(values, low_col, high_col):
    return values[:, :, low_col:high_col].reshape(
        values.shape[0], values.shape[1], (high_col - low_col) // HEAD_DIM, HEAD_DIM
    )


def head_scores(query_heads, key_heads, allowed):
    raw = (
        jnp.einsum("sqhd,skhd->shqk", query_heads, key_heads, preferred_element_type=jnp.float32)
        * SCALE
    )
    return jnp.where(allowed[:, None], raw, MASKED)


def unchanged(state):
    return state


def per_device(
    inputs,
    positions,
    seq_ids,
    ln_gain,
    ln_bias,
    w_qkv,
    b_qkv,
    w_dense,
    b_dense,
    w_fc1,
    b_fc1,
    w_fc2,
    b_fc2,
    cotangent,
):
    (
        gain_all,
        shift_all,
        qkv_all,
        qkv_offset,
        dense_all,
        dense_offset,
        fc1_all,
        fc1_offset,
        fc2_all,
        fc2_offset,
    ) = (
        lax.all_gather(ln_gain, "dp", axis=0, tiled=True),
        lax.all_gather(ln_bias, "dp", axis=0, tiled=True),
        lax.all_gather(w_qkv, "dp", axis=0, tiled=True),
        lax.all_gather(b_qkv, "dp", axis=0, tiled=True),
        lax.all_gather(w_dense, "dp", axis=0, tiled=True),
        lax.all_gather(b_dense, "dp", axis=0, tiled=True),
        lax.all_gather(w_fc1, "dp", axis=0, tiled=True),
        lax.all_gather(b_fc1, "dp", axis=0, tiled=True),
        lax.all_gather(w_fc2, "dp", axis=0, tiled=True),
        lax.all_gather(b_fc2, "dp", axis=0, tiled=True),
    )
    stream_count = inputs.shape[0]
    row_count = inputs.shape[1]
    width = inputs.shape[2]
    flat_rows = stream_count * row_count
    resid = inputs.reshape(flat_rows, width).astype(jnp.float32)
    head_count = width // HEAD_DIM
    group_heads = math.gcd(head_count, 8)
    group_cols = group_heads * HEAD_DIM
    group_count = head_count // group_heads
    angle_pos = positions.reshape(flat_rows).astype(jnp.float32)
    own_seg = seq_ids.astype(jnp.bfloat16)
    row_start = lax.axis_index("ctx") * row_count
    own_index = row_start + jnp.arange(row_count, dtype=jnp.int32)
    normed, norm_back = jax.vjp(
        layer_norm, resid, gain_all.astype(jnp.float32), shift_all.astype(jnp.float32)
    )
    hidden = normed.astype(jnp.bfloat16)
    joint = jnp.dot(hidden, qkv_all, preferred_element_type=jnp.float32) + qkv_offset.astype(
        jnp.float32
    )
    queries = (
        rotate(joint[:, :width], angle_pos)
        .astype(jnp.bfloat16)
        .reshape(stream_count, row_count, width)
    )
    keys_own = (
        rotate(joint[:, width : 2 * width], angle_pos)
        .astype(jnp.bfloat16)
        .reshape(stream_count, row_count, width)
    )
    values_own = joint[:, 2 * width :].astype(jnp.bfloat16).reshape(stream_count, row_count, width)
    start_state = (
        jnp.full((stream_count, head_count, row_count), MASKED, jnp.float32),
        jnp.zeros((stream_count, head_count, row_count), jnp.float32),
        jnp.zeros((stream_count, row_count, width), jnp.float32),
    )
    key_part = lax.all_gather(keys_own, "ctx", axis=1, tiled=True)
    value_part = lax.all_gather(values_own, "ctx", axis=1, tiled=True)
    seg_part = lax.all_gather(own_seg, "ctx", axis=1, tiled=True)
    key_count = key_part.shape[1]
    allowed = visible(own_index, own_seg, jnp.arange(key_count, dtype=jnp.int32), seg_part)

    def forward_compute(state):
        peak_in, total_in, accum_in = state
        peak_list, total_list, accum_list = ([], [], [])
        for group_index in range(group_count):
            low_col = group_index * group_cols
            high_col = low_col + group_cols
            low_head = group_index * group_heads
            high_head = low_head + group_heads
            scores = head_scores(
                split_cols(queries, low_col, high_col),
                split_cols(key_part, low_col, high_col),
                allowed,
            )
            old_peak = peak_in[:, low_head:high_head]
            new_peak = jnp.maximum(old_peak, jnp.max(scores, axis=3))
            weights = jnp.where(allowed[:, None], jnp.exp(scores - new_peak[:, :, :, None]), 0.0)
            total_list.append(jnp.sum(weights, axis=3))
            gathered_vals = jnp.einsum(
                "shqk,skhd->sqhd",
                weights.astype(jnp.bfloat16),
                split_cols(value_part, low_col, high_col),
                preferred_element_type=jnp.float32,
            )
            accum_list.append(gathered_vals.reshape(stream_count, row_count, group_cols))
            peak_list.append(new_peak)
        return (
            jnp.concatenate(peak_list, 1),
            jnp.concatenate(total_list, 1),
            jnp.concatenate(accum_list, 2),
        )

    result_state = lax.cond(
        jnp.int32(0) < row_start + row_count, forward_compute, unchanged, start_state
    )
    peak, total, accum = result_state
    attended = (
        accum.reshape(stream_count, row_count, head_count, HEAD_DIM)
        / jnp.transpose(total, (0, 2, 1))[:, :, :, None]
    ).reshape(stream_count, row_count, width)
    log_total = jnp.transpose(peak + jnp.log(total), (0, 2, 1))
    mixed = attended.astype(jnp.bfloat16).reshape(flat_rows, width)
    inner = jnp.dot(hidden, fc1_all, preferred_element_type=jnp.float32) + fc1_offset.astype(
        jnp.float32
    )
    active, gelu_back = jax.vjp(gelu_tanh, inner)
    active_low = active.astype(jnp.bfloat16)
    summed = (
        resid
        + jnp.dot(mixed, dense_all, preferred_element_type=jnp.float32)
        + dense_offset.astype(jnp.float32)
    )
    summed = (
        summed
        + jnp.dot(active_low, fc2_all, preferred_element_type=jnp.float32)
        + fc2_offset.astype(jnp.float32)
    )
    outputs = summed.astype(jnp.bfloat16).reshape(stream_count, row_count, width)
    upstream = cotangent.reshape(flat_rows, width)
    upstream_f = upstream.astype(jnp.float32)
    bias_term = jnp.sum(upstream_f, axis=0)
    fc2_term = jnp.einsum("tf,td->fd", active_low, upstream, preferred_element_type=jnp.float32)
    fc2_sum = lax.psum_scatter(fc2_term, ("dp", "ctx"), scatter_dimension=0, tiled=True)
    fc2_sum, upstream = lax.optimization_barrier((fc2_sum, upstream))
    act_grad = jnp.einsum("td,fd->tf", upstream, fc2_all, preferred_element_type=jnp.float32)
    inner_grad = gelu_back(act_grad)[0].astype(jnp.bfloat16)
    fc1_term = jnp.einsum("td,tf->df", hidden, inner_grad, preferred_element_type=jnp.float32)
    fc1_bias_term = jnp.sum(inner_grad.astype(jnp.float32), axis=0)
    fc1_sum = lax.psum_scatter(fc1_term, ("dp", "ctx"), scatter_dimension=0, tiled=True)
    fc1_sum, mixed, upstream, upstream_f, fc1_bias_term, inner_grad, hidden = lax.optimization_barrier(
        (fc1_sum, mixed, upstream, upstream_f, fc1_bias_term, inner_grad, hidden)
    )
    fc1_bias_sum, bias_sum = (
        lax.psum_scatter(fc1_bias_term, ("dp", "ctx"), scatter_dimension=0, tiled=True),
        lax.psum_scatter(bias_term, ("dp", "ctx"), scatter_dimension=0, tiled=True),
    )
    dense_term = jnp.einsum("td,te->de", mixed, upstream, preferred_element_type=jnp.float32)
    dense_sum = lax.psum_scatter(dense_term, ("dp", "ctx"), scatter_dimension=0, tiled=True)
    dense_sum, upstream, dense_all = lax.optimization_barrier((dense_sum, upstream, dense_all))
    mixed_grad = (
        jnp.einsum("te,de->td", upstream, dense_all, preferred_element_type=jnp.float32)
        .astype(jnp.bfloat16)
        .reshape(stream_count, row_count, width)
    )
    delta = jnp.sum(
        (mixed_grad.astype(jnp.float32) * attended).reshape(
            stream_count, row_count, head_count, HEAD_DIM
        ),
        axis=3,
    )
    zero_block = jnp.zeros((stream_count, row_count, width), jnp.float32)
    query_key_part = lax.all_gather(keys_own, "ctx", axis=1, tiled=True)
    query_value_part = lax.all_gather(values_own, "ctx", axis=1, tiled=True)
    seg_part = lax.all_gather(own_seg, "ctx", axis=1, tiled=True)
    key_count = query_key_part.shape[1]
    query_allowed = visible(own_index, own_seg, jnp.arange(key_count, dtype=jnp.int32), seg_part)

    def query_compute(grad_in):
        step_list = []
        for group_index in range(group_count):
            low_col = group_index * group_cols
            high_col = low_col + group_cols
            low_head = group_index * group_heads
            high_head = low_head + group_heads
            scores = head_scores(
                split_cols(queries, low_col, high_col),
                split_cols(query_key_part, low_col, high_col),
                query_allowed,
            )
            lse_here = jnp.transpose(log_total[:, :, low_head:high_head], (0, 2, 1))[:, :, :, None]
            delta_here = jnp.transpose(delta[:, :, low_head:high_head], (0, 2, 1))[:, :, :, None]
            probs = jnp.where(query_allowed[:, None], jnp.exp(scores - lse_here), 0.0)
            prob_grad = jnp.einsum(
                "sqhd,skhd->shqk",
                split_cols(mixed_grad, low_col, high_col),
                split_cols(query_value_part, low_col, high_col),
                preferred_element_type=jnp.float32,
            )
            score_grad = (probs * (prob_grad - delta_here)).astype(jnp.bfloat16)
            query_step = (
                jnp.einsum(
                    "shqk,skhd->sqhd",
                    score_grad,
                    split_cols(query_key_part, low_col, high_col),
                    preferred_element_type=jnp.float32,
                )
                * SCALE
            )
            step_list.append(query_step.reshape(stream_count, row_count, group_cols))
        return grad_in + jnp.concatenate(step_list, 2)

    result_grad = lax.cond(
        jnp.int32(0) < row_start + row_count, query_compute, unchanged, zero_block
    )
    log_total_all, delta_all = (
        lax.all_gather(log_total, "ctx", axis=1, tiled=True),
        lax.all_gather(delta, "ctx", axis=1, tiled=True),
    )
    start = jnp.int32(0)
    query_part = lax.all_gather(queries, "ctx", axis=1, tiled=True)
    grad_part = lax.all_gather(mixed_grad, "ctx", axis=1, tiled=True)
    seg_part = lax.all_gather(own_seg, "ctx", axis=1, tiled=True)
    query_count = query_part.shape[1]
    query_index = jnp.arange(query_count, dtype=jnp.int32)
    key_allowed = visible(query_index, seg_part, own_index, own_seg)
    lse_part = lax.dynamic_slice_in_dim(log_total_all, start, query_count, 1)

    def key_compute(state):
        key_in, value_in = state
        key_list, value_list = ([], [])
        for group_index in range(group_count):
            low_col = group_index * group_cols
            high_col = low_col + group_cols
            low_head = group_index * group_heads
            high_head = low_head + group_heads
            scores = head_scores(
                split_cols(query_part, low_col, high_col),
                split_cols(keys_own, low_col, high_col),
                key_allowed,
            )
            lse_here = jnp.transpose(lse_part[:, :, low_head:high_head], (0, 2, 1))[:, :, :, None]
            delta_here = jnp.transpose(delta_all[:, :, low_head:high_head], (0, 2, 1))[
                :, :, :, None
            ]
            probs = jnp.where(key_allowed[:, None], jnp.exp(scores - lse_here), 0.0)
            grad_heads = split_cols(grad_part, low_col, high_col)
            value_step = jnp.einsum(
                "shqk,sqhd->skhd",
                probs.astype(jnp.bfloat16),
                grad_heads,
                preferred_element_type=jnp.float32,
            )
            prob_grad = jnp.einsum(
                "sqhd,skhd->shqk",
                grad_heads,
                split_cols(values_own, low_col, high_col),
                preferred_element_type=jnp.float32,
            )
            score_grad = (probs * (prob_grad - delta_here)).astype(jnp.bfloat16)
            key_step = (
                jnp.einsum(
                    "shqk,sqhd->skhd",
                    score_grad,
                    split_cols(query_part, low_col, high_col),
                    preferred_element_type=jnp.float32,
                )
                * SCALE
            )
            key_list.append(key_step.reshape(stream_count, row_count, group_cols))
            value_list.append(value_step.reshape(stream_count, row_count, group_cols))
        return (key_in + jnp.concatenate(key_list, 2), value_in + jnp.concatenate(value_list, 2))

    result_pair = lax.cond(
        start + query_count > row_start, key_compute, unchanged, (zero_block, zero_block)
    )
    key_grad, value_grad = result_pair
    joint_grad = jnp.concatenate(
        [
            rotate(result_grad.reshape(flat_rows, width), -angle_pos),
            rotate(key_grad.reshape(flat_rows, width), -angle_pos),
            value_grad.reshape(flat_rows, width),
        ],
        axis=1,
    ).astype(jnp.bfloat16)
    qkv_term = jnp.einsum("td,te->de", hidden, joint_grad, preferred_element_type=jnp.float32)
    qkv_bias_term = jnp.sum(joint_grad.astype(jnp.float32), axis=0)
    hidden_grad = jnp.einsum("te,de->td", joint_grad, qkv_all, preferred_element_type=jnp.float32)
    hidden_grad = hidden_grad + jnp.einsum(
        "tf,df->td", inner_grad, fc1_all, preferred_element_type=jnp.float32
    )
    resid_grad, gain_term, shift_term = norm_back(hidden_grad)
    input_grad = (
        (upstream_f + resid_grad).astype(jnp.bfloat16).reshape(stream_count, row_count, width)
    )
    gain_sum, shift_sum, qkv_sum, qkv_bias_sum = (
        lax.psum_scatter(gain_term, ("dp", "ctx"), scatter_dimension=0, tiled=True),
        lax.psum_scatter(shift_term, ("dp", "ctx"), scatter_dimension=0, tiled=True),
        lax.psum_scatter(qkv_term, ("dp", "ctx"), scatter_dimension=0, tiled=True),
        lax.psum_scatter(qkv_bias_term, ("dp", "ctx"), scatter_dimension=0, tiled=True),
    )
    return (
        outputs,
        input_grad,
        gain_sum,
        shift_sum,
        qkv_sum,
        qkv_bias_sum,
        dense_sum,
        bias_sum,
        fc1_sum,
        fc1_bias_sum,
        fc2_sum,
        bias_sum,
    )


BF = jnp.bfloat16
F32 = jnp.float32
BLK = 128
PAIR = 256
NC = 8
ND = 4
TOK = NC * BLK
HEADS_C = 4
MESH_ID = pl.DeviceIdType.MESH
GELU_A = 0.044715
GELU_K = math.sqrt(2.0 / math.pi)

R_N, R_G, R_M, R_V = 0, 8, 16, 24
R_WY, R_WC, R_WF = 28, 32, 36
R_X = (40, 44)
R_Z = (48, 53)
R_C, R_Y = 58, 66
R_A1, R_AQ, R_PC, R_PD = 70, 78, 86, 94
N_RECV = 98
N_SEND = 112
FREQS = [float(np.float32(BASE) ** np.float32(-2.0 * i / ROT)) for i in range(ROT // 2)]


def dot_nn(a, b):
    return lax.dot_general(a, b, (((1,), (0,)), ((), ())), preferred_element_type=F32)


def dot_nt(a, b):
    return lax.dot_general(a, b, (((1,), (1,)), ((), ())), preferred_element_type=F32)


def dot_tn(a, b):
    return lax.dot_general(a, b, (((0,), (0,)), ((), ())), preferred_element_type=F32)


def swap_turned(v):
    lane = lax.broadcasted_iota(jnp.int32, v.shape, 1) % HEAD_DIM
    return jnp.where(lane < 16, pltpu.roll(v, 112, 1), pltpu.roll(v, 16, 1))


def as_rows(v):
    return jnp.concatenate([v[:, i * 128 : (i + 1) * 128] for i in range(v.shape[1] // 128)], 0)


def as_row(v):
    return jnp.concatenate([v[i : i + 1] for i in range(v.shape[0])], 1)


def own_lanes(row, width, index, count):
    total = jnp.zeros((1, width), F32)
    for i in range(count):
        total = total + jnp.where(index == i, row[:, i * width : (i + 1) * width], 0.0)
    return total


def layer_kernel(
    x_ref,
    g_ref,
    seg_ref,
    pos_ref,
    gain_ref,
    shift_ref,
    bd_ref,
    b2_ref,
    bq_ref,
    b1_ref,
    wq_ref,
    w1_ref,
    w2_ref,
    wd_ref,
    out_ref,
    xgrad_ref,
    small_ref,
    w2s_ref,
    wds_ref,
    a1_ref,
    aq_ref,
    nb,
    gb,
    wq,
    w1,
    w2,
    wd,
    vbuf,
    mbuf,
    ctab,
    stab,
    qstart,
    qh,
    kh,
    vh,
    k_t,
    v_t,
    o_t,
    lse,
    delta,
    mixed,
    act,
    ig,
    d_out,
    jg,
    dka,
    dva,
    svec,
    outp,
    rx,
    rz,
    acc,
    cw,
    cq,
    cd,
    a1,
    aq,
    pkc,
    pkd,
    w1s,
    ssem,
    rsem,
    lsem,
    xfree,
    zfree,
    cfree,
    yfree,
):
    dp = lax.axis_index("dp")
    c = lax.axis_index("ctx")
    core = dp % 2
    y = dp // 2
    xx = c % 2
    z = c // 2
    cx = z * 2 + (1 - xx)
    mid = (z == 1) | (z == 2)
    end = (z == 0) | (z == 3)
    far = jnp.where(z < 2, 1, 0)
    zp = [z, z + 1 - 2 * (z % 2), 1 + far, 3 * far]
    dp_core = y * 2 + (1 - core)
    dp_y = (1 - y) * 2 + core
    dp_diag = (1 - y) * 2 + (1 - core)
    to_x = (dp, cx)
    to_outer = (dp, zp[1] * 2 + xx)
    to_inner = (dp, jnp.where(mid, 3 - z, zp[1]) * 2 + xx)
    to_core = (dp_core, c)
    to_y = (dp_y, c)
    dp_peers = [dp_core, dp_y, dp_diag]
    ctx_peers = [(c + o) % NC for o in range(1, NC)]
    pending = []
    counter = [0]

    def rows_of(i, n):
        return pl.ds(pl.multiple_of(i * n, n), n)

    def send(src, dst, ridx, dev, sidx=None):
        if sidx is None:
            sidx = counter[0]
            counter[0] += 1
        copy = pltpu.make_async_remote_copy(
            src_ref=src,
            dst_ref=dst,
            send_sem=ssem.at[sidx],
            recv_sem=rsem.at[ridx],
            device_id=dev,
            device_id_type=MESH_ID,
        )
        copy.start()
        return copy

    def new_send():
        counter[0] += 1
        return counter[0] - 1

    def got(dst, ridx):
        pltpu.make_async_remote_copy(
            src_ref=dst,
            dst_ref=dst,
            send_sem=ssem.at[0],
            recv_sem=rsem.at[ridx],
            device_id=to_x,
            device_id_type=MESH_ID,
        ).wait_recv()

    def sent(src, sidx):
        pltpu.make_async_remote_copy(
            src_ref=src,
            dst_ref=src,
            send_sem=ssem.at[sidx],
            recv_sem=rsem.at[0],
            device_id=to_x,
            device_id_type=MESH_ID,
        ).wait_send()

    def signal(sem, dev):
        pl.semaphore_signal(sem, inc=1, device_id=dev, device_id_type=MESH_ID)

    barrier = pltpu.get_barrier_semaphore()
    for p in dp_peers:
        signal(barrier, (p, c))
    for p in ctx_peers:
        signal(barrier, (dp, p))
    pl.semaphore_wait(barrier, len(dp_peers) + len(ctx_peers))

    pair_cols = outp.at[pl.ds(0, 512)]
    for i in range(12):
        pltpu.make_async_copy(
            wq_ref.at[:, pl.ds(pl.multiple_of(i * 512 + z * 128, 128), 128)],
            pair_cols.at[:, pl.ds(i * 128, 128)],
            lsem.at[0],
        ).start()

    def row_of(ref):
        return ref[...].astype(F32).reshape(1, ref.shape[0])

    bq_all = row_of(bq_ref)
    bq_own = [own_lanes(bq_all[:, j * 512 : (j + 1) * 512], 64, c, NC) for j in range(3)]
    b1_own = own_lanes(row_of(b1_ref), 256, c, NC)
    wide = [row_of(r) for r in (gain_ref, shift_ref, bd_ref, b2_ref)]
    wide += [jnp.concatenate(bq_own + [jnp.zeros((1, 320), F32)], 1)]
    wide += [jnp.concatenate([b1_own, jnp.zeros((1, 256), F32)], 1)]
    vbuf[dp] = jnp.concatenate(wide + [jnp.zeros((10, 512), F32)], 0).astype(BF)
    mbuf[c] = jnp.concatenate([seg_ref[...], pos_ref[...], jnp.zeros((6, BLK), jnp.int32)], 0)
    for p in dp_peers:
        pending.append(send(vbuf.at[dp], vbuf.at[dp], R_V + dp, (p, c)))
    for p in ctx_peers:
        pending.append(send(mbuf.at[c], mbuf.at[c], R_M + c, (dp, p)))

    def blk(buf, cc):
        return buf.at[rows_of(cc, BLK)]

    relays = []

    def send_if(cond, kind, buf, base, cc, dev):
        s = new_send()

        @pl.when(cond)
        def _():
            send(blk(buf, cc), blk(buf, cc), base + cc, dev, s)

        relays.append((kind, s))

    def own_x(buf, base):
        pending.append(send(blk(buf, c), blk(buf, c), base + c, to_x))

    def arrive(buf, base, k, who=None):
        cc = zp[k] * 2 + xx
        to_next = to_inner if k == 1 else to_outer
        if who is None:
            got(blk(buf, cc), base + cc)
            send_if(mid, 1, buf, base, cc, to_next)
            pending.append(send(blk(buf, cc), blk(buf, cc), base + cc, to_x))
            return
        sz, sx = new_send(), new_send()

        @pl.when(mid if who else end)
        def _():
            got(blk(buf, cc), base + cc)
            if who:
                send(blk(buf, cc), blk(buf, cc), base + cc, to_next, sz)
            send(blk(buf, cc), blk(buf, cc), base + cc, to_x, sx)

        relays.extend([(1, sz), (1, sx)] if who else [(0, sx)])

    def from_x(buf, base, k):
        cc = zp[k] * 2 + (1 - xx)
        got(blk(buf, cc), base + cc)

    gb[rows_of(c, BLK), :] = g_ref[...]
    own_x(gb, R_G)

    def pieces(t, slot):
        if t == 0:
            return [(wq.at[rows_of(slot, 512)], wq.at[rows_of(slot, 512)])]
        if t == 1:
            return [
                (
                    w1_ref.at[:, pl.ds(pl.multiple_of(q * 2048 + c * 256, 256), 256)],
                    w1.at[rows_of(slot, 512), pl.ds(q * 256, 256)],
                )
                for q in range(ND)
            ]
        if t == 2:
            return [
                (
                    w2_ref.at[rows_of(c, 256), pl.ds(half * 1024, 1024)],
                    w2.at[pl.ds(pl.multiple_of(half * 1024 + slot * 256, 256), 256)],
                )
                for half in range(2)
            ]
        return [(wd_ref.at[rows_of(c, 64)], wd.at[rows_of(slot, 64)])]

    def whole(t):
        return [wq.at[pl.ds(0, 512)], w1.at[pl.ds(0, 512)], w2.at[pl.ds(0, 512)], wd.at[pl.ds(0, 64)]][t]

    wsent = []

    def weight_send(t):
        sy, sc = new_send(), new_send()
        for src, dst in pieces(t, dp):
            send(src, dst, R_WY + t, to_y, sy)
        for src, dst in pieces(t, dp):
            send(src, dst, R_WC + t, to_core, sc)
        if t > 0:
            for src, dst in pieces(t, dp):
                pltpu.make_async_copy(src, dst, lsem.at[t]).start()
        wsent.extend([(t, sy), (t, sc)])

    def pick_heads():
        pltpu.make_async_copy(wq_ref.at[:, pl.ds(0, 1536)], pair_cols.at[:, pl.ds(0, 1536)], lsem.at[0]).wait()
        low_half = lax.broadcasted_iota(jnp.int32, (512, 128), 1) < 64
        for i in range(6):
            a = outp[0:512, i * 256 : i * 256 + 128].astype(F32)
            b = outp[0:512, i * 256 + 128 : i * 256 + 256].astype(F32)
            left = jnp.where(xx == 1, pltpu.roll(a, 64, 1), a)
            right = jnp.where(xx == 0, pltpu.roll(b, 64, 1), b)
            wq[rows_of(dp, 512), i * 128 : (i + 1) * 128] = jnp.where(low_half, left, right).astype(BF)

    pick_heads()
    for t in range(4):
        weight_send(t)

    def weight_forward(t):
        got(whole(t), R_WY + t)
        sf = new_send()
        for _, dst in pieces(t, dp_y):
            send(dst, dst, R_WF + t, to_core, sf)
        wsent.append((t, sf))

    def weight_ready(t):
        got(whole(t), R_WC + t)
        got(whole(t), R_WF + t)
        if t > 0:
            pltpu.make_async_copy(whole(t), whole(t), lsem.at[t]).wait()

    for p in dp_peers:
        got(vbuf.at[p], R_V + p)
    slots = [vbuf[s].astype(F32) for s in range(ND)]

    def vec_row(i):
        return jnp.concatenate([slots[s][i : i + 1] for s in range(ND)], 1)

    gain = vec_row(0)
    shift = vec_row(1)
    out_bias = vec_row(2) + vec_row(3)
    bias_q = jnp.concatenate([slots[i // 3][4:5, (i % 3) * 64 : (i % 3 + 1) * 64] for i in range(12)], 1)
    bias_1 = jnp.concatenate([slots[s][5:6, :256] for s in range(ND)], 1)

    def norm_parts():
        xv = x_ref[...].astype(F32)
        center = xv - jnp.mean(xv, axis=1, keepdims=True)
        inv = lax.rsqrt(jnp.mean(center * center, axis=1, keepdims=True) + EPS)
        return center * inv, inv

    xhat, _ = norm_parts()
    nb[rows_of(c, BLK), :] = (xhat * gain + shift).astype(BF)

    own_x(nb, R_N)
    pending.append(send(blk(nb, c), blk(nb, c), R_N + c, to_outer))
    send_if(mid, 1, nb, R_N, c, to_inner)
    send_if(end, 0, gb, R_G, c, to_outer)

    for p in ctx_peers:
        got(mbuf.at[p], R_M + p)
    seg = jnp.concatenate([mbuf[i, 0:1, :] for i in range(NC)], 1)
    pos = jnp.concatenate([mbuf[i, 1:2, :] for i in range(NC)], 1).astype(F32)
    first_len = jnp.sum((seg == 0).astype(jnp.int32).astype(F32), axis=1, keepdims=True).astype(jnp.int32)
    last_start = jnp.sum((seg <= 1).astype(jnp.int32).astype(F32), axis=1, keepdims=True).astype(jnp.int32)
    qstart[...] = jnp.where(seg == 0, 0, jnp.where(seg == 1, first_len, last_start))
    lane = lax.broadcasted_iota(jnp.int32, (16, PAIR), 0)
    freqs = jnp.zeros((16, PAIR), F32)
    for i, value in enumerate(FREQS):
        freqs = jnp.where(lane == i, value, freqs)
    for i in range(4):
        angles = freqs * pos[:, i * PAIR : (i + 1) * PAIR]
        cos_h, sin_h = jnp.cos(angles), jnp.sin(angles)
        ones, zeros = jnp.ones((32, PAIR), F32), jnp.zeros((32, PAIR), F32)
        ctab[i * PAIR : (i + 1) * PAIR, :] = jnp.transpose(
            jnp.concatenate([cos_h, cos_h, ones, cos_h, cos_h, ones], 0)
        )
        stab[i * PAIR : (i + 1) * PAIR, :] = jnp.transpose(
            jnp.concatenate([-sin_h, sin_h, zeros, -sin_h, sin_h, zeros], 0)
        )

    def turn(v, rows, sign):
        cos_t, sin_t = ctab[rows, :], stab[rows, :]
        halves = []
        for i in range(v.shape[1] // 128):
            part = v[:, i * 128 : (i + 1) * 128]
            halves.append(part * cos_t + sign * (swap_turned(part) * sin_t))
        return jnp.concatenate(halves, 1) if len(halves) > 1 else halves[0]

    def project(pair):
        rows = rows_of(pair, PAIR)
        xv = nb[rows, :]
        for part in range(3):
            cols = slice(part * 256, (part + 1) * 256)
            val = dot_nn(xv, wq[:, cols]) + bias_q[:, cols]
            if part < 2:
                val = turn(val, rows, 1.0)
            low = val.astype(BF)
            dest = (qh, kh, vh)[part]
            for h in range(HEADS_C):
                dest[h, rows, :] = low[:, h * 64 : (h + 1) * 64]
            if part > 0:
                (k_t, v_t)[part - 1][:, rows] = jnp.transpose(low)

    def project_ff(pair):
        rows = rows_of(pair, PAIR)
        xv = nb[rows, :]
        for f in range(4):
            cols = slice(f * 256, (f + 1) * 256)
            u = dot_nn(xv, w1[:, cols]) + bias_1[:, cols]
            uu = u * u
            th = jnp.tanh(GELU_K * (u + GELU_A * (uu * u)))
            half = 0.5 * (1.0 + th)
            act[rows, cols] = (u * half).astype(BF)
            slope = half + 0.5 * u * (1.0 - th * th) * (GELU_K * (1.0 + 3.0 * GELU_A * uu))
            ig[rows, cols] = slope.astype(BF)

    arrive(nb, R_N, 1)
    send_if(mid, 1, gb, R_G, c, to_inner)
    arrive(nb, R_N, 2, True)
    weight_forward(0)
    weight_ready(0)
    from_x(nb, R_N, 0)
    project(zp[0])
    arrive(nb, R_N, 2, False)
    arrive(nb, R_N, 3)
    send_if(mid, 1, gb, R_G, c, to_outer)
    arrive(gb, R_G, 1, True)
    arrive(gb, R_G, 2, True)
    from_x(nb, R_N, 1)
    project(zp[1])
    weight_forward(1)
    weight_ready(1)
    project_ff(zp[0])
    from_x(nb, R_N, 2)
    project(zp[2])
    project_ff(zp[1])
    arrive(gb, R_G, 1, False)
    from_x(nb, R_N, 3)
    project(zp[3])
    project_ff(zp[2])
    project_ff(zp[3])
    arrive(gb, R_G, 3, True)

    def masked(s, i, kv):
        ji = lax.broadcasted_iota(jnp.int32, (kv, PAIR), 0)
        qi = lax.broadcasted_iota(jnp.int32, (1, PAIR), 1) + i * PAIR
        ok = (ji <= qi) & (ji >= qstart[:, i * PAIR : (i + 1) * PAIR])
        return ok, jnp.where(ok, s * SCALE, MASKED)

    def head_rows(h):
        return pl.ds(pl.multiple_of(h * 64, 64), 64)

    def attend(h, carry):
        for i in range(4):
            kv = (i + 1) * PAIR
            cols = slice(i * PAIR, (i + 1) * PAIR)
            _, s = masked(dot_nt(kh[h, 0:kv, :], qh[h, cols, :]), i, kv)
            m = jnp.max(s, axis=0, keepdims=True)
            p = jnp.exp(s - m)
            total = jnp.sum(p, axis=0, keepdims=True)
            probs = (p * (1.0 / total)).astype(BF)
            o_t[head_rows(h), cols] = dot_nn(v_t[head_rows(h), 0:kv], probs)
            lse[h, :, cols] = m + jnp.log(total)
        return carry

    lax.fori_loop(0, 2, attend, 0)
    arrive(gb, R_G, 2, False)
    lax.fori_loop(2, 4, attend, 0)
    for i in range(4):
        cols = slice(i * PAIR, (i + 1) * PAIR)
        mixed[cols, :] = jnp.transpose(o_t[:, cols]).astype(BF)
    weight_forward(2)
    weight_forward(3)
    weight_ready(2)
    weight_ready(3)
    arrive(gb, R_G, 3, False)

    x_sent = [[None] * 4, [None] * 4]
    z_sent = [[None] * 4, [None] * 4]
    src_of = (outp, gb)

    def reduce_x(op, k):
        cc = zp[k] * 2 + (1 - xx)
        if op == 1:
            pl.semaphore_wait(xfree.at[k], 1)
        x_sent[op][k] = send(blk(src_of[op], cc), rx.at[k], R_X[op] + k, to_x)

    def z_send(op, k, slot, dev, s):
        if op == 1:
            pl.semaphore_wait(zfree.at[slot], 1)
        send(rx.at[k], rz.at[slot], R_Z[op] + slot, dev, s)

    def reduce_z(op, k, middle):
        if z_sent[op][k] is None:
            z_sent[op][k] = new_send()
        s = z_sent[op][k]

        if not middle:

            @pl.when(end)
            def _():
                got(rx.at[k], R_X[op] + k)
                own = src_of[op][rows_of(zp[k] * 2 + xx, BLK), :].astype(F32)
                rx[k] = (rx[k].astype(F32) + own).astype(BF)
                z_send(op, k, 3 - k, to_outer, s)

            return
        slot_in = {3: 0, 2: 1, 1: 3}[k]

        @pl.when(mid)
        def _():
            got(rx.at[k], R_X[op] + k)
            got(rz.at[slot_in], R_Z[op] + slot_in)
            own = src_of[op][rows_of(zp[k] * 2 + xx, BLK), :].astype(F32)
            rx[k] = (rx[k].astype(F32) + own + rz[slot_in].astype(F32)).astype(BF)
            if op == 0:
                signal(zfree.at[slot_in], to_inner if k == 1 else to_outer)
            z_send(op, k, 0 if k == 1 else 6 - k, to_outer if k == 1 else to_inner, s)

    def reduced(op, total):
        @pl.when(end)
        def _():
            got(rz.at[0], R_Z[op])
            acc[...] = total + rz[0].astype(F32)
            if op == 0:
                signal(zfree.at[0], to_outer)

        @pl.when(mid)
        def _():
            got(rz.at[2], R_Z[op] + 2)
            got(rz.at[4], R_Z[op] + 4)
            acc[...] = total + rz[2].astype(F32) + rz[4].astype(F32)
            if op == 0:
                signal(zfree.at[2], to_outer)
                signal(zfree.at[4], to_inner)

        return acc[...]

    def partial_out(pair):
        rows = rows_of(pair, PAIR)
        mv, av = mixed[rows, :], act[rows, :]
        for n in range(8):
            cols = slice(n * 256, (n + 1) * 256)
            half, off = n // 4, (n % 4) * 256
            val = dot_nn(mv, wd[:, cols]) + dot_nn(av, w2[half * 1024 : (half + 1) * 1024, off : off + 256])
            outp[rows, cols] = val.astype(BF)

    for k in (3, 2, 1, 0):
        partial_out(zp[k])
        reduce_x(0, k)

    svec[...] = jnp.zeros_like(svec)

    def backward_in(pair):
        rows = rows_of(pair, PAIR)
        ga, gc = gb[rows, 0:1024], gb[rows, 1024:2048]
        svec[0:1, :] += jnp.sum(gb[rows, :].astype(F32), axis=0, keepdims=True)
        for f in range(4):
            cols = slice(f * 256, (f + 1) * 256)
            val = dot_nt(ga, w2[f * 256 : (f + 1) * 256, :]) + dot_nt(gc, w2[1024 + f * 256 : 1024 + (f + 1) * 256, :])
            low = (val * ig[rows, cols].astype(F32)).astype(BF)
            ig[rows, cols] = low
            svec[1:2, cols] += jnp.sum(low.astype(F32), axis=0, keepdims=True)
        mg = (dot_nt(ga, wd[:, 0:1024]) + dot_nt(gc, wd[:, 1024:2048])).astype(BF)
        for h in range(HEADS_C):
            d_out[h, rows, :] = mg[:, h * 64 : (h + 1) * 64]
        prod = jnp.transpose(mg.astype(F32)) * o_t[:, rows]
        for h in range(HEADS_C):
            delta[h, :, rows] = jnp.sum(prod[h * 64 : (h + 1) * 64], axis=0, keepdims=True)

    for k in range(4):
        from_x(gb, R_G, k)
        backward_in(zp[k])

    for t, s in wsent:
        sent(whole(t), s)
    for s in pending:
        s.wait_send()
    pending.clear()

    for kind, cond in ((1, mid), (0, end)):

        @pl.when(cond)
        def _():
            for kk, s in relays:
                if kk == kind:
                    sent(blk(gb, 0), s)

    def grad_ff_in():
        for f in range(4):
            for n in range(2):
                rows, cols = slice(f * 512, (f + 1) * 512), slice(n * 512, (n + 1) * 512)
                w1s[rows, cols] = dot_tn(nb[:, rows], ig[:, cols]).astype(BF)

    def grad_ff_out():
        for f in range(2):
            for n in range(4):
                cols = slice((n % 2) * 512, (n % 2 + 1) * 512)
                first = (n // 2) * 1024 + f * 512
                w2[first : first + 512, cols] = dot_tn(
                    act[:, f * 512 : (f + 1) * 512], gb[:, n * 512 : (n + 1) * 512]
                ).astype(BF)

    def grad_dense():
        for n in range(4):
            cols = slice(n * 512, (n + 1) * 512)
            wd[:, cols] = dot_tn(mixed[...], gb[:, cols]).astype(BF)

    def grad_joint():
        for f in range(4):
            rows = slice(f * 512, (f + 1) * 512)
            for n in range(3):
                cols = slice(n * 256, (n + 1) * 256)
                wq[rows, cols] = dot_tn(nb[:, rows], jg[:, cols]).astype(BF)

    def quarter(t, q):
        if t == 2:
            return [w2.at[pl.ds(pl.multiple_of(half * 1024 + q * 256, 256), 256)] for half in range(2)]
        if t == 3:
            return [wd.at[rows_of(q, 64)]]
        return [(wq, w1s)[t].at[rows_of(q, 512)]]

    def core_slot(t, yy):
        if t == 0:
            return [cq.at[yy]]
        if t == 1:
            return [cw.at[yy]]
        if t == 2:
            return [cw.at[yy, pl.ds(half * 256, 256)] for half in range(2)]
        return [cd.at[yy]]

    core_sent, y_sent = {}, {}

    def core_send(t):
        ids = []
        for yy in range(2):
            s = new_send()
            for src, dst in zip(quarter(t, yy * 2 + (1 - core)), core_slot(t, yy)):
                send(src, dst, R_C + t * 2 + yy, to_core, s)
            ids.append(s)
        core_sent[t] = ids

    def slot_whole(t, yy):
        return (cq, cw, cw, cd)[t].at[yy]

    def landing(t):
        return quarter(t, 1 - core)

    def y_send(t):
        for s in core_sent[t]:
            sent(slot_whole(t, 0), s)
        signal(yfree.at[t], to_y)
        for yy in range(2):
            got(slot_whole(t, yy), R_C + t * 2 + yy)
            for own, other in zip(quarter(t, yy * 2 + core), core_slot(t, yy)):
                own[...] = (own[...].astype(F32) + other[...].astype(F32)).astype(BF)
        if t == 1:
            signal(cfree.at[0], to_core)
        pl.semaphore_wait(yfree.at[t], 1)
        s = new_send()
        for src, dst in zip(quarter(t, (1 - y) * 2 + core), landing(t)):
            send(src, dst, R_Y + t, to_y, s)
        y_sent[t] = s

    def total(t):
        got(whole(t), R_Y + t)
        for own, other in zip(quarter(t, y * 2 + core), landing(t)):
            own[...] = (own[...].astype(F32) + other[...].astype(F32)).astype(BF)

    def exchange(t, buf, base):
        total(t)
        first = (y * 2 + core) * 8
        buf[c] = (wq, w1s)[t][rows_of(first + c, 64), :]
        for p in ctx_peers:
            pending.append(send((wq, w1s)[t].at[rows_of(first + p, 64)], buf.at[c], base + c, (dp, p)))

    grad_ff_in()
    core_send(1)
    grad_ff_out()
    grad_dense()

    def partial_ff(pair):
        rows = rows_of(pair, PAIR)
        iv = ig[rows, :]
        for n in range(8):
            cols = slice(n * 256, (n + 1) * 256)
            gb[rows, cols] = dot_nt(iv, w1[cols, :]).astype(BF)

    def partial_attn(pair):
        rows = rows_of(pair, PAIR)
        jv = jg[rows, :]
        svec[1:2, 1024:1792] += jnp.sum(jv.astype(F32), axis=0, keepdims=True)
        for n in range(8):
            cols = slice(n * 256, (n + 1) * 256)
            gb[rows, cols] = (dot_nt(jv, wq[cols, :]) + gb[rows, cols].astype(F32)).astype(BF)

    reduce_z(0, 3, False)
    y_send(1)
    pl.semaphore_wait(cfree.at[0], 1)
    core_send(2)
    core_send(3)
    for k in range(4):
        partial_ff(zp[k])
    reduce_z(0, 2, False)

    def attend_back(hp, carry):
        for j in range(2):
            h = hp * 2 + j
            for i in (3, 2, 1, 0):
                kv = (i + 1) * PAIR
                cols = slice(i * PAIR, (i + 1) * PAIR)
                ok, s = masked(dot_nt(kh[h, 0:kv, :], qh[h, cols, :]), i, kv)
                p = jnp.where(ok, jnp.exp(s - lse[h, :, cols]), 0.0)
                dp_t = dot_nt(vh[h, 0:kv, :], d_out[h, cols, :])
                ds = (p * (dp_t - delta[h, :, cols])).astype(BF)
                dv = dot_nn(p.astype(BF), d_out[h, cols, :])
                dk = dot_nn(ds, qh[h, cols, :])
                if i == 3:
                    dva[j, 0:kv, :] = dv
                    dka[j, 0:kv, :] = dk
                else:
                    dva[j, 0:kv, :] += dv
                    dka[j, 0:kv, :] += dk
                o_t[head_rows(h), cols] = dot_nn(k_t[head_rows(h), 0:kv], ds)
        for i in range(4):
            rows = slice(i * PAIR, (i + 1) * PAIR)
            kk = jnp.concatenate([dka[0, rows, :], dka[1, rows, :]], 1) * SCALE
            vv = jnp.concatenate([dva[0, rows, :], dva[1, rows, :]], 1)
            jg[rows, pl.ds(pl.multiple_of(256 + hp * 128, 128), 128)] = turn(kk, rows, -1.0).astype(BF)
            jg[rows, pl.ds(pl.multiple_of(512 + hp * 128, 128), 128)] = vv.astype(BF)
        return carry

    lax.fori_loop(0, 1, attend_back, 0)
    y_send(2)
    y_send(3)
    reduce_z(0, 3, True)
    lax.fori_loop(1, 2, attend_back, 0)
    for i in range(4):
        rows = slice(i * PAIR, (i + 1) * PAIR)
        jg[rows, 0:256] = turn(jnp.transpose(o_t[:, rows]) * SCALE, rows, -1.0).astype(BF)

    def next_x(k):
        sent(rx.at[k], z_sent[0][k])
        signal(xfree.at[k], to_x)
        reduce_x(1, k)

    reduce_z(0, 1, False)
    partial_attn(zp[3])
    partial_attn(zp[2])
    reduce_z(0, 2, True)
    partial_attn(zp[1])
    partial_attn(zp[0])
    next_x(3)
    exchange(1, a1, R_A1)
    reduce_z(0, 1, True)
    grad_joint()
    core_send(0)
    next_x(2)

    got(rx.at[0], R_X[0])
    x_sent[0][0].wait_send()
    outp[rows_of(cx, BLK), :] = rx[0]
    signal(xfree.at[0], to_x)
    next_x(1)
    reduce_x(1, 0)
    y_send(0)

    total_o = outp[rows_of(cx, BLK), :].astype(F32) + outp[rows_of(c, BLK), :].astype(F32)
    out_ref[...] = (x_ref[...].astype(F32) + out_bias + reduced(0, total_o)).astype(BF)

    outs = []

    def out_copy(src, dst):
        copy = pltpu.make_async_copy(src, dst, lsem.at[4 + len(outs)])
        copy.start()
        outs.append(copy)

    def finish_out_weights():
        total(2)
        for half in range(2):
            out_copy(quarter(2, y * 2 + core)[half], w2s_ref.at[:, pl.ds(half * 1024, 1024)])
        total(3)
        out_copy(quarter(3, y * 2 + core)[0], wds_ref)

    reduce_z(1, 3, False)
    reduce_z(1, 2, False)
    reduce_z(1, 3, True)
    reduce_z(1, 1, False)
    reduce_z(1, 2, True)
    exchange(0, aq, R_AQ)
    reduce_z(1, 1, True)
    finish_out_weights()

    got(rx.at[0], R_X[1])
    ng = reduced(1, rx[0].astype(F32) + gb[rows_of(c, BLK), :].astype(F32))
    xhat, inv = norm_parts()
    e = ng * gain
    m1 = jnp.mean(e, axis=1, keepdims=True)
    m2 = jnp.mean(e * xhat, axis=1, keepdims=True)
    xgrad_ref[...] = (g_ref[...].astype(F32) + (e - m1 - xhat * m2) * inv).astype(BF)
    pkc[c, 0:16, :] = as_rows(jnp.sum(ng * xhat, axis=0, keepdims=True))
    pkc[c, 16:32, :] = as_rows(jnp.sum(ng, axis=0, keepdims=True))
    pkc[c, 32:40, :] = as_rows(svec[1:2, 1024:2048])
    for p in ctx_peers:
        pending.append(send(pkc.at[c], pkc.at[c], R_PC + c, (dp, p)))

    for p in ctx_peers:
        got(pkc.at[p], R_PC + p)
    norm_sum = pkc[0, 0:32, :]
    for i in range(1, NC):
        norm_sum = norm_sum + pkc[i, 0:32, :]
    pkd[dp, 0:32, :] = norm_sum
    for i in range(NC):
        pkd[dp, 32 + i * 8 : 40 + i * 8, :] = pkc[i, 32:40, :]
    pkd[dp, 96:112, :] = as_rows(svec[0:1, :])
    pkd[dp, 112:120, :] = as_rows(svec[1:2, 0:1024])
    for p in dp_peers:
        pending.append(send(pkd.at[dp], pkd.at[dp], R_PD + dp, (p, c)))

    for p in ctx_peers:
        got(a1.at[p], R_A1 + p)
    out_copy(a1, a1_ref)
    for p in dp_peers:
        got(pkd.at[p], R_PD + p)
    small_ref[...] = pkd[0] + pkd[1] + pkd[2] + pkd[3]
    for p in ctx_peers:
        got(aq.at[p], R_AQ + p)
    out_copy(aq, aq_ref)

    for s in pending:
        s.wait_send()
    for k in (3, 2, 1):
        x_sent[0][k].wait_send()
    for k in range(4):
        x_sent[1][k].wait_send()
    for k in (3, 2, 1):
        sent(rx.at[k], z_sent[1][k])
    for t in range(4):
        sent(whole(t), y_sent[t])
    for copy in outs:
        copy.wait()


def finish_kernel(
    out_in,
    xgrad_in,
    small,
    w2s_in,
    wds_in,
    a1_in,
    aq_in,
    out_ref,
    xgrad_ref,
    gain_ref,
    shift_ref,
    wqg_ref,
    bqg_ref,
    wdg_ref,
    bd_ref,
    w1g_ref,
    b1_ref,
    w2g_ref,
    b2_ref,
    w2s,
    wds,
    a1,
    aq,
    w2w,
    wdw,
    w1w,
    wqw,
    rows_o,
    rows_x,
    sems,
):
    dp = lax.axis_index("dp")
    c = lax.axis_index("ctx")
    me = dp * NC + c
    used = []

    def move(src, dst):
        copy = pltpu.make_async_copy(src, dst, sems.at[len(used)])
        copy.start()
        used.append(copy)
        return copy

    pairs = ((w2s_in, w2s), (a1_in, a1), (aq_in, aq), (wds_in, wds), (out_in, rows_o), (xgrad_in, rows_x))
    loads = [move(*p) for p in pairs]
    stores = []
    loads[0].wait()
    w2w[...] = w2s[...].astype(F32)
    stores.append(move(w2w, w2g_ref))
    loads[1].wait()
    for q in range(ND):
        for i in range(NC):
            w1w[:, q * 2048 + i * 256 : q * 2048 + (i + 1) * 256] = a1[i, :, q * 256 : (q + 1) * 256].astype(F32)
    stores.append(move(w1w, w1g_ref))
    loads[2].wait()
    for o in range(12):
        for i in range(NC // 2):
            both = [aq[2 * i + j, :, o * 64 : (o + 1) * 64].astype(F32) for j in range(2)]
            wqw[:, o * 512 + i * 128 : o * 512 + (i + 1) * 128] = jnp.concatenate(both, 1)
    stores.append(move(wqw, wqg_ref))
    loads[3].wait()
    wdw[...] = wds[...].astype(F32)
    stores.append(move(wdw, wdg_ref))
    loads[4].wait()
    stores.append(move(rows_o, out_ref))
    loads[5].wait()
    stores.append(move(rows_x, xgrad_ref))

    def own_64(first):
        row = small[pl.ds(first + me // 2, 1), :]
        return jnp.where(me % 2 == 0, row[:, 0:64], row[:, 64:128]).reshape(64)

    gain_ref[...] = own_64(0)
    shift_ref[...] = own_64(16)
    summed = own_64(96)
    bd_ref[...] = summed
    b2_ref[...] = summed
    rows = small[pl.ds(112 + dp * 2, 2), :]
    b1_ref[...] = jnp.concatenate([rows[0:1], rows[1:2]], 1).reshape(256)

    picked = []
    for j in range(3):
        head = me * 3 + j
        o, i = head // NC, head % NC
        row = small[pl.ds(32 + i * 8 + o // 2, 1), :]
        picked.append(jnp.where(o % 2 == 0, row[:, 0:64], row[:, 64:128]))
    bqg_ref[...] = jnp.concatenate(picked, 1).reshape(192)
    for copy in stores:
        copy.wait()


def fast_device(inputs, positions, seq_ids, ln_gain, ln_bias, w_qkv, b_qkv, w_dense, b_dense, w_fc1, b_fc1, w_fc2, b_fc2, cotangent):
    width = inputs.shape[2]
    vm = pl.BlockSpec(memory_space=pltpu.VMEM)
    hbm = pl.BlockSpec(memory_space=pl.ANY)
    dma = pltpu.SemaphoreType.DMA
    reg = pltpu.SemaphoreType.REGULAR
    sd = jax.ShapeDtypeStruct
    parts = pl.pallas_call(
        layer_kernel,
        out_shape=(
            sd((BLK, width), BF),
            sd((BLK, width), BF),
            sd((120, 128), F32),
            sd((256, 2048), BF),
            sd((64, 2048), BF),
            sd((NC, 64, 1024), BF),
            sd((NC, 64, 768), BF),
        ),
        in_specs=[vm] * 10 + [hbm] * 4,
        out_specs=(vm, vm, vm, hbm, hbm, hbm, hbm),
        scratch_shapes=[
            pltpu.VMEM((TOK, 2048), BF),
            pltpu.VMEM((TOK, 2048), BF),
            pltpu.VMEM((2048, 768), BF),
            pltpu.VMEM((2048, 1024), BF),
            pltpu.VMEM((2048, 1024), BF),
            pltpu.VMEM((256, 2048), BF),
            pltpu.VMEM((ND, 16, 512), BF),
            pltpu.VMEM((NC, 8, BLK), jnp.int32),
            pltpu.VMEM((TOK, 128), F32),
            pltpu.VMEM((TOK, 128), F32),
            pltpu.VMEM((1, TOK), jnp.int32),
            pltpu.VMEM((4, TOK, 64), BF),
            pltpu.VMEM((4, TOK, 64), BF),
            pltpu.VMEM((4, TOK, 64), BF),
            pltpu.VMEM((256, TOK), BF),
            pltpu.VMEM((256, TOK), BF),
            pltpu.VMEM((256, TOK), F32),
            pltpu.VMEM((4, 1, TOK), F32),
            pltpu.VMEM((4, 1, TOK), F32),
            pltpu.VMEM((TOK, 256), BF),
            pltpu.VMEM((TOK, 1024), BF),
            pltpu.VMEM((TOK, 1024), BF),
            pltpu.VMEM((4, TOK, 64), BF),
            pltpu.VMEM((TOK, 768), BF),
            pltpu.VMEM((2, TOK, 64), F32),
            pltpu.VMEM((2, TOK, 64), F32),
            pltpu.VMEM((8, 2048), F32),
            pltpu.VMEM((TOK, 2048), BF),
            pltpu.VMEM((4, BLK, 2048), BF),
            pltpu.VMEM((5, BLK, 2048), BF),
            pltpu.VMEM((BLK, 2048), F32),
            pltpu.VMEM((2, 512, 1024), BF),
            pltpu.VMEM((2, 512, 768), BF),
            pltpu.VMEM((2, 64, 2048), BF),
            pltpu.VMEM((NC, 64, 1024), BF),
            pltpu.VMEM((NC, 64, 768), BF),
            pltpu.VMEM((NC, 40, 128), F32),
            pltpu.VMEM((ND, 120, 128), F32),
            pltpu.VMEM((2048, 1024), BF),
            dma((N_SEND,)),
            dma((N_RECV,)),
            dma((9,)),
            reg((4,)),
            reg((5,)),
            reg((1,)),
            reg((4,)),
        ],
        compiler_params=pltpu.CompilerParams(
            collective_id=0, has_side_effects=True, vmem_limit_bytes=63 * 1024 * 1024
        ),
        name="layer",
    )(
        inputs[0], cotangent[0], seq_ids, positions, ln_gain, ln_bias, b_dense, b_fc2, b_qkv, b_fc1, w_qkv, w_fc1, w_fc2, w_dense
    )
    done = pl.pallas_call(
        finish_kernel,
        out_shape=(
            sd((BLK, width), BF),
            sd((BLK, width), BF),
            sd((64,), F32),
            sd((64,), F32),
            sd((64, 6144), F32),
            sd((192,), F32),
            sd((64, 2048), F32),
            sd((64,), F32),
            sd((64, 8192), F32),
            sd((256,), F32),
            sd((256, 2048), F32),
            sd((64,), F32),
        ),
        in_specs=[hbm, hbm, vm, hbm, hbm, hbm, hbm],
        out_specs=(hbm, hbm, vm, vm, hbm, vm, hbm, vm, hbm, vm, hbm, vm),
        scratch_shapes=[
            pltpu.VMEM((256, 2048), BF),
            pltpu.VMEM((64, 2048), BF),
            pltpu.VMEM((NC, 64, 1024), BF),
            pltpu.VMEM((NC, 64, 768), BF),
            pltpu.VMEM((256, 2048), F32),
            pltpu.VMEM((64, 2048), F32),
            pltpu.VMEM((64, 8192), F32),
            pltpu.VMEM((64, 6144), F32),
            pltpu.VMEM((BLK, 2048), BF),
            pltpu.VMEM((BLK, 2048), BF),
            dma((12,)),
        ],
        compiler_params=pltpu.CompilerParams(vmem_limit_bytes=62 * 1024 * 1024),
        name="finish",
    )(*parts)
    return (done[0][None], done[1][None]) + tuple(done[2:])


def solution(mesh):
    placed = (
        P("dp", "ctx", None),
        P("dp", "ctx"),
        P("dp", "ctx"),
        P("dp"),
        P("dp"),
        P("dp", None),
        P("dp"),
        P("dp", None),
        P("dp"),
        P("dp", None),
        P("dp"),
        P("dp", None),
        P("dp"),
        P("dp", "ctx", None),
    )
    fits = mesh.shape["dp"] == ND and mesh.shape["ctx"] == NC
    return jax.shard_map(
        fast_device if fits else per_device,
        mesh=mesh,
        in_specs=placed,
        out_specs=(
            P("dp", "ctx", None),
            P("dp", "ctx", None),
            P(("dp", "ctx")),
            P(("dp", "ctx")),
            P(("dp", "ctx"), None),
            P(("dp", "ctx")),
            P(("dp", "ctx"), None),
            P(("dp", "ctx")),
            P(("dp", "ctx"), None),
            P(("dp", "ctx")),
            P(("dp", "ctx"), None),
            P(("dp", "ctx")),
        ),
        check_vma=False,
    )
```

```python
import math

import jax
import jax.numpy as jnp
import numpy as np
from jax import lax
from jax.experimental import pallas as pl
from jax.experimental.pallas import tpu as pltpu
from jax.sharding import PartitionSpec as P

HEAD_DIM = 64
ROT = 32


EPS = 1e-05
MASKED = -1e30
SCALE = 0.125
BASE = 10000.0


def layer_norm(values, gain_vec, shift_vec):
    center = values - jnp.mean(values, axis=1, keepdims=True)
    spread = jnp.mean(center * center, axis=1, keepdims=True)
    return center * lax.rsqrt(spread + EPS) * gain_vec + shift_vec


def gelu_tanh(values):
    return jax.nn.gelu(values, approximate=True)


def rotate(values, angle_pos):
    row_count = values.shape[0]
    head_count = values.shape[1] // HEAD_DIM
    half_rot = ROT // 2
    split_heads = values.reshape(row_count, head_count, HEAD_DIM)
    freqs = BASE ** (-(jnp.arange(half_rot, dtype=jnp.float32) * 2.0) / ROT)
    angles = angle_pos[:, None] * freqs[None, :]
    cosine = jnp.cos(angles)[:, None, :]
    sine = jnp.sin(angles)[:, None, :]
    first_half = split_heads[:, :, :half_rot]
    second_half = split_heads[:, :, half_rot:ROT]
    turned = jnp.concatenate(
        [
            first_half * cosine - second_half * sine,
            second_half * cosine + first_half * sine,
            split_heads[:, :, ROT:],
        ],
        axis=2,
    )
    return turned.reshape(row_count, head_count * HEAD_DIM)


def visible(query_index, query_seg, key_index, key_seg):
    causal = key_index[None, :] <= query_index[:, None]
    return causal[None] & (key_seg[:, None, :] == query_seg[:, :, None])


def split_cols(values, low_col, high_col):
    return values[:, :, low_col:high_col].reshape(
        values.shape[0], values.shape[1], (high_col - low_col) // HEAD_DIM, HEAD_DIM
    )


def head_scores(query_heads, key_heads, allowed):
    raw = (
        jnp.einsum("sqhd,skhd->shqk", query_heads, key_heads, preferred_element_type=jnp.float32)
        * SCALE
    )
    return jnp.where(allowed[:, None], raw, MASKED)


def unchanged(state):
    return state


def per_device(
    inputs,
    positions,
    seq_ids,
    ln_gain,
    ln_bias,
    w_qkv,
    b_qkv,
    w_dense,
    b_dense,
    w_fc1,
    b_fc1,
    w_fc2,
    b_fc2,
    cotangent,
):
    (
        gain_all,
        shift_all,
        qkv_all,
        qkv_offset,
        dense_all,
        dense_offset,
        fc1_all,
        fc1_offset,
        fc2_all,
        fc2_offset,
    ) = (
        lax.all_gather(ln_gain, "dp", axis=0, tiled=True),
        lax.all_gather(ln_bias, "dp", axis=0, tiled=True),
        lax.all_gather(w_qkv, "dp", axis=0, tiled=True),
        lax.all_gather(b_qkv, "dp", axis=0, tiled=True),
        lax.all_gather(w_dense, "dp", axis=0, tiled=True),
        lax.all_gather(b_dense, "dp", axis=0, tiled=True),
        lax.all_gather(w_fc1, "dp", axis=0, tiled=True),
        lax.all_gather(b_fc1, "dp", axis=0, tiled=True),
        lax.all_gather(w_fc2, "dp", axis=0, tiled=True),
        lax.all_gather(b_fc2, "dp", axis=0, tiled=True),
    )
    stream_count = inputs.shape[0]
    row_count = inputs.shape[1]
    width = inputs.shape[2]
    flat_rows = stream_count * row_count
    resid = inputs.reshape(flat_rows, width).astype(jnp.float32)
    head_count = width // HEAD_DIM
    group_heads = math.gcd(head_count, 8)
    group_cols = group_heads * HEAD_DIM
    group_count = head_count // group_heads
    angle_pos = positions.reshape(flat_rows).astype(jnp.float32)
    own_seg = seq_ids.astype(jnp.bfloat16)
    row_start = lax.axis_index("ctx") * row_count
    own_index = row_start + jnp.arange(row_count, dtype=jnp.int32)
    normed, norm_back = jax.vjp(
        layer_norm, resid, gain_all.astype(jnp.float32), shift_all.astype(jnp.float32)
    )
    hidden = normed.astype(jnp.bfloat16)
    joint = jnp.dot(hidden, qkv_all, preferred_element_type=jnp.float32) + qkv_offset.astype(
        jnp.float32
    )
    queries = (
        rotate(joint[:, :width], angle_pos)
        .astype(jnp.bfloat16)
        .reshape(stream_count, row_count, width)
    )
    keys_own = (
        rotate(joint[:, width : 2 * width], angle_pos)
        .astype(jnp.bfloat16)
        .reshape(stream_count, row_count, width)
    )
    values_own = joint[:, 2 * width :].astype(jnp.bfloat16).reshape(stream_count, row_count, width)
    start_state = (
        jnp.full((stream_count, head_count, row_count), MASKED, jnp.float32),
        jnp.zeros((stream_count, head_count, row_count), jnp.float32),
        jnp.zeros((stream_count, row_count, width), jnp.float32),
    )
    key_part = lax.all_gather(keys_own, "ctx", axis=1, tiled=True)
    value_part = lax.all_gather(values_own, "ctx", axis=1, tiled=True)
    seg_part = lax.all_gather(own_seg, "ctx", axis=1, tiled=True)
    key_count = key_part.shape[1]
    allowed = visible(own_index, own_seg, jnp.arange(key_count, dtype=jnp.int32), seg_part)

    def forward_compute(state):
        peak_in, total_in, accum_in = state
        peak_list, total_list, accum_list = ([], [], [])
        for group_index in range(group_count):
            low_col = group_index * group_cols
            high_col = low_col + group_cols
            low_head = group_index * group_heads
            high_head = low_head + group_heads
            scores = head_scores(
                split_cols(queries, low_col, high_col),
                split_cols(key_part, low_col, high_col),
                allowed,
            )
            old_peak = peak_in[:, low_head:high_head]
            new_peak = jnp.maximum(old_peak, jnp.max(scores, axis=3))
            weights = jnp.where(allowed[:, None], jnp.exp(scores - new_peak[:, :, :, None]), 0.0)
            total_list.append(jnp.sum(weights, axis=3))
            gathered_vals = jnp.einsum(
                "shqk,skhd->sqhd",
                weights.astype(jnp.bfloat16),
                split_cols(value_part, low_col, high_col),
                preferred_element_type=jnp.float32,
            )
            accum_list.append(gathered_vals.reshape(stream_count, row_count, group_cols))
            peak_list.append(new_peak)
        return (
            jnp.concatenate(peak_list, 1),
            jnp.concatenate(total_list, 1),
            jnp.concatenate(accum_list, 2),
        )

    result_state = lax.cond(
        jnp.int32(0) < row_start + row_count, forward_compute, unchanged, start_state
    )
    peak, total, accum = result_state
    attended = (
        accum.reshape(stream_count, row_count, head_count, HEAD_DIM)
        / jnp.transpose(total, (0, 2, 1))[:, :, :, None]
    ).reshape(stream_count, row_count, width)
    log_total = jnp.transpose(peak + jnp.log(total), (0, 2, 1))
    mixed = attended.astype(jnp.bfloat16).reshape(flat_rows, width)
    inner = jnp.dot(hidden, fc1_all, preferred_element_type=jnp.float32) + fc1_offset.astype(
        jnp.float32
    )
    active, gelu_back = jax.vjp(gelu_tanh, inner)
    active_low = active.astype(jnp.bfloat16)
    summed = (
        resid
        + jnp.dot(mixed, dense_all, preferred_element_type=jnp.float32)
        + dense_offset.astype(jnp.float32)
    )
    summed = (
        summed
        + jnp.dot(active_low, fc2_all, preferred_element_type=jnp.float32)
        + fc2_offset.astype(jnp.float32)
    )
    outputs = summed.astype(jnp.bfloat16).reshape(stream_count, row_count, width)
    upstream = cotangent.reshape(flat_rows, width)
    upstream_f = upstream.astype(jnp.float32)
    bias_term = jnp.sum(upstream_f, axis=0)
    fc2_term = jnp.einsum("tf,td->fd", active_low, upstream, preferred_element_type=jnp.float32)
    fc2_sum = lax.psum_scatter(fc2_term, ("dp", "ctx"), scatter_dimension=0, tiled=True)
    fc2_sum, upstream = lax.optimization_barrier((fc2_sum, upstream))
    act_grad = jnp.einsum("td,fd->tf", upstream, fc2_all, preferred_element_type=jnp.float32)
    inner_grad = gelu_back(act_grad)[0].astype(jnp.bfloat16)
    fc1_term = jnp.einsum("td,tf->df", hidden, inner_grad, preferred_element_type=jnp.float32)
    fc1_bias_term = jnp.sum(inner_grad.astype(jnp.float32), axis=0)
    fc1_sum = lax.psum_scatter(fc1_term, ("dp", "ctx"), scatter_dimension=0, tiled=True)
    fc1_sum, mixed, upstream, upstream_f, fc1_bias_term, inner_grad, hidden = lax.optimization_barrier(
        (fc1_sum, mixed, upstream, upstream_f, fc1_bias_term, inner_grad, hidden)
    )
    fc1_bias_sum, bias_sum = (
        lax.psum_scatter(fc1_bias_term, ("dp", "ctx"), scatter_dimension=0, tiled=True),
        lax.psum_scatter(bias_term, ("dp", "ctx"), scatter_dimension=0, tiled=True),
    )
    dense_term = jnp.einsum("td,te->de", mixed, upstream, preferred_element_type=jnp.float32)
    dense_sum = lax.psum_scatter(dense_term, ("dp", "ctx"), scatter_dimension=0, tiled=True)
    dense_sum, upstream, dense_all = lax.optimization_barrier((dense_sum, upstream, dense_all))
    mixed_grad = (
        jnp.einsum("te,de->td", upstream, dense_all, preferred_element_type=jnp.float32)
        .astype(jnp.bfloat16)
        .reshape(stream_count, row_count, width)
    )
    delta = jnp.sum(
        (mixed_grad.astype(jnp.float32) * attended).reshape(
            stream_count, row_count, head_count, HEAD_DIM
        ),
        axis=3,
    )
    zero_block = jnp.zeros((stream_count, row_count, width), jnp.float32)
    query_key_part = lax.all_gather(keys_own, "ctx", axis=1, tiled=True)
    query_value_part = lax.all_gather(values_own, "ctx", axis=1, tiled=True)
    seg_part = lax.all_gather(own_seg, "ctx", axis=1, tiled=True)
    key_count = query_key_part.shape[1]
    query_allowed = visible(own_index, own_seg, jnp.arange(key_count, dtype=jnp.int32), seg_part)

    def query_compute(grad_in):
        step_list = []
        for group_index in range(group_count):
            low_col = group_index * group_cols
            high_col = low_col + group_cols
            low_head = group_index * group_heads
            high_head = low_head + group_heads
            scores = head_scores(
                split_cols(queries, low_col, high_col),
                split_cols(query_key_part, low_col, high_col),
                query_allowed,
            )
            lse_here = jnp.transpose(log_total[:, :, low_head:high_head], (0, 2, 1))[:, :, :, None]
            delta_here = jnp.transpose(delta[:, :, low_head:high_head], (0, 2, 1))[:, :, :, None]
            probs = jnp.where(query_allowed[:, None], jnp.exp(scores - lse_here), 0.0)
            prob_grad = jnp.einsum(
                "sqhd,skhd->shqk",
                split_cols(mixed_grad, low_col, high_col),
                split_cols(query_value_part, low_col, high_col),
                preferred_element_type=jnp.float32,
            )
            score_grad = (probs * (prob_grad - delta_here)).astype(jnp.bfloat16)
            query_step = (
                jnp.einsum(
                    "shqk,skhd->sqhd",
                    score_grad,
                    split_cols(query_key_part, low_col, high_col),
                    preferred_element_type=jnp.float32,
                )
                * SCALE
            )
            step_list.append(query_step.reshape(stream_count, row_count, group_cols))
        return grad_in + jnp.concatenate(step_list, 2)

    result_grad = lax.cond(
        jnp.int32(0) < row_start + row_count, query_compute, unchanged, zero_block
    )
    log_total_all, delta_all = (
        lax.all_gather(log_total, "ctx", axis=1, tiled=True),
        lax.all_gather(delta, "ctx", axis=1, tiled=True),
    )
    start = jnp.int32(0)
    query_part = lax.all_gather(queries, "ctx", axis=1, tiled=True)
    grad_part = lax.all_gather(mixed_grad, "ctx", axis=1, tiled=True)
    seg_part = lax.all_gather(own_seg, "ctx", axis=1, tiled=True)
    query_count = query_part.shape[1]
    query_index = jnp.arange(query_count, dtype=jnp.int32)
    key_allowed = visible(query_index, seg_part, own_index, own_seg)
    lse_part = lax.dynamic_slice_in_dim(log_total_all, start, query_count, 1)

    def key_compute(state):
        key_in, value_in = state
        key_list, value_list = ([], [])
        for group_index in range(group_count):
            low_col = group_index * group_cols
            high_col = low_col + group_cols
            low_head = group_index * group_heads
            high_head = low_head + group_heads
            scores = head_scores(
                split_cols(query_part, low_col, high_col),
                split_cols(keys_own, low_col, high_col),
                key_allowed,
            )
            lse_here = jnp.transpose(lse_part[:, :, low_head:high_head], (0, 2, 1))[:, :, :, None]
            delta_here = jnp.transpose(delta_all[:, :, low_head:high_head], (0, 2, 1))[
                :, :, :, None
            ]
            probs = jnp.where(key_allowed[:, None], jnp.exp(scores - lse_here), 0.0)
            grad_heads = split_cols(grad_part, low_col, high_col)
            value_step = jnp.einsum(
                "shqk,sqhd->skhd",
                probs.astype(jnp.bfloat16),
                grad_heads,
                preferred_element_type=jnp.float32,
            )
            prob_grad = jnp.einsum(
                "sqhd,skhd->shqk",
                grad_heads,
                split_cols(values_own, low_col, high_col),
                preferred_element_type=jnp.float32,
            )
            score_grad = (probs * (prob_grad - delta_here)).astype(jnp.bfloat16)
            key_step = (
                jnp.einsum(
                    "shqk,sqhd->skhd",
                    score_grad,
                    split_cols(query_part, low_col, high_col),
                    preferred_element_type=jnp.float32,
                )
                * SCALE
            )
            key_list.append(key_step.reshape(stream_count, row_count, group_cols))
            value_list.append(value_step.reshape(stream_count, row_count, group_cols))
        return (key_in + jnp.concatenate(key_list, 2), value_in + jnp.concatenate(value_list, 2))

    result_pair = lax.cond(
        start + query_count > row_start, key_compute, unchanged, (zero_block, zero_block)
    )
    key_grad, value_grad = result_pair
    joint_grad = jnp.concatenate(
        [
            rotate(result_grad.reshape(flat_rows, width), -angle_pos),
            rotate(key_grad.reshape(flat_rows, width), -angle_pos),
            value_grad.reshape(flat_rows, width),
        ],
        axis=1,
    ).astype(jnp.bfloat16)
    qkv_term = jnp.einsum("td,te->de", hidden, joint_grad, preferred_element_type=jnp.float32)
    qkv_bias_term = jnp.sum(joint_grad.astype(jnp.float32), axis=0)
    hidden_grad = jnp.einsum("te,de->td", joint_grad, qkv_all, preferred_element_type=jnp.float32)
    hidden_grad = hidden_grad + jnp.einsum(
        "tf,df->td", inner_grad, fc1_all, preferred_element_type=jnp.float32
    )
    resid_grad, gain_term, shift_term = norm_back(hidden_grad)
    input_grad = (
        (upstream_f + resid_grad).astype(jnp.bfloat16).reshape(stream_count, row_count, width)
    )
    gain_sum, shift_sum, qkv_sum, qkv_bias_sum = (
        lax.psum_scatter(gain_term, ("dp", "ctx"), scatter_dimension=0, tiled=True),
        lax.psum_scatter(shift_term, ("dp", "ctx"), scatter_dimension=0, tiled=True),
        lax.psum_scatter(qkv_term, ("dp", "ctx"), scatter_dimension=0, tiled=True),
        lax.psum_scatter(qkv_bias_term, ("dp", "ctx"), scatter_dimension=0, tiled=True),
    )
    return (
        outputs,
        input_grad,
        gain_sum,
        shift_sum,
        qkv_sum,
        qkv_bias_sum,
        dense_sum,
        bias_sum,
        fc1_sum,
        fc1_bias_sum,
        fc2_sum,
        bias_sum,
    )


BF = jnp.bfloat16
F32 = jnp.float32
BLK = 128
PAIR = 256
NC = 8
ND = 4
TOK = NC * BLK
HEADS_C = 4
MESH_ID = pl.DeviceIdType.MESH
GELU_A = 0.044715
GELU_K = math.sqrt(2.0 / math.pi)

R_N, R_G, R_M, R_V = 0, 8, 16, 24
R_WY, R_WC, R_WF = 28, 32, 36
R_X = (40, 44)
R_Z = (48, 53)
R_C, R_Y = 58, 66
R_A1, R_AQ, R_PC, R_PD = 70, 78, 86, 94
R_B = {R_N: 98, R_G: 99}
N_RECV = 100
CUT = 1024
N_SEND = 112
FREQS = [float(np.float32(BASE) ** np.float32(-2.0 * i / ROT)) for i in range(ROT // 2)]


def dot_nn(a, b):
    return lax.dot_general(a, b, (((1,), (0,)), ((), ())), preferred_element_type=F32)


def dot_nt(a, b):
    return lax.dot_general(a, b, (((1,), (1,)), ((), ())), preferred_element_type=F32)


def dot_tn(a, b):
    return lax.dot_general(a, b, (((0,), (0,)), ((), ())), preferred_element_type=F32)


def swap_turned(v):
    lane = lax.broadcasted_iota(jnp.int32, v.shape, 1) % HEAD_DIM
    return jnp.where(lane < 16, pltpu.roll(v, 112, 1), pltpu.roll(v, 16, 1))


def as_rows(v):
    return jnp.concatenate([v[:, i * 128 : (i + 1) * 128] for i in range(v.shape[1] // 128)], 0)


def as_row(v):
    return jnp.concatenate([v[i : i + 1] for i in range(v.shape[0])], 1)


def own_lanes(row, width, index, count):
    total = jnp.zeros((1, width), F32)
    for i in range(count):
        total = total + jnp.where(index == i, row[:, i * width : (i + 1) * width], 0.0)
    return total


def layer_kernel(
    x_ref,
    g_ref,
    seg_ref,
    pos_ref,
    gain_ref,
    shift_ref,
    bd_ref,
    b2_ref,
    bq_ref,
    b1_ref,
    wq_ref,
    w1_ref,
    w2_ref,
    wd_ref,
    out_ref,
    xgrad_ref,
    small_ref,
    w2s_ref,
    wds_ref,
    a1_ref,
    aq_ref,
    nb,
    gb,
    wq,
    w1,
    w2,
    wd,
    vbuf,
    mbuf,
    ctab,
    stab,
    qstart,
    qh,
    kh,
    vh,
    o_t,
    lse,
    delta,
    mixed,
    act,
    ig,
    d_out,
    jg,
    dkv,
    svec,
    outp,
    rx,
    rz,
    cw,
    cq,
    cd,
    a1,
    aq,
    pkc,
    pkd,
    w1s,
    ssem,
    rsem,
    lsem,
    xfree,
    zfree,
    cfree,
    yfree,
):
    dp = lax.axis_index("dp")
    c = lax.axis_index("ctx")
    core = dp % 2
    y = dp // 2
    xx = c % 2
    z = c // 2
    cx = z * 2 + (1 - xx)
    mid = (z == 1) | (z == 2)
    end = (z == 0) | (z == 3)
    far = jnp.where(z < 2, 1, 0)
    zp = [z, z + 1 - 2 * (z % 2), 1 + far, 3 * far]
    dp_core = y * 2 + (1 - core)
    dp_y = (1 - y) * 2 + core
    dp_diag = (1 - y) * 2 + (1 - core)
    to_x = (dp, cx)
    to_outer = (dp, zp[1] * 2 + xx)
    to_inner = (dp, jnp.where(mid, 3 - z, zp[1]) * 2 + xx)
    to_core = (dp_core, c)
    to_y = (dp_y, c)
    dp_peers = [dp_core, dp_y, dp_diag]
    ctx_peers = [(c + o) % NC for o in range(1, NC)]
    pending = []
    counter = [0]

    def rows_of(i, n):
        return pl.ds(pl.multiple_of(i * n, n), n)

    def send(src, dst, ridx, dev, sidx=None):
        if sidx is None:
            sidx = counter[0]
            counter[0] += 1
        copy = pltpu.make_async_remote_copy(
            src_ref=src,
            dst_ref=dst,
            send_sem=ssem.at[sidx],
            recv_sem=rsem.at[ridx],
            device_id=dev,
            device_id_type=MESH_ID,
        )
        copy.start()
        return copy

    def new_send():
        counter[0] += 1
        return counter[0] - 1

    def got(dst, ridx):
        pltpu.make_async_remote_copy(
            src_ref=dst,
            dst_ref=dst,
            send_sem=ssem.at[0],
            recv_sem=rsem.at[ridx],
            device_id=to_x,
            device_id_type=MESH_ID,
        ).wait_recv()

    def sent(src, sidx):
        pltpu.make_async_remote_copy(
            src_ref=src,
            dst_ref=src,
            send_sem=ssem.at[sidx],
            recv_sem=rsem.at[0],
            device_id=to_x,
            device_id_type=MESH_ID,
        ).wait_send()

    def signal(sem, dev):
        pl.semaphore_signal(sem, inc=1, device_id=dev, device_id_type=MESH_ID)

    barrier = pltpu.get_barrier_semaphore()
    for p in dp_peers:
        signal(barrier, (p, c))
    for p in ctx_peers:
        signal(barrier, (dp, p))
    pl.semaphore_wait(barrier, len(dp_peers) + len(ctx_peers))

    def blk(buf, cc):
        return buf.at[rows_of(cc, BLK)]

    relays = []

    def send_if(cond, kind, buf, base, cc, dev):
        s = new_send()

        @pl.when(cond)
        def _():
            send(blk(buf, cc), blk(buf, cc), base + cc, dev, s)

        relays.append((kind, blk(buf, cc), s))

    def arrive(buf, base, k, who):
        cc = zp[k] * 2 + xx
        sz, sx = new_send(), new_send()
        part = blk(buf, cc).at[:, pl.ds(CUT, 2048 - CUT)] if k == 1 else blk(buf, cc)

        @pl.when(mid if who else end)
        def _():
            got(blk(buf, cc), base + cc)
            if who:
                send(blk(buf, cc), blk(buf, cc), base + cc, to_inner if k == 1 else to_outer, sz)
            send(part, part, base + cc, to_x, sx)

        relays.extend([(1, blk(buf, cc), sz)] if who else [])
        relays.append((int(who), part, sx))

    partner_here = set()

    def from_x(buf, base, k):
        cc = zp[k] * 2 + (1 - xx)
        if k == 0:
            if base not in partner_here:
                partner_here.add(base)
                got(blk(buf, cc), base + cc)
        elif k == 1:
            got(blk(buf, cc).at[:, pl.ds(CUT, 2048 - CUT)], base + cc)
            got(blk(buf, cc).at[:, pl.ds(0, CUT)], R_B[base])
        else:
            got(blk(buf, cc), base + cc)

    def partner_part(buf, base):
        from_x(buf, base, 0)
        part = blk(buf, cx).at[:, pl.ds(0, CUT)]
        pending.append(send(part, part, R_B[base], to_outer))

    gb[rows_of(c, BLK), :] = g_ref[...]
    pending.append(send(g_ref, blk(gb, c), R_G + c, to_x))
    pending.append(send(g_ref, blk(gb, c), R_G + c, to_outer))
    send_if(mid, 1, gb, R_G, c, to_inner)

    pair_cols = outp.at[pl.ds(0, 512)]
    for i in range(12):
        pltpu.make_async_copy(
            wq_ref.at[:, pl.ds(pl.multiple_of(i * 512 + z * 128, 128), 128)],
            pair_cols.at[:, pl.ds(i * 128, 128)],
            lsem.at[0],
        ).start()

    def row_of(ref):
        return ref[...].astype(F32).reshape(1, ref.shape[0])

    bq_all = row_of(bq_ref)
    bq_own = [own_lanes(bq_all[:, j * 512 : (j + 1) * 512], 64, c, NC) for j in range(3)]
    b1_own = own_lanes(row_of(b1_ref), 256, c, NC)
    wide = [row_of(r) for r in (gain_ref, shift_ref, bd_ref, b2_ref)]
    wide += [jnp.concatenate(bq_own + [jnp.zeros((1, 320), F32)], 1)]
    wide += [jnp.concatenate([b1_own, jnp.zeros((1, 256), F32)], 1)]
    vbuf[dp] = jnp.concatenate(wide + [jnp.zeros((10, 512), F32)], 0).astype(BF)
    mbuf[c] = jnp.concatenate([seg_ref[...], pos_ref[...], jnp.zeros((6, BLK), jnp.int32)], 0)
    for p in dp_peers:
        pending.append(send(vbuf.at[dp], vbuf.at[dp], R_V + dp, (p, c)))
    for p in ctx_peers:
        pending.append(send(mbuf.at[c], mbuf.at[c], R_M + c, (dp, p)))

    def pieces(t, slot):
        if t == 0:
            return [(wq.at[rows_of(slot, 512)], wq.at[rows_of(slot, 512)])]
        if t == 1:
            return [
                (
                    w1_ref.at[:, pl.ds(pl.multiple_of(q * 2048 + c * 256, 256), 256)],
                    w1.at[rows_of(slot, 512), pl.ds(q * 256, 256)],
                )
                for q in range(ND)
            ]
        if t == 2:
            return [
                (
                    w2_ref.at[rows_of(c, 256), pl.ds(half * 1024, 1024)],
                    w2.at[pl.ds(pl.multiple_of(half * 1024 + slot * 256, 256), 256)],
                )
                for half in range(2)
            ]
        return [(wd_ref.at[rows_of(c, 64)], wd.at[rows_of(slot, 64)])]

    def whole(t):
        return [wq.at[pl.ds(0, 512)], w1.at[pl.ds(0, 512)], w2.at[pl.ds(0, 512)], wd.at[pl.ds(0, 64)]][t]

    wsent = []

    def weight_send(t):
        sy, sc = new_send(), new_send()
        for src, dst in pieces(t, dp):
            send(src, dst, R_WY + t, to_y, sy)
        for src, dst in pieces(t, dp):
            send(src, dst, R_WC + t, to_core, sc)
        if t > 0:
            for src, dst in pieces(t, dp):
                pltpu.make_async_copy(src, dst, lsem.at[t]).start()
        wsent.extend([(t, sy), (t, sc)])

    def pick_heads():
        pltpu.make_async_copy(wq_ref.at[:, pl.ds(0, 1536)], pair_cols.at[:, pl.ds(0, 1536)], lsem.at[0]).wait()
        low_half = lax.broadcasted_iota(jnp.int32, (512, 128), 1) < 64
        for i in range(6):
            a = outp[0:512, i * 256 : i * 256 + 128].astype(F32)
            b = outp[0:512, i * 256 + 128 : i * 256 + 256].astype(F32)
            left = jnp.where(xx == 1, pltpu.roll(a, 64, 1), a)
            right = jnp.where(xx == 0, pltpu.roll(b, 64, 1), b)
            wq[rows_of(dp, 512), i * 128 : (i + 1) * 128] = jnp.where(low_half, left, right).astype(BF)

    pick_heads()
    for t in range(4):
        weight_send(t)

    def weight_forward(t):
        got(whole(t), R_WY + t)
        sf = new_send()
        for _, dst in pieces(t, dp_y):
            send(dst, dst, R_WF + t, to_core, sf)
        wsent.append((t, sf))

    def weight_ready(t):
        got(whole(t), R_WC + t)
        got(whole(t), R_WF + t)
        if t > 0:
            pltpu.make_async_copy(whole(t), whole(t), lsem.at[t]).wait()

    for p in dp_peers:
        got(vbuf.at[p], R_V + p)
    slots = [vbuf[s].astype(F32) for s in range(ND)]

    def vec_row(i):
        return jnp.concatenate([slots[s][i : i + 1] for s in range(ND)], 1)

    gain = vec_row(0)
    shift = vec_row(1)
    out_bias = vec_row(2) + vec_row(3)
    bias_q = jnp.concatenate([slots[i // 3][4:5, (i % 3) * 64 : (i % 3 + 1) * 64] for i in range(12)], 1)
    bias_1 = jnp.concatenate([slots[s][5:6, :256] for s in range(ND)], 1)

    def norm_parts():
        xv = x_ref[...].astype(F32)
        center = xv - jnp.mean(xv, axis=1, keepdims=True)
        inv = lax.rsqrt(jnp.mean(center * center, axis=1, keepdims=True) + EPS)
        return center * inv, inv

    xhat, _ = norm_parts()
    nb[rows_of(c, BLK), :] = (xhat * gain + shift).astype(BF)

    pending.append(send(blk(nb, c), blk(nb, c), R_N + c, to_x))
    pending.append(send(blk(nb, c), blk(nb, c), R_N + c, to_outer))
    send_if(mid, 1, nb, R_N, c, to_inner)

    for p in ctx_peers:
        got(mbuf.at[p], R_M + p)
    seg = jnp.concatenate([mbuf[i, 0:1, :] for i in range(NC)], 1)
    pos = jnp.concatenate([mbuf[i, 1:2, :] for i in range(NC)], 1).astype(F32)
    first_len = jnp.sum((seg == 0).astype(jnp.int32).astype(F32), axis=1, keepdims=True).astype(jnp.int32)
    last_start = jnp.sum((seg <= 1).astype(jnp.int32).astype(F32), axis=1, keepdims=True).astype(jnp.int32)
    qstart[...] = jnp.where(seg == 0, 0, jnp.where(seg == 1, first_len, last_start))
    lane = lax.broadcasted_iota(jnp.int32, (16, PAIR), 0)
    freqs = jnp.zeros((16, PAIR), F32)
    for i, value in enumerate(FREQS):
        freqs = jnp.where(lane == i, value, freqs)
    for i in range(4):
        angles = freqs * pos[:, i * PAIR : (i + 1) * PAIR]
        cos_h, sin_h = jnp.cos(angles), jnp.sin(angles)
        ones, zeros = jnp.ones((32, PAIR), F32), jnp.zeros((32, PAIR), F32)
        ctab[i * PAIR : (i + 1) * PAIR, :] = jnp.transpose(
            jnp.concatenate([cos_h, cos_h, ones, cos_h, cos_h, ones], 0)
        )
        stab[i * PAIR : (i + 1) * PAIR, :] = jnp.transpose(
            jnp.concatenate([-sin_h, sin_h, zeros, -sin_h, sin_h, zeros], 0)
        )

    def turn(v, rows, sign):
        cos_t, sin_t = ctab[rows, :], stab[rows, :]
        halves = []
        for i in range(v.shape[1] // 128):
            part = v[:, i * 128 : (i + 1) * 128]
            halves.append(part * cos_t + sign * (swap_turned(part) * sin_t))
        return jnp.concatenate(halves, 1) if len(halves) > 1 else halves[0]

    def project(pair):
        rows = rows_of(pair, PAIR)
        xv = nb[rows, :]
        for part in range(3):
            cols = slice(part * 256, (part + 1) * 256)
            val = dot_nn(xv, wq[:, cols]) + bias_q[:, cols]
            if part < 2:
                val = turn(val, rows, 1.0)
            low = val.astype(BF)
            dest = (qh, kh, vh)[part]
            for h in range(HEADS_C):
                dest[h, rows, :] = low[:, h * 64 : (h + 1) * 64]

    def project_ff(pair):
        rows = rows_of(pair, PAIR)
        xv = nb[rows, :]
        for f in range(4):
            cols = slice(f * 256, (f + 1) * 256)
            u = dot_nn(xv, w1[:, cols]) + bias_1[:, cols]
            uu = u * u
            th = jnp.tanh(GELU_K * (u + GELU_A * (uu * u)))
            half = 0.5 * (1.0 + th)
            act[rows, cols] = (u * half).astype(BF)
            slope = half + 0.5 * u * (1.0 - th * th) * (GELU_K * (1.0 + 3.0 * GELU_A * uu))
            ig[rows, cols] = slope.astype(BF)

    def masked(s, i, kv):
        ji = lax.broadcasted_iota(jnp.int32, (kv, PAIR), 0)
        qi = lax.broadcasted_iota(jnp.int32, (1, PAIR), 1) + i * PAIR
        ok = (ji <= qi) & (ji >= qstart[:, i * PAIR : (i + 1) * PAIR])
        return ok, jnp.where(ok, s * SCALE, MASKED)

    def head_rows(h):
        return pl.ds(pl.multiple_of(h * 64, 64), 64)

    def attend(h, carry):
        for i in range(4):
            kv = (i + 1) * PAIR
            cols = slice(i * PAIR, (i + 1) * PAIR)
            _, s = masked(dot_nt(kh[h, 0:kv, :], qh[h, cols, :]), i, kv)
            m = jnp.max(s, axis=0, keepdims=True)
            p = jnp.exp(s - m)
            total = jnp.sum(p, axis=0, keepdims=True)
            probs = (p * (1.0 / total)).astype(BF)
            o_t[head_rows(h), cols] = dot_tn(vh[h, 0:kv, :], probs)
            lse[h, :, cols] = m + jnp.log(total)
        return carry

    x_sent = [[None] * 4, [None] * 4]
    z_sent = [[None] * 4, [None] * 4]
    src_of = (outp, gb)

    def reduce_x(op, k):
        cc = zp[k] * 2 + (1 - xx)
        if op == 1:
            pl.semaphore_wait(xfree.at[k], 1)
        x_sent[op][k] = send(blk(src_of[op], cc), rx.at[k], R_X[op] + k, to_x)

    def z_send(op, k, slot, dev, s):
        if op == 1:
            pl.semaphore_wait(zfree.at[slot], 1)
        send(rx.at[k], rz.at[slot], R_Z[op] + slot, dev, s)

    def reduce_z(op, k, middle):
        if z_sent[op][k] is None:
            z_sent[op][k] = new_send()
        s = z_sent[op][k]

        if not middle:

            @pl.when(end)
            def _():
                got(rx.at[k], R_X[op] + k)
                own = src_of[op][rows_of(zp[k] * 2 + xx, BLK), :].astype(F32)
                rx[k] = (rx[k].astype(F32) + own).astype(BF)
                z_send(op, k, 3 - k, to_outer, s)

            return
        slot_in = {3: 0, 2: 1, 1: 3}[k]

        @pl.when(mid)
        def _():
            got(rx.at[k], R_X[op] + k)
            got(rz.at[slot_in], R_Z[op] + slot_in)
            own = src_of[op][rows_of(zp[k] * 2 + xx, BLK), :].astype(F32)
            rx[k] = (rx[k].astype(F32) + own + rz[slot_in].astype(F32)).astype(BF)
            if op == 0:
                signal(zfree.at[slot_in], to_inner if k == 1 else to_outer)
            z_send(op, k, 0 if k == 1 else 6 - k, to_outer if k == 1 else to_inner, s)

    def keep(total):
        for j in range(16):
            dkv[j // 8, (j % 8) * 128 : (j % 8 + 1) * 128, :] = total[:, j * 128 : (j + 1) * 128]

    def reduced(op, total):
        @pl.when(end)
        def _():
            got(rz.at[0], R_Z[op])
            keep(total + rz[0].astype(F32))
            if op == 0:
                signal(zfree.at[0], to_outer)

        @pl.when(mid)
        def _():
            got(rz.at[2], R_Z[op] + 2)
            got(rz.at[4], R_Z[op] + 4)
            keep(total + rz[2].astype(F32) + rz[4].astype(F32))
            if op == 0:
                signal(zfree.at[2], to_outer)
                signal(zfree.at[4], to_inner)

        return jnp.concatenate([dkv[j // 8, (j % 8) * 128 : (j % 8 + 1) * 128, :] for j in range(16)], 1)

    def partial_out(pair):
        rows = rows_of(pair, PAIR)
        mv, av = mixed[rows, :], act[rows, :]
        for n in range(8):
            cols = slice(n * 256, (n + 1) * 256)
            half, off = n // 4, (n % 4) * 256
            val = dot_nn(mv, wd[:, cols]) + dot_nn(av, w2[half * 1024 : (half + 1) * 1024, off : off + 256])
            outp[rows, cols] = val.astype(BF)

    svec[...] = jnp.zeros_like(svec)

    def backward_in(pair):
        rows = rows_of(pair, PAIR)
        ga, gc = gb[rows, 0:1024], gb[rows, 1024:2048]
        svec[0:1, :] += jnp.sum(gb[rows, :].astype(F32), axis=0, keepdims=True)
        for f in range(4):
            cols = slice(f * 256, (f + 1) * 256)
            val = dot_nt(ga, w2[f * 256 : (f + 1) * 256, :]) + dot_nt(gc, w2[1024 + f * 256 : 1024 + (f + 1) * 256, :])
            low = (val * ig[rows, cols].astype(F32)).astype(BF)
            ig[rows, cols] = low
            svec[1:2, cols] += jnp.sum(low.astype(F32), axis=0, keepdims=True)
        mg = (dot_nt(ga, wd[:, 0:1024]) + dot_nt(gc, wd[:, 1024:2048])).astype(BF)
        for h in range(HEADS_C):
            d_out[h, rows, :] = mg[:, h * 64 : (h + 1) * 64]
        prod = jnp.transpose(mg.astype(F32)) * o_t[:, rows]
        for h in range(HEADS_C):
            delta[h, :, rows] = jnp.sum(prod[h * 64 : (h + 1) * 64], axis=0, keepdims=True)

    def mix():
        for i in range(4):
            cols = slice(i * PAIR, (i + 1) * PAIR)
            mixed[cols, :] = jnp.transpose(o_t[:, cols]).astype(BF)

    arrive(nb, R_N, 1, False)
    weight_forward(0)
    arrive(nb, R_N, 1, True)
    arrive(nb, R_N, 2, True)
    arrive(nb, R_N, 3, True)
    arrive(nb, R_N, 2, False)
    arrive(gb, R_G, 1, True)
    arrive(gb, R_G, 2, True)
    from_x(nb, R_N, 0)
    weight_ready(0)
    weight_forward(1)
    partner_part(nb, R_N)
    weight_ready(1)
    arrive(gb, R_G, 3, True)
    project_ff(zp[0])
    arrive(nb, R_N, 3, False)
    project(zp[0])
    from_x(nb, R_N, 2)
    arrive(gb, R_G, 1, False)
    project(zp[2])
    from_x(nb, R_N, 3)
    partner_part(gb, R_G)
    from_x(nb, R_N, 1)
    arrive(gb, R_G, 2, False)
    project_ff(zp[2])
    weight_forward(2)
    from_x(gb, R_G, 0)
    project(zp[3])
    project(zp[1])
    project_ff(zp[3])
    weight_forward(3)
    lax.fori_loop(0, 2, attend, 0)
    arrive(gb, R_G, 3, False)
    weight_ready(2)
    weight_ready(3)
    lax.fori_loop(2, 4, attend, 0)
    mix()
    partial_out(zp[3])
    reduce_x(0, 3)
    project_ff(zp[1])
    from_x(gb, R_G, 1)
    partial_out(zp[2])
    reduce_x(0, 2)
    backward_in(zp[0])
    from_x(gb, R_G, 2)
    partial_out(zp[1])
    reduce_x(0, 1)
    partial_out(zp[0])
    reduce_x(0, 0)
    backward_in(zp[1])
    backward_in(zp[2])
    from_x(gb, R_G, 3)
    backward_in(zp[3])

    def sends_done():
        for t, s in wsent:
            sent(whole(t), s)
        for s in pending:
            s.wait_send()
        pending.clear()
        for kind, cond in ((1, mid), (0, end)):

            @pl.when(cond)
            def _():
                for kk, src, s in relays:
                    if kk == kind:
                        sent(src, s)

    def grad_ff_in():
        for f in range(8):
            for n in range(2):
                rows, cols = slice(f * 256, (f + 1) * 256), slice(n * 512, (n + 1) * 512)
                w1s[rows, cols] = dot_tn(nb[:, rows], ig[:, cols]).astype(BF)

    def grad_ff_out():
        for f in range(4):
            for n in range(4):
                cols = slice((n % 2) * 512, (n % 2 + 1) * 512)
                first = (n // 2) * 1024 + f * 256
                w2[first : first + 256, cols] = dot_tn(
                    act[:, f * 256 : (f + 1) * 256], gb[:, n * 512 : (n + 1) * 512]
                ).astype(BF)

    def grad_dense():
        for n in range(4):
            cols = slice(n * 512, (n + 1) * 512)
            wd[:, cols] = dot_tn(mixed[...], gb[:, cols]).astype(BF)

    def grad_joint():
        for f in range(8):
            rows = slice(f * 256, (f + 1) * 256)
            for n in range(3):
                cols = slice(n * 256, (n + 1) * 256)
                wq[rows, cols] = dot_tn(nb[:, rows], jg[:, cols]).astype(BF)

    def quarter(t, q):
        if t == 2:
            return [w2.at[pl.ds(pl.multiple_of(half * 1024 + q * 256, 256), 256)] for half in range(2)]
        if t == 3:
            return [wd.at[rows_of(q, 64)]]
        return [(wq, w1s)[t].at[rows_of(q, 512)]]

    def core_slot(t, yy):
        if t == 0:
            return [cq.at[yy]]
        if t == 1:
            return [cw.at[yy]]
        if t == 2:
            return [cw.at[yy, pl.ds(half * 256, 256)] for half in range(2)]
        return [cd.at[yy]]

    core_sent, y_sent = {}, {}

    def core_send(t):
        ids = []
        for yy in range(2):
            s = new_send()
            for src, dst in zip(quarter(t, yy * 2 + (1 - core)), core_slot(t, yy)):
                send(src, dst, R_C + t * 2 + yy, to_core, s)
            ids.append(s)
        core_sent[t] = ids

    def slot_whole(t, yy):
        return (cq, cw, cw, cd)[t].at[yy]

    def landing(t):
        return quarter(t, 1 - core)

    def y_send(t):
        for s in core_sent[t]:
            sent(slot_whole(t, 0), s)
        signal(yfree.at[t], to_y)
        for yy in range(2):
            got(slot_whole(t, yy), R_C + t * 2 + yy)
            for own, other in zip(quarter(t, yy * 2 + core), core_slot(t, yy)):
                own[...] = (own[...].astype(F32) + other[...].astype(F32)).astype(BF)
        if t == 1:
            signal(cfree.at[0], to_core)
        pl.semaphore_wait(yfree.at[t], 1)
        s = new_send()
        for src, dst in zip(quarter(t, (1 - y) * 2 + core), landing(t)):
            send(src, dst, R_Y + t, to_y, s)
        y_sent[t] = s

    def total(t):
        got(whole(t), R_Y + t)
        for own, other in zip(quarter(t, y * 2 + core), landing(t)):
            own[...] = (own[...].astype(F32) + other[...].astype(F32)).astype(BF)

    totalled = set()

    def exchange(t, buf, base, other):
        src = (wq, w1s)[t]
        first = (y * 2 + core) * 8
        if t not in totalled:
            totalled.add(t)
            total(t)
            buf[c] = src[rows_of(first + c, 64), :]
        if other:
            peers = [zp[k] * 2 + (1 - xx) for k in range(4)]
        else:
            peers = [zp[k] * 2 + xx for k in (1, 2, 3)]
        for p in peers:
            pending.append(send(src.at[rows_of(first + p, 64)], buf.at[c], base + c, (dp, p)))

    def partial_ff(pair):
        rows = rows_of(pair, PAIR)
        iv = ig[rows, :]
        for n in range(8):
            cols = slice(n * 256, (n + 1) * 256)
            gb[rows, cols] = dot_nt(iv, w1[cols, :]).astype(BF)

    def partial_attn(pair):
        rows = rows_of(pair, PAIR)
        jv = jg[rows, :]
        svec[1:2, 1024:1792] += jnp.sum(jv.astype(F32), axis=0, keepdims=True)
        for n in range(8):
            cols = slice(n * 256, (n + 1) * 256)
            gb[rows, cols] = (dot_nt(jv, wq[cols, :]) + gb[rows, cols].astype(F32)).astype(BF)

    def attend_back(hp, carry):
        for j in range(2):
            h = hp * 2 + j
            for i in (3, 2, 1, 0):
                kv = (i + 1) * PAIR
                cols = slice(i * PAIR, (i + 1) * PAIR)
                ok, s = masked(dot_nt(kh[h, 0:kv, :], qh[h, cols, :]), i, kv)
                p = jnp.where(ok, jnp.exp(s - lse[h, :, cols]), 0.0)
                dp_t = dot_nt(vh[h, 0:kv, :], d_out[h, cols, :])
                ds = (p * (dp_t - delta[h, :, cols])).astype(BF)
                dv = dot_nn(p.astype(BF), d_out[h, cols, :])
                dk = dot_nn(ds, qh[h, cols, :])
                both = jnp.concatenate([dk, dv], 1)
                if i == 3:
                    dkv[j, 0:kv, :] = both
                else:
                    dkv[j, 0:kv, :] += both
                o_t[head_rows(h), cols] = dot_tn(kh[h, 0:kv, :], ds)
        for i in range(4):
            rows = slice(i * PAIR, (i + 1) * PAIR)
            kk = jnp.concatenate([dkv[0, rows, 0:64], dkv[1, rows, 0:64]], 1) * SCALE
            vv = jnp.concatenate([dkv[0, rows, 64:128], dkv[1, rows, 64:128]], 1)
            jg[rows, pl.ds(pl.multiple_of(256 + hp * 128, 128), 128)] = turn(kk, rows, -1.0).astype(BF)
            jg[rows, pl.ds(pl.multiple_of(512 + hp * 128, 128), 128)] = vv.astype(BF)
        return carry

    def next_x(k):
        sent(rx.at[k], z_sent[0][k])
        signal(xfree.at[k], to_x)
        reduce_x(1, k)

    outs = []

    def out_copy(src, dst):
        copy = pltpu.make_async_copy(src, dst, lsem.at[4 + len(outs)])
        copy.start()
        outs.append(copy)

    def finish_out_weights():
        total(2)
        for half in range(2):
            out_copy(quarter(2, y * 2 + core)[half], w2s_ref.at[:, pl.ds(half * 1024, 1024)])
        total(3)
        out_copy(quarter(3, y * 2 + core)[0], wds_ref)

    grad_ff_in()
    core_send(1)
    reduce_z(0, 3, False)
    y_send(1)
    sends_done()
    grad_ff_out()
    grad_dense()
    reduce_z(0, 2, False)
    lax.fori_loop(0, 1, attend_back, 0)
    reduce_z(0, 3, True)
    pl.semaphore_wait(cfree.at[0], 1)
    core_send(2)
    core_send(3)
    lax.fori_loop(1, 2, attend_back, 0)
    for i in range(4):
        rows = slice(i * PAIR, (i + 1) * PAIR)
        jg[rows, 0:256] = turn(jnp.transpose(o_t[:, rows]) * SCALE, rows, -1.0).astype(BF)

    reduce_z(0, 1, False)
    for k in range(4):
        partial_ff(zp[k])
    for k in range(4):
        partial_attn(zp[k])
    reduce_z(0, 2, True)
    reduce_z(0, 1, True)
    exchange(1, a1, R_A1, False)
    next_x(3)
    grad_joint()
    core_send(0)
    next_x(2)
    next_x(1)
    got(rx.at[0], R_X[0])
    x_sent[0][0].wait_send()
    outp[rows_of(cx, BLK), :] = rx[0]
    signal(xfree.at[0], to_x)
    reduce_x(1, 0)
    y_send(0)
    exchange(1, a1, R_A1, True)
    total_o = outp[rows_of(cx, BLK), :].astype(F32) + outp[rows_of(c, BLK), :].astype(F32)
    out_ref[...] = (x_ref[...].astype(F32) + out_bias + reduced(0, total_o)).astype(BF)

    y_send(2)
    y_send(3)
    reduce_z(1, 3, False)
    reduce_z(1, 2, False)
    reduce_z(1, 1, False)
    exchange(0, aq, R_AQ, True)
    reduce_z(1, 3, True)
    reduce_z(1, 2, True)
    reduce_z(1, 1, True)
    exchange(0, aq, R_AQ, False)

    got(rx.at[0], R_X[1])
    ng = reduced(1, rx[0].astype(F32) + gb[rows_of(c, BLK), :].astype(F32))
    xhat, inv = norm_parts()
    e = ng * gain
    m1 = jnp.mean(e, axis=1, keepdims=True)
    m2 = jnp.mean(e * xhat, axis=1, keepdims=True)
    xgrad_ref[...] = (g_ref[...].astype(F32) + (e - m1 - xhat * m2) * inv).astype(BF)
    pkc[c, 0:16, :] = as_rows(jnp.sum(ng * xhat, axis=0, keepdims=True))
    pkc[c, 16:32, :] = as_rows(jnp.sum(ng, axis=0, keepdims=True))
    pkc[c, 32:40, :] = as_rows(svec[1:2, 1024:2048])
    for p in ctx_peers:
        pending.append(send(pkc.at[c], pkc.at[c], R_PC + c, (dp, p)))
    finish_out_weights()

    for p in ctx_peers:
        got(pkc.at[p], R_PC + p)
    norm_sum = pkc[0, 0:32, :]
    for i in range(1, NC):
        norm_sum = norm_sum + pkc[i, 0:32, :]
    pkd[dp, 0:32, :] = norm_sum
    for i in range(NC):
        pkd[dp, 32 + i * 8 : 40 + i * 8, :] = pkc[i, 32:40, :]
    pkd[dp, 96:112, :] = as_rows(svec[0:1, :])
    pkd[dp, 112:120, :] = as_rows(svec[1:2, 0:1024])
    for p in dp_peers:
        pending.append(send(pkd.at[dp], pkd.at[dp], R_PD + dp, (p, c)))

    for p in ctx_peers:
        got(a1.at[p], R_A1 + p)
    out_copy(a1, a1_ref)
    for p in dp_peers:
        got(pkd.at[p], R_PD + p)
    small_ref[...] = pkd[0] + pkd[1] + pkd[2] + pkd[3]
    for p in ctx_peers:
        got(aq.at[p], R_AQ + p)
    out_copy(aq, aq_ref)

    for s in pending:
        s.wait_send()
    for k in (3, 2, 1):
        x_sent[0][k].wait_send()
    for k in range(4):
        x_sent[1][k].wait_send()
    for k in (3, 2, 1):
        sent(rx.at[k], z_sent[1][k])
    for t in range(4):
        sent(whole(t), y_sent[t])
    for copy in outs:
        copy.wait()


def finish_kernel(
    out_in,
    xgrad_in,
    small,
    w2s_in,
    wds_in,
    a1_in,
    aq_in,
    out_ref,
    xgrad_ref,
    gain_ref,
    shift_ref,
    wqg_ref,
    bqg_ref,
    wdg_ref,
    bd_ref,
    w1g_ref,
    b1_ref,
    w2g_ref,
    b2_ref,
    w2s,
    wds,
    a1,
    aq,
    w2w,
    wdw,
    w1w,
    wqw,
    rows_o,
    rows_x,
    sems,
):
    dp = lax.axis_index("dp")
    c = lax.axis_index("ctx")
    me = dp * NC + c
    used = []

    def move(src, dst):
        copy = pltpu.make_async_copy(src, dst, sems.at[len(used)])
        copy.start()
        used.append(copy)
        return copy

    pairs = ((w2s_in, w2s), (a1_in, a1), (aq_in, aq), (wds_in, wds), (out_in, rows_o), (xgrad_in, rows_x))
    loads = [move(*p) for p in pairs]
    stores = []
    loads[0].wait()
    w2w[...] = w2s[...].astype(F32)
    stores.append(move(w2w, w2g_ref))
    loads[1].wait()
    for q in range(ND):
        for i in range(NC):
            w1w[:, q * 2048 + i * 256 : q * 2048 + (i + 1) * 256] = a1[i, :, q * 256 : (q + 1) * 256].astype(F32)
    stores.append(move(w1w, w1g_ref))
    loads[2].wait()
    for o in range(12):
        for i in range(NC // 2):
            both = [aq[2 * i + j, :, o * 64 : (o + 1) * 64].astype(F32) for j in range(2)]
            wqw[:, o * 512 + i * 128 : o * 512 + (i + 1) * 128] = jnp.concatenate(both, 1)
    stores.append(move(wqw, wqg_ref))
    loads[3].wait()
    wdw[...] = wds[...].astype(F32)
    stores.append(move(wdw, wdg_ref))
    loads[4].wait()
    stores.append(move(rows_o, out_ref))
    loads[5].wait()
    stores.append(move(rows_x, xgrad_ref))

    def own_64(first):
        row = small[pl.ds(first + me // 2, 1), :]
        return jnp.where(me % 2 == 0, row[:, 0:64], row[:, 64:128]).reshape(64)

    gain_ref[...] = own_64(0)
    shift_ref[...] = own_64(16)
    summed = own_64(96)
    bd_ref[...] = summed
    b2_ref[...] = summed
    rows = small[pl.ds(112 + dp * 2, 2), :]
    b1_ref[...] = jnp.concatenate([rows[0:1], rows[1:2]], 1).reshape(256)

    picked = []
    for j in range(3):
        head = me * 3 + j
        o, i = head // NC, head % NC
        row = small[pl.ds(32 + i * 8 + o // 2, 1), :]
        picked.append(jnp.where(o % 2 == 0, row[:, 0:64], row[:, 64:128]))
    bqg_ref[...] = jnp.concatenate(picked, 1).reshape(192)
    for copy in stores:
        copy.wait()


def fast_device(inputs, positions, seq_ids, ln_gain, ln_bias, w_qkv, b_qkv, w_dense, b_dense, w_fc1, b_fc1, w_fc2, b_fc2, cotangent):
    width = inputs.shape[2]
    vm = pl.BlockSpec(memory_space=pltpu.VMEM)
    hbm = pl.BlockSpec(memory_space=pl.ANY)
    dma = pltpu.SemaphoreType.DMA
    reg = pltpu.SemaphoreType.REGULAR
    sd = jax.ShapeDtypeStruct
    parts = pl.pallas_call(
        layer_kernel,
        out_shape=(
            sd((BLK, width), BF),
            sd((BLK, width), BF),
            sd((120, 128), F32),
            sd((256, 2048), BF),
            sd((64, 2048), BF),
            sd((NC, 64, 1024), BF),
            sd((NC, 64, 768), BF),
        ),
        in_specs=[vm] * 10 + [hbm] * 4,
        out_specs=(vm, vm, vm, hbm, hbm, hbm, hbm),
        scratch_shapes=[
            pltpu.VMEM((TOK, 2048), BF),
            pltpu.VMEM((TOK, 2048), BF),
            pltpu.VMEM((2048, 768), BF),
            pltpu.VMEM((2048, 1024), BF),
            pltpu.VMEM((2048, 1024), BF),
            pltpu.VMEM((256, 2048), BF),
            pltpu.VMEM((ND, 16, 512), BF),
            pltpu.VMEM((NC, 8, BLK), jnp.int32),
            pltpu.VMEM((TOK, 128), F32),
            pltpu.VMEM((TOK, 128), F32),
            pltpu.VMEM((1, TOK), jnp.int32),
            pltpu.VMEM((4, TOK, 64), BF),
            pltpu.VMEM((4, TOK, 64), BF),
            pltpu.VMEM((4, TOK, 64), BF),
            pltpu.VMEM((256, TOK), F32),
            pltpu.VMEM((4, 1, TOK), F32),
            pltpu.VMEM((4, 1, TOK), F32),
            pltpu.VMEM((TOK, 256), BF),
            pltpu.VMEM((TOK, 1024), BF),
            pltpu.VMEM((TOK, 1024), BF),
            pltpu.VMEM((4, TOK, 64), BF),
            pltpu.VMEM((TOK, 768), BF),
            pltpu.VMEM((2, TOK, 128), F32),
            pltpu.VMEM((8, 2048), F32),
            pltpu.VMEM((TOK, 2048), BF),
            pltpu.VMEM((4, BLK, 2048), BF),
            pltpu.VMEM((5, BLK, 2048), BF),
            pltpu.VMEM((2, 512, 1024), BF),
            pltpu.VMEM((2, 512, 768), BF),
            pltpu.VMEM((2, 64, 2048), BF),
            pltpu.VMEM((NC, 64, 1024), BF),
            pltpu.VMEM((NC, 64, 768), BF),
            pltpu.VMEM((NC, 40, 128), F32),
            pltpu.VMEM((ND, 120, 128), F32),
            pltpu.VMEM((2048, 1024), BF),
            dma((N_SEND,)),
            dma((N_RECV,)),
            dma((9,)),
            reg((4,)),
            reg((5,)),
            reg((1,)),
            reg((4,)),
        ],
        compiler_params=pltpu.CompilerParams(
            collective_id=0, has_side_effects=True, vmem_limit_bytes=63 * 1024 * 1024
        ),
        name="layer",
    )(
        inputs[0], cotangent[0], seq_ids, positions, ln_gain, ln_bias, b_dense, b_fc2, b_qkv, b_fc1, w_qkv, w_fc1, w_fc2, w_dense
    )
    done = pl.pallas_call(
        finish_kernel,
        out_shape=(
            sd((BLK, width), BF),
            sd((BLK, width), BF),
            sd((64,), F32),
            sd((64,), F32),
            sd((64, 6144), F32),
            sd((192,), F32),
            sd((64, 2048), F32),
            sd((64,), F32),
            sd((64, 8192), F32),
            sd((256,), F32),
            sd((256, 2048), F32),
            sd((64,), F32),
        ),
        in_specs=[hbm, hbm, vm, hbm, hbm, hbm, hbm],
        out_specs=(hbm, hbm, vm, vm, hbm, vm, hbm, vm, hbm, vm, hbm, vm),
        scratch_shapes=[
            pltpu.VMEM((256, 2048), BF),
            pltpu.VMEM((64, 2048), BF),
            pltpu.VMEM((NC, 64, 1024), BF),
            pltpu.VMEM((NC, 64, 768), BF),
            pltpu.VMEM((256, 2048), F32),
            pltpu.VMEM((64, 2048), F32),
            pltpu.VMEM((64, 8192), F32),
            pltpu.VMEM((64, 6144), F32),
            pltpu.VMEM((BLK, 2048), BF),
            pltpu.VMEM((BLK, 2048), BF),
            dma((12,)),
        ],
        compiler_params=pltpu.CompilerParams(vmem_limit_bytes=62 * 1024 * 1024),
        name="finish",
    )(*parts)
    return (done[0][None], done[1][None]) + tuple(done[2:])


def solution(mesh):
    placed = (
        P("dp", "ctx", None),
        P("dp", "ctx"),
        P("dp", "ctx"),
        P("dp"),
        P("dp"),
        P("dp", None),
        P("dp"),
        P("dp", None),
        P("dp"),
        P("dp", None),
        P("dp"),
        P("dp", None),
        P("dp"),
        P("dp", "ctx", None),
    )
    fits = mesh.shape["dp"] == ND and mesh.shape["ctx"] == NC
    return jax.shard_map(
        fast_device if fits else per_device,
        mesh=mesh,
        in_specs=placed,
        out_specs=(
            P("dp", "ctx", None),
            P("dp", "ctx", None),
            P(("dp", "ctx")),
            P(("dp", "ctx")),
            P(("dp", "ctx"), None),
            P(("dp", "ctx")),
            P(("dp", "ctx"), None),
            P(("dp", "ctx")),
            P(("dp", "ctx"), None),
            P(("dp", "ctx")),
            P(("dp", "ctx"), None),
            P(("dp", "ctx")),
        ),
        check_vma=False,
    )
```

```python
import math

import jax
import jax.numpy as jnp
import numpy as np
from jax import lax
from jax.experimental import pallas as pl
from jax.experimental.pallas import tpu as pltpu
from jax.sharding import PartitionSpec as P

HEAD_DIM = 64
ROT = 32


EPS = 1e-05
MASKED = -1e30
SCALE = 0.125
BASE = 10000.0


def layer_norm(values, gain_vec, shift_vec):
    center = values - jnp.mean(values, axis=1, keepdims=True)
    spread = jnp.mean(center * center, axis=1, keepdims=True)
    return center * lax.rsqrt(spread + EPS) * gain_vec + shift_vec


def gelu_tanh(values):
    return jax.nn.gelu(values, approximate=True)


def rotate(values, angle_pos):
    row_count = values.shape[0]
    head_count = values.shape[1] // HEAD_DIM
    half_rot = ROT // 2
    split_heads = values.reshape(row_count, head_count, HEAD_DIM)
    freqs = BASE ** (-(jnp.arange(half_rot, dtype=jnp.float32) * 2.0) / ROT)
    angles = angle_pos[:, None] * freqs[None, :]
    cosine = jnp.cos(angles)[:, None, :]
    sine = jnp.sin(angles)[:, None, :]
    first_half = split_heads[:, :, :half_rot]
    second_half = split_heads[:, :, half_rot:ROT]
    turned = jnp.concatenate(
        [
            first_half * cosine - second_half * sine,
            second_half * cosine + first_half * sine,
            split_heads[:, :, ROT:],
        ],
        axis=2,
    )
    return turned.reshape(row_count, head_count * HEAD_DIM)


def visible(query_index, query_seg, key_index, key_seg):
    causal = key_index[None, :] <= query_index[:, None]
    return causal[None] & (key_seg[:, None, :] == query_seg[:, :, None])


def split_cols(values, low_col, high_col):
    return values[:, :, low_col:high_col].reshape(
        values.shape[0], values.shape[1], (high_col - low_col) // HEAD_DIM, HEAD_DIM
    )


def head_scores(query_heads, key_heads, allowed):
    raw = (
        jnp.einsum("sqhd,skhd->shqk", query_heads, key_heads, preferred_element_type=jnp.float32)
        * SCALE
    )
    return jnp.where(allowed[:, None], raw, MASKED)


def unchanged(state):
    return state


def per_device(
    inputs,
    positions,
    seq_ids,
    ln_gain,
    ln_bias,
    w_qkv,
    b_qkv,
    w_dense,
    b_dense,
    w_fc1,
    b_fc1,
    w_fc2,
    b_fc2,
    cotangent,
):
    (
        gain_all,
        shift_all,
        qkv_all,
        qkv_offset,
        dense_all,
        dense_offset,
        fc1_all,
        fc1_offset,
        fc2_all,
        fc2_offset,
    ) = (
        lax.all_gather(ln_gain, "dp", axis=0, tiled=True),
        lax.all_gather(ln_bias, "dp", axis=0, tiled=True),
        lax.all_gather(w_qkv, "dp", axis=0, tiled=True),
        lax.all_gather(b_qkv, "dp", axis=0, tiled=True),
        lax.all_gather(w_dense, "dp", axis=0, tiled=True),
        lax.all_gather(b_dense, "dp", axis=0, tiled=True),
        lax.all_gather(w_fc1, "dp", axis=0, tiled=True),
        lax.all_gather(b_fc1, "dp", axis=0, tiled=True),
        lax.all_gather(w_fc2, "dp", axis=0, tiled=True),
        lax.all_gather(b_fc2, "dp", axis=0, tiled=True),
    )
    stream_count = inputs.shape[0]
    row_count = inputs.shape[1]
    width = inputs.shape[2]
    flat_rows = stream_count * row_count
    resid = inputs.reshape(flat_rows, width).astype(jnp.float32)
    head_count = width // HEAD_DIM
    group_heads = math.gcd(head_count, 8)
    group_cols = group_heads * HEAD_DIM
    group_count = head_count // group_heads
    angle_pos = positions.reshape(flat_rows).astype(jnp.float32)
    own_seg = seq_ids.astype(jnp.bfloat16)
    row_start = lax.axis_index("ctx") * row_count
    own_index = row_start + jnp.arange(row_count, dtype=jnp.int32)
    normed, norm_back = jax.vjp(
        layer_norm, resid, gain_all.astype(jnp.float32), shift_all.astype(jnp.float32)
    )
    hidden = normed.astype(jnp.bfloat16)
    joint = jnp.dot(hidden, qkv_all, preferred_element_type=jnp.float32) + qkv_offset.astype(
        jnp.float32
    )
    queries = (
        rotate(joint[:, :width], angle_pos)
        .astype(jnp.bfloat16)
        .reshape(stream_count, row_count, width)
    )
    keys_own = (
        rotate(joint[:, width : 2 * width], angle_pos)
        .astype(jnp.bfloat16)
        .reshape(stream_count, row_count, width)
    )
    values_own = joint[:, 2 * width :].astype(jnp.bfloat16).reshape(stream_count, row_count, width)
    start_state = (
        jnp.full((stream_count, head_count, row_count), MASKED, jnp.float32),
        jnp.zeros((stream_count, head_count, row_count), jnp.float32),
        jnp.zeros((stream_count, row_count, width), jnp.float32),
    )
    key_part = lax.all_gather(keys_own, "ctx", axis=1, tiled=True)
    value_part = lax.all_gather(values_own, "ctx", axis=1, tiled=True)
    seg_part = lax.all_gather(own_seg, "ctx", axis=1, tiled=True)
    key_count = key_part.shape[1]
    allowed = visible(own_index, own_seg, jnp.arange(key_count, dtype=jnp.int32), seg_part)

    def forward_compute(state):
        peak_in, total_in, accum_in = state
        peak_list, total_list, accum_list = ([], [], [])
        for group_index in range(group_count):
            low_col = group_index * group_cols
            high_col = low_col + group_cols
            low_head = group_index * group_heads
            high_head = low_head + group_heads
            scores = head_scores(
                split_cols(queries, low_col, high_col),
                split_cols(key_part, low_col, high_col),
                allowed,
            )
            old_peak = peak_in[:, low_head:high_head]
            new_peak = jnp.maximum(old_peak, jnp.max(scores, axis=3))
            weights = jnp.where(allowed[:, None], jnp.exp(scores - new_peak[:, :, :, None]), 0.0)
            total_list.append(jnp.sum(weights, axis=3))
            gathered_vals = jnp.einsum(
                "shqk,skhd->sqhd",
                weights.astype(jnp.bfloat16),
                split_cols(value_part, low_col, high_col),
                preferred_element_type=jnp.float32,
            )
            accum_list.append(gathered_vals.reshape(stream_count, row_count, group_cols))
            peak_list.append(new_peak)
        return (
            jnp.concatenate(peak_list, 1),
            jnp.concatenate(total_list, 1),
            jnp.concatenate(accum_list, 2),
        )

    result_state = lax.cond(
        jnp.int32(0) < row_start + row_count, forward_compute, unchanged, start_state
    )
    peak, total, accum = result_state
    attended = (
        accum.reshape(stream_count, row_count, head_count, HEAD_DIM)
        / jnp.transpose(total, (0, 2, 1))[:, :, :, None]
    ).reshape(stream_count, row_count, width)
    log_total = jnp.transpose(peak + jnp.log(total), (0, 2, 1))
    mixed = attended.astype(jnp.bfloat16).reshape(flat_rows, width)
    inner = jnp.dot(hidden, fc1_all, preferred_element_type=jnp.float32) + fc1_offset.astype(
        jnp.float32
    )
    active, gelu_back = jax.vjp(gelu_tanh, inner)
    active_low = active.astype(jnp.bfloat16)
    summed = (
        resid
        + jnp.dot(mixed, dense_all, preferred_element_type=jnp.float32)
        + dense_offset.astype(jnp.float32)
    )
    summed = (
        summed
        + jnp.dot(active_low, fc2_all, preferred_element_type=jnp.float32)
        + fc2_offset.astype(jnp.float32)
    )
    outputs = summed.astype(jnp.bfloat16).reshape(stream_count, row_count, width)
    upstream = cotangent.reshape(flat_rows, width)
    upstream_f = upstream.astype(jnp.float32)
    bias_term = jnp.sum(upstream_f, axis=0)
    fc2_term = jnp.einsum("tf,td->fd", active_low, upstream, preferred_element_type=jnp.float32)
    fc2_sum = lax.psum_scatter(fc2_term, ("dp", "ctx"), scatter_dimension=0, tiled=True)
    fc2_sum, upstream = lax.optimization_barrier((fc2_sum, upstream))
    act_grad = jnp.einsum("td,fd->tf", upstream, fc2_all, preferred_element_type=jnp.float32)
    inner_grad = gelu_back(act_grad)[0].astype(jnp.bfloat16)
    fc1_term = jnp.einsum("td,tf->df", hidden, inner_grad, preferred_element_type=jnp.float32)
    fc1_bias_term = jnp.sum(inner_grad.astype(jnp.float32), axis=0)
    fc1_sum = lax.psum_scatter(fc1_term, ("dp", "ctx"), scatter_dimension=0, tiled=True)
    fc1_sum, mixed, upstream, upstream_f, fc1_bias_term, inner_grad, hidden = lax.optimization_barrier(
        (fc1_sum, mixed, upstream, upstream_f, fc1_bias_term, inner_grad, hidden)
    )
    fc1_bias_sum, bias_sum = (
        lax.psum_scatter(fc1_bias_term, ("dp", "ctx"), scatter_dimension=0, tiled=True),
        lax.psum_scatter(bias_term, ("dp", "ctx"), scatter_dimension=0, tiled=True),
    )
    dense_term = jnp.einsum("td,te->de", mixed, upstream, preferred_element_type=jnp.float32)
    dense_sum = lax.psum_scatter(dense_term, ("dp", "ctx"), scatter_dimension=0, tiled=True)
    dense_sum, upstream, dense_all = lax.optimization_barrier((dense_sum, upstream, dense_all))
    mixed_grad = (
        jnp.einsum("te,de->td", upstream, dense_all, preferred_element_type=jnp.float32)
        .astype(jnp.bfloat16)
        .reshape(stream_count, row_count, width)
    )
    delta = jnp.sum(
        (mixed_grad.astype(jnp.float32) * attended).reshape(
            stream_count, row_count, head_count, HEAD_DIM
        ),
        axis=3,
    )
    zero_block = jnp.zeros((stream_count, row_count, width), jnp.float32)
    query_key_part = lax.all_gather(keys_own, "ctx", axis=1, tiled=True)
    query_value_part = lax.all_gather(values_own, "ctx", axis=1, tiled=True)
    seg_part = lax.all_gather(own_seg, "ctx", axis=1, tiled=True)
    key_count = query_key_part.shape[1]
    query_allowed = visible(own_index, own_seg, jnp.arange(key_count, dtype=jnp.int32), seg_part)

    def query_compute(grad_in):
        step_list = []
        for group_index in range(group_count):
            low_col = group_index * group_cols
            high_col = low_col + group_cols
            low_head = group_index * group_heads
            high_head = low_head + group_heads
            scores = head_scores(
                split_cols(queries, low_col, high_col),
                split_cols(query_key_part, low_col, high_col),
                query_allowed,
            )
            lse_here = jnp.transpose(log_total[:, :, low_head:high_head], (0, 2, 1))[:, :, :, None]
            delta_here = jnp.transpose(delta[:, :, low_head:high_head], (0, 2, 1))[:, :, :, None]
            probs = jnp.where(query_allowed[:, None], jnp.exp(scores - lse_here), 0.0)
            prob_grad = jnp.einsum(
                "sqhd,skhd->shqk",
                split_cols(mixed_grad, low_col, high_col),
                split_cols(query_value_part, low_col, high_col),
                preferred_element_type=jnp.float32,
            )
            score_grad = (probs * (prob_grad - delta_here)).astype(jnp.bfloat16)
            query_step = (
                jnp.einsum(
                    "shqk,skhd->sqhd",
                    score_grad,
                    split_cols(query_key_part, low_col, high_col),
                    preferred_element_type=jnp.float32,
                )
                * SCALE
            )
            step_list.append(query_step.reshape(stream_count, row_count, group_cols))
        return grad_in + jnp.concatenate(step_list, 2)

    result_grad = lax.cond(
        jnp.int32(0) < row_start + row_count, query_compute, unchanged, zero_block
    )
    log_total_all, delta_all = (
        lax.all_gather(log_total, "ctx", axis=1, tiled=True),
        lax.all_gather(delta, "ctx", axis=1, tiled=True),
    )
    start = jnp.int32(0)
    query_part = lax.all_gather(queries, "ctx", axis=1, tiled=True)
    grad_part = lax.all_gather(mixed_grad, "ctx", axis=1, tiled=True)
    seg_part = lax.all_gather(own_seg, "ctx", axis=1, tiled=True)
    query_count = query_part.shape[1]
    query_index = jnp.arange(query_count, dtype=jnp.int32)
    key_allowed = visible(query_index, seg_part, own_index, own_seg)
    lse_part = lax.dynamic_slice_in_dim(log_total_all, start, query_count, 1)

    def key_compute(state):
        key_in, value_in = state
        key_list, value_list = ([], [])
        for group_index in range(group_count):
            low_col = group_index * group_cols
            high_col = low_col + group_cols
            low_head = group_index * group_heads
            high_head = low_head + group_heads
            scores = head_scores(
                split_cols(query_part, low_col, high_col),
                split_cols(keys_own, low_col, high_col),
                key_allowed,
            )
            lse_here = jnp.transpose(lse_part[:, :, low_head:high_head], (0, 2, 1))[:, :, :, None]
            delta_here = jnp.transpose(delta_all[:, :, low_head:high_head], (0, 2, 1))[
                :, :, :, None
            ]
            probs = jnp.where(key_allowed[:, None], jnp.exp(scores - lse_here), 0.0)
            grad_heads = split_cols(grad_part, low_col, high_col)
            value_step = jnp.einsum(
                "shqk,sqhd->skhd",
                probs.astype(jnp.bfloat16),
                grad_heads,
                preferred_element_type=jnp.float32,
            )
            prob_grad = jnp.einsum(
                "sqhd,skhd->shqk",
                grad_heads,
                split_cols(values_own, low_col, high_col),
                preferred_element_type=jnp.float32,
            )
            score_grad = (probs * (prob_grad - delta_here)).astype(jnp.bfloat16)
            key_step = (
                jnp.einsum(
                    "shqk,sqhd->skhd",
                    score_grad,
                    split_cols(query_part, low_col, high_col),
                    preferred_element_type=jnp.float32,
                )
                * SCALE
            )
            key_list.append(key_step.reshape(stream_count, row_count, group_cols))
            value_list.append(value_step.reshape(stream_count, row_count, group_cols))
        return (key_in + jnp.concatenate(key_list, 2), value_in + jnp.concatenate(value_list, 2))

    result_pair = lax.cond(
        start + query_count > row_start, key_compute, unchanged, (zero_block, zero_block)
    )
    key_grad, value_grad = result_pair
    joint_grad = jnp.concatenate(
        [
            rotate(result_grad.reshape(flat_rows, width), -angle_pos),
            rotate(key_grad.reshape(flat_rows, width), -angle_pos),
            value_grad.reshape(flat_rows, width),
        ],
        axis=1,
    ).astype(jnp.bfloat16)
    qkv_term = jnp.einsum("td,te->de", hidden, joint_grad, preferred_element_type=jnp.float32)
    qkv_bias_term = jnp.sum(joint_grad.astype(jnp.float32), axis=0)
    hidden_grad = jnp.einsum("te,de->td", joint_grad, qkv_all, preferred_element_type=jnp.float32)
    hidden_grad = hidden_grad + jnp.einsum(
        "tf,df->td", inner_grad, fc1_all, preferred_element_type=jnp.float32
    )
    resid_grad, gain_term, shift_term = norm_back(hidden_grad)
    input_grad = (
        (upstream_f + resid_grad).astype(jnp.bfloat16).reshape(stream_count, row_count, width)
    )
    gain_sum, shift_sum, qkv_sum, qkv_bias_sum = (
        lax.psum_scatter(gain_term, ("dp", "ctx"), scatter_dimension=0, tiled=True),
        lax.psum_scatter(shift_term, ("dp", "ctx"), scatter_dimension=0, tiled=True),
        lax.psum_scatter(qkv_term, ("dp", "ctx"), scatter_dimension=0, tiled=True),
        lax.psum_scatter(qkv_bias_term, ("dp", "ctx"), scatter_dimension=0, tiled=True),
    )
    return (
        outputs,
        input_grad,
        gain_sum,
        shift_sum,
        qkv_sum,
        qkv_bias_sum,
        dense_sum,
        bias_sum,
        fc1_sum,
        fc1_bias_sum,
        fc2_sum,
        bias_sum,
    )


BF = jnp.bfloat16
F32 = jnp.float32
BLK = 128
PAIR = 256
NC = 8
ND = 4
TOK = NC * BLK
HEADS_C = 4
MESH_ID = pl.DeviceIdType.MESH
GELU_A = 0.044715
GELU_K = math.sqrt(2.0 / math.pi)

R_N, R_G, R_M, R_V = 0, 16, 32, 40
R_WY, R_WC, R_WF = 44, 48, 52
R_X = (56, 64)
R_Z = (72, 82)
R_C, R_Y = 92, 100
R_A1, R_AQ, R_PC, R_PD = 104, 112, 120, 128
R_B = {R_N: 132, R_G: 133}
N_RECV = 134
N_SEND = 200
HALF = 1024
FREQS = [float(np.float32(BASE) ** np.float32(-2.0 * i / ROT)) for i in range(ROT // 2)]


def dot_nn(a, b):
    return lax.dot_general(a, b, (((1,), (0,)), ((), ())), preferred_element_type=F32)


def dot_nt(a, b):
    return lax.dot_general(a, b, (((1,), (1,)), ((), ())), preferred_element_type=F32)


def dot_tn(a, b):
    return lax.dot_general(a, b, (((0,), (0,)), ((), ())), preferred_element_type=F32)


def swap_turned(v):
    lane = lax.broadcasted_iota(jnp.int32, v.shape, 1) % HEAD_DIM
    return jnp.where(lane < 16, pltpu.roll(v, 112, 1), pltpu.roll(v, 16, 1))


def as_rows(v):
    return jnp.concatenate([v[:, i * 128 : (i + 1) * 128] for i in range(v.shape[1] // 128)], 0)


def as_row(v):
    return jnp.concatenate([v[i : i + 1] for i in range(v.shape[0])], 1)


def own_lanes(row, width, index, count):
    total = jnp.zeros((1, width), F32)
    for i in range(count):
        total = total + jnp.where(index == i, row[:, i * width : (i + 1) * width], 0.0)
    return total


def layer_kernel(
    x_ref,
    g_ref,
    seg_ref,
    pos_ref,
    gain_ref,
    shift_ref,
    bd_ref,
    b2_ref,
    bq_ref,
    b1_ref,
    wq_ref,
    w1_ref,
    w2_ref,
    wd_ref,
    out_ref,
    xgrad_ref,
    small_ref,
    w2s_ref,
    wds_ref,
    a1_ref,
    aq_ref,
    nb,
    gb,
    wq,
    w1,
    w2,
    wd,
    vbuf,
    mbuf,
    ctab,
    stab,
    qstart,
    qh,
    kh,
    vh,
    o_t,
    lse,
    delta,
    mixed,
    act,
    ig,
    d_out,
    jg,
    dkv,
    svec,
    outp,
    rx,
    rz,
    cw,
    cq,
    cd,
    a1,
    aq,
    pkc,
    pkd,
    w1s,
    ssem,
    rsem,
    lsem,
    xfree,
    zfree,
    cfree,
    yfree,
):
    dp = lax.axis_index("dp")
    c = lax.axis_index("ctx")
    core = dp % 2
    y = dp // 2
    xx = c % 2
    z = c // 2
    cx = z * 2 + (1 - xx)
    mid = (z == 1) | (z == 2)
    end = (z == 0) | (z == 3)
    far = jnp.where(z < 2, 1, 0)
    zp = [z, z + 1 - 2 * (z % 2), 1 + far, 3 * far]
    dp_core = y * 2 + (1 - core)
    dp_y = (1 - y) * 2 + core
    dp_diag = (1 - y) * 2 + (1 - core)
    to_x = (dp, cx)
    to_outer = (dp, zp[1] * 2 + xx)
    to_inner = (dp, jnp.where(mid, 3 - z, zp[1]) * 2 + xx)
    to_core = (dp_core, c)
    to_y = (dp_y, c)
    dp_peers = [dp_core, dp_y, dp_diag]
    ctx_peers = [(c + o) % NC for o in range(1, NC)]
    pending = []
    counter = [0]

    def rows_of(i, n):
        return pl.ds(pl.multiple_of(i * n, n), n)

    def send(src, dst, ridx, dev, sidx=None):
        if sidx is None:
            sidx = counter[0]
            counter[0] += 1
        copy = pltpu.make_async_remote_copy(
            src_ref=src,
            dst_ref=dst,
            send_sem=ssem.at[sidx],
            recv_sem=rsem.at[ridx],
            device_id=dev,
            device_id_type=MESH_ID,
        )
        copy.start()
        return copy

    def new_send():
        counter[0] += 1
        return counter[0] - 1

    def got(dst, ridx):
        pltpu.make_async_remote_copy(
            src_ref=dst,
            dst_ref=dst,
            send_sem=ssem.at[0],
            recv_sem=rsem.at[ridx],
            device_id=to_x,
            device_id_type=MESH_ID,
        ).wait_recv()

    def sent(src, sidx):
        pltpu.make_async_remote_copy(
            src_ref=src,
            dst_ref=src,
            send_sem=ssem.at[sidx],
            recv_sem=rsem.at[0],
            device_id=to_x,
            device_id_type=MESH_ID,
        ).wait_send()

    def signal(sem, dev):
        pl.semaphore_signal(sem, inc=1, device_id=dev, device_id_type=MESH_ID)

    barrier = pltpu.get_barrier_semaphore()
    for p in dp_peers:
        signal(barrier, (p, c))
    for p in ctx_peers:
        signal(barrier, (dp, p))
    pl.semaphore_wait(barrier, len(dp_peers) + len(ctx_peers))

    def blk(buf, cc):
        return buf.at[rows_of(cc, BLK)]

    relays = []

    def half(ref, h):
        return ref.at[:, pl.ds(h * HALF, HALF)]

    def send_block(src, buf, base, cc, dev):
        for h in range(2):
            pending.append(send(half(src, h), half(blk(buf, cc), h), base + 2 * cc + h, dev))

    def send_if(cond, kind, buf, base, cc, dev):
        ids = [new_send(), new_send()]

        @pl.when(cond)
        def _():
            for h in range(2):
                part = half(blk(buf, cc), h)
                send(part, part, base + 2 * cc + h, dev, ids[h])

        relays.extend((kind, half(blk(buf, cc), h), ids[h]) for h in range(2))

    def arrive(buf, base, k, who):
        cc = zp[k] * 2 + xx
        over_x = (1,) if k == 1 else (0, 1)
        ids = [(new_send(), new_send()) for _ in range(2)]

        @pl.when(mid if who else end)
        def _():
            for h in range(2):
                part = half(blk(buf, cc), h)
                got(part, base + 2 * cc + h)
                if who:
                    send(part, part, base + 2 * cc + h, to_inner if k == 1 else to_outer, ids[h][0])
                if h in over_x:
                    send(part, part, base + 2 * cc + h, to_x, ids[h][1])

        for h in range(2):
            part = half(blk(buf, cc), h)
            if who:
                relays.append((1, part, ids[h][0]))
            if h in over_x:
                relays.append((int(who), part, ids[h][1]))

    partner_here = set()

    def from_x(buf, base, k):
        cc = zp[k] * 2 + (1 - xx)
        if k == 0:
            if base in partner_here:
                return
            partner_here.add(base)
        for h in range(2):
            got(half(blk(buf, cc), h), R_B[base] if (k, h) == (1, 0) else base + 2 * cc + h)

    def partner_part(buf, base):
        from_x(buf, base, 0)
        part = half(blk(buf, cx), 0)
        pending.append(send(part, part, R_B[base], to_outer))

    gb[rows_of(c, BLK), :] = g_ref[...]
    send_block(g_ref, gb, R_G, c, to_x)
    send_block(g_ref, gb, R_G, c, to_outer)
    send_if(mid, 1, gb, R_G, c, to_inner)

    pair_cols = outp.at[pl.ds(0, 512)]
    for i in range(12):
        pltpu.make_async_copy(
            wq_ref.at[:, pl.ds(pl.multiple_of(i * 512 + z * 128, 128), 128)],
            pair_cols.at[:, pl.ds(i * 128, 128)],
            lsem.at[0],
        ).start()

    def row_of(ref):
        return ref[...].astype(F32).reshape(1, ref.shape[0])

    bq_all = row_of(bq_ref)
    bq_own = [own_lanes(bq_all[:, j * 512 : (j + 1) * 512], 64, c, NC) for j in range(3)]
    b1_own = own_lanes(row_of(b1_ref), 256, c, NC)
    wide = [row_of(r) for r in (gain_ref, shift_ref, bd_ref, b2_ref)]
    wide += [jnp.concatenate(bq_own + [jnp.zeros((1, 320), F32)], 1)]
    wide += [jnp.concatenate([b1_own, jnp.zeros((1, 256), F32)], 1)]
    vbuf[dp] = jnp.concatenate(wide + [jnp.zeros((10, 512), F32)], 0).astype(BF)
    mbuf[c] = jnp.concatenate([seg_ref[...], pos_ref[...], jnp.zeros((6, BLK), jnp.int32)], 0)
    for p in dp_peers:
        pending.append(send(vbuf.at[dp], vbuf.at[dp], R_V + dp, (p, c)))
    for p in ctx_peers:
        pending.append(send(mbuf.at[c], mbuf.at[c], R_M + c, (dp, p)))

    def pieces(t, slot):
        if t == 0:
            return [(wq.at[rows_of(slot, 512)], wq.at[rows_of(slot, 512)])]
        if t == 1:
            return [
                (
                    w1_ref.at[:, pl.ds(pl.multiple_of(q * 2048 + c * 256, 256), 256)],
                    w1.at[rows_of(slot, 512), pl.ds(q * 256, 256)],
                )
                for q in range(ND)
            ]
        if t == 2:
            return [
                (
                    w2_ref.at[rows_of(c, 256), pl.ds(half * 1024, 1024)],
                    w2.at[pl.ds(pl.multiple_of(half * 1024 + slot * 256, 256), 256)],
                )
                for half in range(2)
            ]
        return [(wd_ref.at[rows_of(c, 64)], wd.at[rows_of(slot, 64)])]

    def whole(t):
        return [wq.at[pl.ds(0, 512)], w1.at[pl.ds(0, 512)], w2.at[pl.ds(0, 512)], wd.at[pl.ds(0, 64)]][t]

    wsent = []

    def weight_send(t):
        sy, sc = new_send(), new_send()
        for src, dst in pieces(t, dp):
            send(src, dst, R_WY + t, to_y, sy)
        for src, dst in pieces(t, dp):
            send(src, dst, R_WC + t, to_core, sc)
        if t > 0:
            for src, dst in pieces(t, dp):
                pltpu.make_async_copy(src, dst, lsem.at[t]).start()
        wsent.extend([(t, sy), (t, sc)])

    def pick_heads():
        pltpu.make_async_copy(wq_ref.at[:, pl.ds(0, 1536)], pair_cols.at[:, pl.ds(0, 1536)], lsem.at[0]).wait()
        low_half = lax.broadcasted_iota(jnp.int32, (512, 128), 1) < 64
        for i in range(6):
            a = outp[0:512, i * 256 : i * 256 + 128].astype(F32)
            b = outp[0:512, i * 256 + 128 : i * 256 + 256].astype(F32)
            left = jnp.where(xx == 1, pltpu.roll(a, 64, 1), a)
            right = jnp.where(xx == 0, pltpu.roll(b, 64, 1), b)
            wq[rows_of(dp, 512), i * 128 : (i + 1) * 128] = jnp.where(low_half, left, right).astype(BF)

    pick_heads()
    for t in range(4):
        weight_send(t)

    def weight_forward(t):
        got(whole(t), R_WY + t)
        sf = new_send()
        for _, dst in pieces(t, dp_y):
            send(dst, dst, R_WF + t, to_core, sf)
        wsent.append((t, sf))

    def weight_ready(t):
        got(whole(t), R_WC + t)
        got(whole(t), R_WF + t)
        if t > 0:
            pltpu.make_async_copy(whole(t), whole(t), lsem.at[t]).wait()

    for p in dp_peers:
        got(vbuf.at[p], R_V + p)
    slots = [vbuf[s].astype(F32) for s in range(ND)]

    def vec_row(i):
        return jnp.concatenate([slots[s][i : i + 1] for s in range(ND)], 1)

    gain = vec_row(0)
    shift = vec_row(1)
    out_bias = vec_row(2) + vec_row(3)
    bias_q = jnp.concatenate([slots[i // 3][4:5, (i % 3) * 64 : (i % 3 + 1) * 64] for i in range(12)], 1)
    bias_1 = jnp.concatenate([slots[s][5:6, :256] for s in range(ND)], 1)

    def norm_parts():
        xv = x_ref[...].astype(F32)
        center = xv - jnp.mean(xv, axis=1, keepdims=True)
        inv = lax.rsqrt(jnp.mean(center * center, axis=1, keepdims=True) + EPS)
        return center * inv, inv

    xhat, _ = norm_parts()
    nb[rows_of(c, BLK), :] = (xhat * gain + shift).astype(BF)

    send_block(blk(nb, c), nb, R_N, c, to_x)
    send_block(blk(nb, c), nb, R_N, c, to_outer)
    send_if(mid, 1, nb, R_N, c, to_inner)

    for p in ctx_peers:
        got(mbuf.at[p], R_M + p)
    seg = jnp.concatenate([mbuf[i, 0:1, :] for i in range(NC)], 1)
    pos = jnp.concatenate([mbuf[i, 1:2, :] for i in range(NC)], 1).astype(F32)
    first_len = jnp.sum((seg == 0).astype(jnp.int32).astype(F32), axis=1, keepdims=True).astype(jnp.int32)
    last_start = jnp.sum((seg <= 1).astype(jnp.int32).astype(F32), axis=1, keepdims=True).astype(jnp.int32)
    qstart[...] = jnp.where(seg == 0, 0, jnp.where(seg == 1, first_len, last_start))
    lane = lax.broadcasted_iota(jnp.int32, (16, PAIR), 0)
    freqs = jnp.zeros((16, PAIR), F32)
    for i, value in enumerate(FREQS):
        freqs = jnp.where(lane == i, value, freqs)
    for i in range(4):
        angles = freqs * pos[:, i * PAIR : (i + 1) * PAIR]
        cos_h, sin_h = jnp.cos(angles), jnp.sin(angles)
        ones, zeros = jnp.ones((32, PAIR), F32), jnp.zeros((32, PAIR), F32)
        ctab[i * PAIR : (i + 1) * PAIR, :] = jnp.transpose(
            jnp.concatenate([cos_h, cos_h, ones, cos_h, cos_h, ones], 0)
        )
        stab[i * PAIR : (i + 1) * PAIR, :] = jnp.transpose(
            jnp.concatenate([-sin_h, sin_h, zeros, -sin_h, sin_h, zeros], 0)
        )

    def turn(v, rows, sign):
        cos_t, sin_t = ctab[rows, :], stab[rows, :]
        halves = []
        for i in range(v.shape[1] // 128):
            part = v[:, i * 128 : (i + 1) * 128]
            halves.append(part * cos_t + sign * (swap_turned(part) * sin_t))
        return jnp.concatenate(halves, 1) if len(halves) > 1 else halves[0]

    def project(pair):
        rows = rows_of(pair, PAIR)
        xv = nb[rows, :]
        for part in range(3):
            cols = slice(part * 256, (part + 1) * 256)
            val = dot_nn(xv, wq[:, cols]) + bias_q[:, cols]
            if part < 2:
                val = turn(val, rows, 1.0)
            low = val.astype(BF)
            dest = (qh, kh, vh)[part]
            for h in range(HEADS_C):
                dest[h, rows, :] = low[:, h * 64 : (h + 1) * 64]

    def project_ff(pair):
        rows = rows_of(pair, PAIR)
        xv = nb[rows, :]
        for f in range(4):
            cols = slice(f * 256, (f + 1) * 256)
            u = dot_nn(xv, w1[:, cols]) + bias_1[:, cols]
            uu = u * u
            th = jnp.tanh(GELU_K * (u + GELU_A * (uu * u)))
            half = 0.5 * (1.0 + th)
            act[rows, cols] = (u * half).astype(BF)
            slope = half + 0.5 * u * (1.0 - th * th) * (GELU_K * (1.0 + 3.0 * GELU_A * uu))
            ig[rows, cols] = slope.astype(BF)

    def masked(s, i, kv):
        ji = lax.broadcasted_iota(jnp.int32, (kv, PAIR), 0)
        qi = lax.broadcasted_iota(jnp.int32, (1, PAIR), 1) + i * PAIR
        ok = (ji <= qi) & (ji >= qstart[:, i * PAIR : (i + 1) * PAIR])
        return ok, jnp.where(ok, s * SCALE, MASKED)

    def head_rows(h):
        return pl.ds(pl.multiple_of(h * 64, 64), 64)

    def attend(h, carry):
        for i in range(4):
            kv = (i + 1) * PAIR
            cols = slice(i * PAIR, (i + 1) * PAIR)
            _, s = masked(dot_nt(kh[h, 0:kv, :], qh[h, cols, :]), i, kv)
            m = jnp.max(s, axis=0, keepdims=True)
            p = jnp.exp(s - m)
            total = jnp.sum(p, axis=0, keepdims=True)
            probs = (p * (1.0 / total)).astype(BF)
            o_t[head_rows(h), cols] = dot_tn(vh[h, 0:kv, :], probs)
            lse[h, :, cols] = m + jnp.log(total)
        return carry

    x_sent = [[None] * 4, [None] * 4]
    z_sent = [[None] * 4, [None] * 4]
    src_of = (outp, gb)

    def reduce_x(op, k):
        cc = zp[k] * 2 + (1 - xx)
        if op == 1:
            pl.semaphore_wait(xfree.at[k], 1)
        x_sent[op][k] = [
            send(half(blk(src_of[op], cc), h), half(rx.at[k], h), R_X[op] + 2 * k + h, to_x) for h in range(2)
        ]

    def z_send(op, k, h, slot, dev):
        if op == 1 and h == 0:
            pl.semaphore_wait(zfree.at[slot], 1)
        send(half(rx.at[k], h), half(rz.at[slot], h), R_Z[op] + 2 * slot + h, dev, z_sent[op][k][h])

    def reduce_z(op, k, middle, h):
        if z_sent[op][k] is None:
            z_sent[op][k] = [new_send(), new_send()]
        slot_in = {3: 0, 2: 1, 1: 3}[k]

        def step():
            cols = slice(h * HALF, (h + 1) * HALF)
            got(half(rx.at[k], h), R_X[op] + 2 * k + h)
            total = rx[k, :, cols].astype(F32) + src_of[op][rows_of(zp[k] * 2 + xx, BLK), cols].astype(F32)
            if middle:
                got(half(rz.at[slot_in], h), R_Z[op] + 2 * slot_in + h)
                total = total + rz[slot_in, :, cols].astype(F32)
            rx[k, :, cols] = total.astype(BF)
            if not middle:
                z_send(op, k, h, 3 - k, to_outer)
            elif k == 1:
                z_send(op, k, h, 0, to_outer)
            else:
                z_send(op, k, h, 6 - k, to_inner)

        @pl.when(mid if middle else end)
        def _():
            step()
            if middle and op == 0 and h == 1:
                signal(zfree.at[slot_in], to_inner if k == 1 else to_outer)

    def got_slot(op, slot):
        for h in range(2):
            got(half(rz.at[slot], h), R_Z[op] + 2 * slot + h)

    def keep(total):
        for j in range(16):
            dkv[j // 8, (j % 8) * 128 : (j % 8 + 1) * 128, :] = total[:, j * 128 : (j + 1) * 128]

    def reduced(op, total):
        @pl.when(end)
        def _():
            got_slot(op, 0)
            keep(total + rz[0].astype(F32))
            if op == 0:
                signal(zfree.at[0], to_outer)

        @pl.when(mid)
        def _():
            got_slot(op, 2)
            got_slot(op, 4)
            keep(total + rz[2].astype(F32) + rz[4].astype(F32))
            if op == 0:
                signal(zfree.at[2], to_outer)
                signal(zfree.at[4], to_inner)

        return jnp.concatenate([dkv[j // 8, (j % 8) * 128 : (j % 8 + 1) * 128, :] for j in range(16)], 1)

    def partial_out(pair):
        rows = rows_of(pair, PAIR)
        mv, av = mixed[rows, :], act[rows, :]
        for n in range(8):
            cols = slice(n * 256, (n + 1) * 256)
            half, off = n // 4, (n % 4) * 256
            val = dot_nn(mv, wd[:, cols]) + dot_nn(av, w2[half * 1024 : (half + 1) * 1024, off : off + 256])
            outp[rows, cols] = val.astype(BF)

    svec[...] = jnp.zeros_like(svec)

    def backward_in(pair):
        rows = rows_of(pair, PAIR)
        ga, gc = gb[rows, 0:1024], gb[rows, 1024:2048]
        svec[0:1, :] += jnp.sum(gb[rows, :].astype(F32), axis=0, keepdims=True)
        for f in range(4):
            cols = slice(f * 256, (f + 1) * 256)
            val = dot_nt(ga, w2[f * 256 : (f + 1) * 256, :]) + dot_nt(gc, w2[1024 + f * 256 : 1024 + (f + 1) * 256, :])
            low = (val * ig[rows, cols].astype(F32)).astype(BF)
            ig[rows, cols] = low
            svec[1:2, cols] += jnp.sum(low.astype(F32), axis=0, keepdims=True)
        mg = (dot_nt(ga, wd[:, 0:1024]) + dot_nt(gc, wd[:, 1024:2048])).astype(BF)
        for h in range(HEADS_C):
            d_out[h, rows, :] = mg[:, h * 64 : (h + 1) * 64]
        prod = jnp.transpose(mg.astype(F32)) * o_t[:, rows]
        for h in range(HEADS_C):
            delta[h, :, rows] = jnp.sum(prod[h * 64 : (h + 1) * 64], axis=0, keepdims=True)

    def mix():
        for i in range(4):
            cols = slice(i * PAIR, (i + 1) * PAIR)
            mixed[cols, :] = jnp.transpose(o_t[:, cols]).astype(BF)

    arrive(nb, R_N, 1, True)
    arrive(nb, R_N, 1, False)
    arrive(nb, R_N, 2, True)
    weight_forward(0)
    from_x(gb, R_G, 0)
    from_x(nb, R_N, 0)
    arrive(nb, R_N, 2, False)
    arrive(nb, R_N, 3, False)
    arrive(nb, R_N, 3, True)
    partner_part(nb, R_N)
    weight_forward(1)
    arrive(gb, R_G, 1, True)
    arrive(gb, R_G, 2, True)
    weight_ready(1)
    arrive(gb, R_G, 3, True)
    arrive(gb, R_G, 1, False)
    from_x(nb, R_N, 1)
    project_ff(zp[1])
    weight_ready(0)
    project(zp[1])
    from_x(nb, R_N, 3)
    partner_part(gb, R_G)
    project(zp[0])
    project_ff(zp[3])
    from_x(nb, R_N, 2)
    project_ff(zp[0])
    project(zp[3])
    project(zp[2])
    arrive(gb, R_G, 2, False)
    lax.fori_loop(0, 2, attend, 0)
    weight_forward(2)
    lax.fori_loop(2, 4, attend, 0)
    mix()
    arrive(gb, R_G, 3, False)
    weight_forward(3)
    from_x(gb, R_G, 2)
    project_ff(zp[2])
    weight_ready(3)
    weight_ready(2)
    backward_in(zp[2])
    partial_out(zp[3])
    reduce_x(0, 3)
    partial_out(zp[2])
    reduce_x(0, 2)
    from_x(gb, R_G, 1)
    backward_in(zp[0])
    partial_out(zp[1])
    reduce_x(0, 1)
    backward_in(zp[1])
    partial_out(zp[0])
    reduce_x(0, 0)
    from_x(gb, R_G, 3)
    backward_in(zp[3])

    def sends_done():
        for t, s in wsent:
            sent(whole(t), s)
        for s in pending:
            s.wait_send()
        pending.clear()
        for kind, cond in ((1, mid), (0, end)):

            @pl.when(cond)
            def _():
                for kk, src, s in relays:
                    if kk == kind:
                        sent(src, s)

    def grad_ff_in():
        for f in range(8):
            for n in range(2):
                rows, cols = slice(f * 256, (f + 1) * 256), slice(n * 512, (n + 1) * 512)
                w1s[rows, cols] = dot_tn(nb[:, rows], ig[:, cols]).astype(BF)

    def grad_ff_out():
        for f in range(4):
            for n in range(4):
                cols = slice((n % 2) * 512, (n % 2 + 1) * 512)
                first = (n // 2) * 1024 + f * 256
                w2[first : first + 256, cols] = dot_tn(
                    act[:, f * 256 : (f + 1) * 256], gb[:, n * 512 : (n + 1) * 512]
                ).astype(BF)

    def grad_dense():
        for n in range(4):
            cols = slice(n * 512, (n + 1) * 512)
            wd[:, cols] = dot_tn(mixed[...], gb[:, cols]).astype(BF)

    def grad_joint():
        for f in range(8):
            rows = slice(f * 256, (f + 1) * 256)
            for n in range(3):
                cols = slice(n * 256, (n + 1) * 256)
                wq[rows, cols] = dot_tn(nb[:, rows], jg[:, cols]).astype(BF)

    def quarter(t, q):
        if t == 2:
            return [w2.at[pl.ds(pl.multiple_of(half * 1024 + q * 256, 256), 256)] for half in range(2)]
        if t == 3:
            return [wd.at[rows_of(q, 64)]]
        return [(wq, w1s)[t].at[rows_of(q, 512)]]

    def core_slot(t, yy):
        if t == 0:
            return [cq.at[yy]]
        if t == 1:
            return [cw.at[yy]]
        if t == 2:
            return [cw.at[yy, pl.ds(half * 256, 256)] for half in range(2)]
        return [cd.at[yy]]

    core_sent, y_sent = {}, {}

    def core_send(t):
        ids = []
        for yy in range(2):
            s = new_send()
            for src, dst in zip(quarter(t, yy * 2 + (1 - core)), core_slot(t, yy)):
                send(src, dst, R_C + t * 2 + yy, to_core, s)
            ids.append(s)
        core_sent[t] = ids

    def slot_whole(t, yy):
        return (cq, cw, cw, cd)[t].at[yy]

    def landing(t):
        return quarter(t, 1 - core)

    def y_send(t):
        for s in core_sent[t]:
            sent(slot_whole(t, 0), s)
        signal(yfree.at[t], to_y)
        for yy in range(2):
            got(slot_whole(t, yy), R_C + t * 2 + yy)
            for own, other in zip(quarter(t, yy * 2 + core), core_slot(t, yy)):
                own[...] = (own[...].astype(F32) + other[...].astype(F32)).astype(BF)
        if t == 1:
            signal(cfree.at[0], to_core)
        pl.semaphore_wait(yfree.at[t], 1)
        s = new_send()
        for src, dst in zip(quarter(t, (1 - y) * 2 + core), landing(t)):
            send(src, dst, R_Y + t, to_y, s)
        y_sent[t] = s

    def total(t):
        got(whole(t), R_Y + t)
        for own, other in zip(quarter(t, y * 2 + core), landing(t)):
            own[...] = (own[...].astype(F32) + other[...].astype(F32)).astype(BF)

    totalled = set()

    def exchange(t, buf, base, other):
        src = (wq, w1s)[t]
        first = (y * 2 + core) * 8
        if t not in totalled:
            totalled.add(t)
            total(t)
            buf[c] = src[rows_of(first + c, 64), :]
        if other:
            peers = [zp[k] * 2 + (1 - xx) for k in range(4)]
        else:
            peers = [zp[k] * 2 + xx for k in (1, 2, 3)]
        for p in peers:
            pending.append(send(src.at[rows_of(first + p, 64)], buf.at[c], base + c, (dp, p)))

    def partial_ff(pair):
        rows = rows_of(pair, PAIR)
        iv = ig[rows, :]
        for n in range(8):
            cols = slice(n * 256, (n + 1) * 256)
            gb[rows, cols] = dot_nt(iv, w1[cols, :]).astype(BF)

    def partial_attn(pair):
        rows = rows_of(pair, PAIR)
        jv = jg[rows, :]
        svec[1:2, 1024:1792] += jnp.sum(jv.astype(F32), axis=0, keepdims=True)
        for n in range(8):
            cols = slice(n * 256, (n + 1) * 256)
            gb[rows, cols] = (dot_nt(jv, wq[cols, :]) + gb[rows, cols].astype(F32)).astype(BF)

    def attend_back(hp, carry):
        for j in range(2):
            h = hp * 2 + j
            for i in (3, 2, 1, 0):
                kv = (i + 1) * PAIR
                cols = slice(i * PAIR, (i + 1) * PAIR)
                ok, s = masked(dot_nt(kh[h, 0:kv, :], qh[h, cols, :]), i, kv)
                p = jnp.where(ok, jnp.exp(s - lse[h, :, cols]), 0.0)
                dp_t = dot_nt(vh[h, 0:kv, :], d_out[h, cols, :])
                ds = (p * (dp_t - delta[h, :, cols])).astype(BF)
                dv = dot_nn(p.astype(BF), d_out[h, cols, :])
                dk = dot_nn(ds, qh[h, cols, :])
                both = jnp.concatenate([dk, dv], 1)
                if i == 3:
                    dkv[j, 0:kv, :] = both
                else:
                    dkv[j, 0:kv, :] += both
                o_t[head_rows(h), cols] = dot_tn(kh[h, 0:kv, :], ds)
        for i in range(4):
            rows = slice(i * PAIR, (i + 1) * PAIR)
            kk = jnp.concatenate([dkv[0, rows, 0:64], dkv[1, rows, 0:64]], 1) * SCALE
            vv = jnp.concatenate([dkv[0, rows, 64:128], dkv[1, rows, 64:128]], 1)
            jg[rows, pl.ds(pl.multiple_of(256 + hp * 128, 128), 128)] = turn(kk, rows, -1.0).astype(BF)
            jg[rows, pl.ds(pl.multiple_of(512 + hp * 128, 128), 128)] = vv.astype(BF)
        return carry

    def next_x(k):
        for h in range(2):
            sent(half(rx.at[k], h), z_sent[0][k][h])
        signal(xfree.at[k], to_x)
        reduce_x(1, k)

    outs = []

    def out_copy(src, dst):
        copy = pltpu.make_async_copy(src, dst, lsem.at[4 + len(outs)])
        copy.start()
        outs.append(copy)

    def finish_out_weights():
        total(2)
        for half in range(2):
            out_copy(quarter(2, y * 2 + core)[half], w2s_ref.at[:, pl.ds(half * 1024, 1024)])
        total(3)
        out_copy(quarter(3, y * 2 + core)[0], wds_ref)

    grad_ff_in()
    core_send(1)
    reduce_z(0, 3, False, 0)
    lax.fori_loop(0, 1, attend_back, 0)
    reduce_z(0, 3, False, 1)
    y_send(1)
    reduce_z(0, 2, False, 0)
    reduce_z(0, 3, True, 0)
    reduce_z(0, 3, True, 1)
    sends_done()
    grad_ff_out()
    grad_dense()
    reduce_z(0, 2, True, 0)
    reduce_z(0, 2, False, 1)
    for k in range(4):
        partial_ff(zp[k])
    reduce_z(0, 2, True, 1)
    reduce_z(0, 1, True, 0)
    reduce_z(0, 1, False, 0)
    lax.fori_loop(1, 2, attend_back, 0)
    for i in range(4):
        rows = slice(i * PAIR, (i + 1) * PAIR)
        jg[rows, 0:256] = turn(jnp.transpose(o_t[:, rows]) * SCALE, rows, -1.0).astype(BF)

    reduce_z(0, 1, False, 1)
    for k in range(4):
        partial_attn(zp[k])
    reduce_z(0, 1, True, 1)
    exchange(1, a1, R_A1, False)
    next_x(3)
    next_x(2)
    grad_joint()
    core_send(0)
    next_x(1)
    for h in range(2):
        got(half(rx.at[0], h), R_X[0] + h)
        x_sent[0][0][h].wait_send()
    outp[rows_of(cx, BLK), :] = rx[0]
    signal(xfree.at[0], to_x)
    reduce_x(1, 0)
    pl.semaphore_wait(cfree.at[0], 1)
    core_send(2)
    core_send(3)
    total_o = outp[rows_of(cx, BLK), :].astype(F32) + outp[rows_of(c, BLK), :].astype(F32)
    out_ref[...] = (x_ref[...].astype(F32) + out_bias + reduced(0, total_o)).astype(BF)

    reduce_z(1, 3, False, 0)
    y_send(0)
    reduce_z(1, 3, False, 1)
    reduce_z(1, 3, True, 0)
    reduce_z(1, 2, False, 0)
    reduce_z(1, 3, True, 1)
    reduce_z(1, 2, True, 0)
    reduce_z(1, 2, False, 1)
    exchange(0, aq, R_AQ, False)
    y_send(2)
    y_send(3)
    reduce_z(1, 2, True, 1)
    reduce_z(1, 1, False, 0)
    reduce_z(1, 1, True, 0)
    reduce_z(1, 1, False, 1)
    reduce_z(1, 1, True, 1)
    exchange(0, aq, R_AQ, True)
    exchange(1, a1, R_A1, True)

    for h in range(2):
        got(half(rx.at[0], h), R_X[1] + h)
    ng = reduced(1, rx[0].astype(F32) + gb[rows_of(c, BLK), :].astype(F32))
    xhat, inv = norm_parts()
    e = ng * gain
    m1 = jnp.mean(e, axis=1, keepdims=True)
    m2 = jnp.mean(e * xhat, axis=1, keepdims=True)
    xgrad_ref[...] = (g_ref[...].astype(F32) + (e - m1 - xhat * m2) * inv).astype(BF)
    pkc[c, 0:16, :] = as_rows(jnp.sum(ng * xhat, axis=0, keepdims=True))
    pkc[c, 16:32, :] = as_rows(jnp.sum(ng, axis=0, keepdims=True))
    pkc[c, 32:40, :] = as_rows(svec[1:2, 1024:2048])
    for p in ctx_peers:
        pending.append(send(pkc.at[c], pkc.at[c], R_PC + c, (dp, p)))
    finish_out_weights()

    for p in ctx_peers:
        got(pkc.at[p], R_PC + p)
    norm_sum = pkc[0, 0:32, :]
    for i in range(1, NC):
        norm_sum = norm_sum + pkc[i, 0:32, :]
    pkd[dp, 0:32, :] = norm_sum
    for i in range(NC):
        pkd[dp, 32 + i * 8 : 40 + i * 8, :] = pkc[i, 32:40, :]
    pkd[dp, 96:112, :] = as_rows(svec[0:1, :])
    pkd[dp, 112:120, :] = as_rows(svec[1:2, 0:1024])
    for p in dp_peers:
        pending.append(send(pkd.at[dp], pkd.at[dp], R_PD + dp, (p, c)))

    for p in ctx_peers:
        got(a1.at[p], R_A1 + p)
    out_copy(a1, a1_ref)
    for p in dp_peers:
        got(pkd.at[p], R_PD + p)
    small_ref[...] = pkd[0] + pkd[1] + pkd[2] + pkd[3]
    for p in ctx_peers:
        got(aq.at[p], R_AQ + p)
    out_copy(aq, aq_ref)

    for s in pending:
        s.wait_send()
    for h in range(2):
        for k in (3, 2, 1):
            x_sent[0][k][h].wait_send()
            sent(half(rx.at[k], h), z_sent[1][k][h])
        for k in range(4):
            x_sent[1][k][h].wait_send()
    for t in range(4):
        sent(whole(t), y_sent[t])
    for copy in outs:
        copy.wait()


def finish_kernel(
    out_in,
    xgrad_in,
    small,
    w2s_in,
    wds_in,
    a1_in,
    aq_in,
    out_ref,
    xgrad_ref,
    gain_ref,
    shift_ref,
    wqg_ref,
    bqg_ref,
    wdg_ref,
    bd_ref,
    w1g_ref,
    b1_ref,
    w2g_ref,
    b2_ref,
    w2s,
    wds,
    a1,
    aq,
    w2w,
    wdw,
    w1w,
    wqw,
    rows_o,
    rows_x,
    sems,
):
    dp = lax.axis_index("dp")
    c = lax.axis_index("ctx")
    me = dp * NC + c
    used = []

    def move(src, dst):
        copy = pltpu.make_async_copy(src, dst, sems.at[len(used)])
        copy.start()
        used.append(copy)
        return copy

    pairs = ((wds_in, wds), (out_in, rows_o), (xgrad_in, rows_x), (w2s_in, w2s), (a1_in, a1), (aq_in, aq))
    loads = [move(*p) for p in pairs]
    stores = []
    loads[0].wait()
    wdw[...] = wds[...].astype(F32)
    stores.append(move(wdw, wdg_ref))
    loads[1].wait()
    stores.append(move(rows_o, out_ref))
    loads[2].wait()
    stores.append(move(rows_x, xgrad_ref))
    loads[3].wait()
    w2w[...] = w2s[...].astype(F32)
    stores.append(move(w2w, w2g_ref))
    loads[4].wait()
    for q in range(ND):
        for i in range(NC):
            w1w[:, q * 2048 + i * 256 : q * 2048 + (i + 1) * 256] = a1[i, :, q * 256 : (q + 1) * 256].astype(F32)
    stores.append(move(w1w, w1g_ref))
    loads[5].wait()
    for o in range(12):
        for i in range(NC // 2):
            both = [aq[2 * i + j, :, o * 64 : (o + 1) * 64].astype(F32) for j in range(2)]
            wqw[:, o * 512 + i * 128 : o * 512 + (i + 1) * 128] = jnp.concatenate(both, 1)
    stores.append(move(wqw, wqg_ref))

    def own_64(first):
        row = small[pl.ds(first + me // 2, 1), :]
        return jnp.where(me % 2 == 0, row[:, 0:64], row[:, 64:128]).reshape(64)

    gain_ref[...] = own_64(0)
    shift_ref[...] = own_64(16)
    summed = own_64(96)
    bd_ref[...] = summed
    b2_ref[...] = summed
    rows = small[pl.ds(112 + dp * 2, 2), :]
    b1_ref[...] = jnp.concatenate([rows[0:1], rows[1:2]], 1).reshape(256)

    picked = []
    for j in range(3):
        head = me * 3 + j
        o, i = head // NC, head % NC
        row = small[pl.ds(32 + i * 8 + o // 2, 1), :]
        picked.append(jnp.where(o % 2 == 0, row[:, 0:64], row[:, 64:128]))
    bqg_ref[...] = jnp.concatenate(picked, 1).reshape(192)
    for copy in stores:
        copy.wait()


def fast_device(inputs, positions, seq_ids, ln_gain, ln_bias, w_qkv, b_qkv, w_dense, b_dense, w_fc1, b_fc1, w_fc2, b_fc2, cotangent):
    width = inputs.shape[2]
    vm = pl.BlockSpec(memory_space=pltpu.VMEM)
    hbm = pl.BlockSpec(memory_space=pl.ANY)
    dma = pltpu.SemaphoreType.DMA
    reg = pltpu.SemaphoreType.REGULAR
    sd = jax.ShapeDtypeStruct
    parts = pl.pallas_call(
        layer_kernel,
        out_shape=(
            sd((BLK, width), BF),
            sd((BLK, width), BF),
            sd((120, 128), F32),
            sd((256, 2048), BF),
            sd((64, 2048), BF),
            sd((NC, 64, 1024), BF),
            sd((NC, 64, 768), BF),
        ),
        in_specs=[vm] * 10 + [hbm] * 4,
        out_specs=(vm, vm, vm, hbm, hbm, hbm, hbm),
        scratch_shapes=[
            pltpu.VMEM((TOK, 2048), BF),
            pltpu.VMEM((TOK, 2048), BF),
            pltpu.VMEM((2048, 768), BF),
            pltpu.VMEM((2048, 1024), BF),
            pltpu.VMEM((2048, 1024), BF),
            pltpu.VMEM((256, 2048), BF),
            pltpu.VMEM((ND, 16, 512), BF),
            pltpu.VMEM((NC, 8, BLK), jnp.int32),
            pltpu.VMEM((TOK, 128), F32),
            pltpu.VMEM((TOK, 128), F32),
            pltpu.VMEM((1, TOK), jnp.int32),
            pltpu.VMEM((4, TOK, 64), BF),
            pltpu.VMEM((4, TOK, 64), BF),
            pltpu.VMEM((4, TOK, 64), BF),
            pltpu.VMEM((256, TOK), F32),
            pltpu.VMEM((4, 1, TOK), F32),
            pltpu.VMEM((4, 1, TOK), F32),
            pltpu.VMEM((TOK, 256), BF),
            pltpu.VMEM((TOK, 1024), BF),
            pltpu.VMEM((TOK, 1024), BF),
            pltpu.VMEM((4, TOK, 64), BF),
            pltpu.VMEM((TOK, 768), BF),
            pltpu.VMEM((2, TOK, 128), F32),
            pltpu.VMEM((8, 2048), F32),
            pltpu.VMEM((TOK, 2048), BF),
            pltpu.VMEM((4, BLK, 2048), BF),
            pltpu.VMEM((5, BLK, 2048), BF),
            pltpu.VMEM((2, 512, 1024), BF),
            pltpu.VMEM((2, 512, 768), BF),
            pltpu.VMEM((2, 64, 2048), BF),
            pltpu.VMEM((NC, 64, 1024), BF),
            pltpu.VMEM((NC, 64, 768), BF),
            pltpu.VMEM((NC, 40, 128), F32),
            pltpu.VMEM((ND, 120, 128), F32),
            pltpu.VMEM((2048, 1024), BF),
            dma((N_SEND,)),
            dma((N_RECV,)),
            dma((9,)),
            reg((4,)),
            reg((5,)),
            reg((1,)),
            reg((4,)),
        ],
        compiler_params=pltpu.CompilerParams(
            collective_id=0, has_side_effects=True, vmem_limit_bytes=63 * 1024 * 1024
        ),
        name="layer",
    )(
        inputs[0], cotangent[0], seq_ids, positions, ln_gain, ln_bias, b_dense, b_fc2, b_qkv, b_fc1, w_qkv, w_fc1, w_fc2, w_dense
    )
    done = pl.pallas_call(
        finish_kernel,
        out_shape=(
            sd((BLK, width), BF),
            sd((BLK, width), BF),
            sd((64,), F32),
            sd((64,), F32),
            sd((64, 6144), F32),
            sd((192,), F32),
            sd((64, 2048), F32),
            sd((64,), F32),
            sd((64, 8192), F32),
            sd((256,), F32),
            sd((256, 2048), F32),
            sd((64,), F32),
        ),
        in_specs=[hbm, hbm, vm, hbm, hbm, hbm, hbm],
        out_specs=(hbm, hbm, vm, vm, hbm, vm, hbm, vm, hbm, vm, hbm, vm),
        scratch_shapes=[
            pltpu.VMEM((256, 2048), BF),
            pltpu.VMEM((64, 2048), BF),
            pltpu.VMEM((NC, 64, 1024), BF),
            pltpu.VMEM((NC, 64, 768), BF),
            pltpu.VMEM((256, 2048), F32),
            pltpu.VMEM((64, 2048), F32),
            pltpu.VMEM((64, 8192), F32),
            pltpu.VMEM((64, 6144), F32),
            pltpu.VMEM((BLK, 2048), BF),
            pltpu.VMEM((BLK, 2048), BF),
            dma((12,)),
        ],
        compiler_params=pltpu.CompilerParams(vmem_limit_bytes=62 * 1024 * 1024),
        name="finish",
    )(*parts)
    return (done[0][None], done[1][None]) + tuple(done[2:])


def solution(mesh):
    placed = (
        P("dp", "ctx", None),
        P("dp", "ctx"),
        P("dp", "ctx"),
        P("dp"),
        P("dp"),
        P("dp", None),
        P("dp"),
        P("dp", None),
        P("dp"),
        P("dp", None),
        P("dp"),
        P("dp", None),
        P("dp"),
        P("dp", "ctx", None),
    )
    fits = mesh.shape["dp"] == ND and mesh.shape["ctx"] == NC
    return jax.shard_map(
        fast_device if fits else per_device,
        mesh=mesh,
        in_specs=placed,
        out_specs=(
            P("dp", "ctx", None),
            P("dp", "ctx", None),
            P(("dp", "ctx")),
            P(("dp", "ctx")),
            P(("dp", "ctx"), None),
            P(("dp", "ctx")),
            P(("dp", "ctx"), None),
            P(("dp", "ctx")),
            P(("dp", "ctx"), None),
            P(("dp", "ctx")),
            P(("dp", "ctx"), None),
            P(("dp", "ctx")),
        ),
        check_vma=False,
    )
```

```python
import math

import jax
import jax.numpy as jnp
import numpy as np
from jax import lax
from jax.experimental import pallas as pl
from jax.experimental.pallas import tpu as pltpu
from jax.sharding import PartitionSpec as P

HEAD_DIM = 64
ROT = 32


EPS = 1e-05
MASKED = -1e30
SCALE = 0.125
BASE = 10000.0


def layer_norm(values, gain_vec, shift_vec):
    center = values - jnp.mean(values, axis=1, keepdims=True)
    spread = jnp.mean(center * center, axis=1, keepdims=True)
    return center * lax.rsqrt(spread + EPS) * gain_vec + shift_vec


def gelu_tanh(values):
    return jax.nn.gelu(values, approximate=True)


def rotate(values, angle_pos):
    row_count = values.shape[0]
    head_count = values.shape[1] // HEAD_DIM
    half_rot = ROT // 2
    split_heads = values.reshape(row_count, head_count, HEAD_DIM)
    freqs = BASE ** (-(jnp.arange(half_rot, dtype=jnp.float32) * 2.0) / ROT)
    angles = angle_pos[:, None] * freqs[None, :]
    cosine = jnp.cos(angles)[:, None, :]
    sine = jnp.sin(angles)[:, None, :]
    first_half = split_heads[:, :, :half_rot]
    second_half = split_heads[:, :, half_rot:ROT]
    turned = jnp.concatenate(
        [
            first_half * cosine - second_half * sine,
            second_half * cosine + first_half * sine,
            split_heads[:, :, ROT:],
        ],
        axis=2,
    )
    return turned.reshape(row_count, head_count * HEAD_DIM)


def visible(query_index, query_seg, key_index, key_seg):
    causal = key_index[None, :] <= query_index[:, None]
    return causal[None] & (key_seg[:, None, :] == query_seg[:, :, None])


def split_cols(values, low_col, high_col):
    return values[:, :, low_col:high_col].reshape(
        values.shape[0], values.shape[1], (high_col - low_col) // HEAD_DIM, HEAD_DIM
    )


def head_scores(query_heads, key_heads, allowed):
    raw = (
        jnp.einsum("sqhd,skhd->shqk", query_heads, key_heads, preferred_element_type=jnp.float32)
        * SCALE
    )
    return jnp.where(allowed[:, None], raw, MASKED)


def unchanged(state):
    return state


def per_device(
    inputs,
    positions,
    seq_ids,
    ln_gain,
    ln_bias,
    w_qkv,
    b_qkv,
    w_dense,
    b_dense,
    w_fc1,
    b_fc1,
    w_fc2,
    b_fc2,
    cotangent,
):
    (
        gain_all,
        shift_all,
        qkv_all,
        qkv_offset,
        dense_all,
        dense_offset,
        fc1_all,
        fc1_offset,
        fc2_all,
        fc2_offset,
    ) = (
        lax.all_gather(ln_gain, "dp", axis=0, tiled=True),
        lax.all_gather(ln_bias, "dp", axis=0, tiled=True),
        lax.all_gather(w_qkv, "dp", axis=0, tiled=True),
        lax.all_gather(b_qkv, "dp", axis=0, tiled=True),
        lax.all_gather(w_dense, "dp", axis=0, tiled=True),
        lax.all_gather(b_dense, "dp", axis=0, tiled=True),
        lax.all_gather(w_fc1, "dp", axis=0, tiled=True),
        lax.all_gather(b_fc1, "dp", axis=0, tiled=True),
        lax.all_gather(w_fc2, "dp", axis=0, tiled=True),
        lax.all_gather(b_fc2, "dp", axis=0, tiled=True),
    )
    stream_count = inputs.shape[0]
    row_count = inputs.shape[1]
    width = inputs.shape[2]
    flat_rows = stream_count * row_count
    resid = inputs.reshape(flat_rows, width).astype(jnp.float32)
    head_count = width // HEAD_DIM
    group_heads = math.gcd(head_count, 8)
    group_cols = group_heads * HEAD_DIM
    group_count = head_count // group_heads
    angle_pos = positions.reshape(flat_rows).astype(jnp.float32)
    own_seg = seq_ids.astype(jnp.bfloat16)
    row_start = lax.axis_index("ctx") * row_count
    own_index = row_start + jnp.arange(row_count, dtype=jnp.int32)
    normed, norm_back = jax.vjp(
        layer_norm, resid, gain_all.astype(jnp.float32), shift_all.astype(jnp.float32)
    )
    hidden = normed.astype(jnp.bfloat16)
    joint = jnp.dot(hidden, qkv_all, preferred_element_type=jnp.float32) + qkv_offset.astype(
        jnp.float32
    )
    queries = (
        rotate(joint[:, :width], angle_pos)
        .astype(jnp.bfloat16)
        .reshape(stream_count, row_count, width)
    )
    keys_own = (
        rotate(joint[:, width : 2 * width], angle_pos)
        .astype(jnp.bfloat16)
        .reshape(stream_count, row_count, width)
    )
    values_own = joint[:, 2 * width :].astype(jnp.bfloat16).reshape(stream_count, row_count, width)
    start_state = (
        jnp.full((stream_count, head_count, row_count), MASKED, jnp.float32),
        jnp.zeros((stream_count, head_count, row_count), jnp.float32),
        jnp.zeros((stream_count, row_count, width), jnp.float32),
    )
    key_part = lax.all_gather(keys_own, "ctx", axis=1, tiled=True)
    value_part = lax.all_gather(values_own, "ctx", axis=1, tiled=True)
    seg_part = lax.all_gather(own_seg, "ctx", axis=1, tiled=True)
    key_count = key_part.shape[1]
    allowed = visible(own_index, own_seg, jnp.arange(key_count, dtype=jnp.int32), seg_part)

    def forward_compute(state):
        peak_in, total_in, accum_in = state
        peak_list, total_list, accum_list = ([], [], [])
        for group_index in range(group_count):
            low_col = group_index * group_cols
            high_col = low_col + group_cols
            low_head = group_index * group_heads
            high_head = low_head + group_heads
            scores = head_scores(
                split_cols(queries, low_col, high_col),
                split_cols(key_part, low_col, high_col),
                allowed,
            )
            old_peak = peak_in[:, low_head:high_head]
            new_peak = jnp.maximum(old_peak, jnp.max(scores, axis=3))
            weights = jnp.where(allowed[:, None], jnp.exp(scores - new_peak[:, :, :, None]), 0.0)
            total_list.append(jnp.sum(weights, axis=3))
            gathered_vals = jnp.einsum(
                "shqk,skhd->sqhd",
                weights.astype(jnp.bfloat16),
                split_cols(value_part, low_col, high_col),
                preferred_element_type=jnp.float32,
            )
            accum_list.append(gathered_vals.reshape(stream_count, row_count, group_cols))
            peak_list.append(new_peak)
        return (
            jnp.concatenate(peak_list, 1),
            jnp.concatenate(total_list, 1),
            jnp.concatenate(accum_list, 2),
        )

    result_state = lax.cond(
        jnp.int32(0) < row_start + row_count, forward_compute, unchanged, start_state
    )
    peak, total, accum = result_state
    attended = (
        accum.reshape(stream_count, row_count, head_count, HEAD_DIM)
        / jnp.transpose(total, (0, 2, 1))[:, :, :, None]
    ).reshape(stream_count, row_count, width)
    log_total = jnp.transpose(peak + jnp.log(total), (0, 2, 1))
    mixed = attended.astype(jnp.bfloat16).reshape(flat_rows, width)
    inner = jnp.dot(hidden, fc1_all, preferred_element_type=jnp.float32) + fc1_offset.astype(
        jnp.float32
    )
    active, gelu_back = jax.vjp(gelu_tanh, inner)
    active_low = active.astype(jnp.bfloat16)
    summed = (
        resid
        + jnp.dot(mixed, dense_all, preferred_element_type=jnp.float32)
        + dense_offset.astype(jnp.float32)
    )
    summed = (
        summed
        + jnp.dot(active_low, fc2_all, preferred_element_type=jnp.float32)
        + fc2_offset.astype(jnp.float32)
    )
    outputs = summed.astype(jnp.bfloat16).reshape(stream_count, row_count, width)
    upstream = cotangent.reshape(flat_rows, width)
    upstream_f = upstream.astype(jnp.float32)
    bias_term = jnp.sum(upstream_f, axis=0)
    fc2_term = jnp.einsum("tf,td->fd", active_low, upstream, preferred_element_type=jnp.float32)
    fc2_sum = lax.psum_scatter(fc2_term, ("dp", "ctx"), scatter_dimension=0, tiled=True)
    fc2_sum, upstream = lax.optimization_barrier((fc2_sum, upstream))
    act_grad = jnp.einsum("td,fd->tf", upstream, fc2_all, preferred_element_type=jnp.float32)
    inner_grad = gelu_back(act_grad)[0].astype(jnp.bfloat16)
    fc1_term = jnp.einsum("td,tf->df", hidden, inner_grad, preferred_element_type=jnp.float32)
    fc1_bias_term = jnp.sum(inner_grad.astype(jnp.float32), axis=0)
    fc1_sum = lax.psum_scatter(fc1_term, ("dp", "ctx"), scatter_dimension=0, tiled=True)
    fc1_sum, mixed, upstream, upstream_f, fc1_bias_term, inner_grad, hidden = lax.optimization_barrier(
        (fc1_sum, mixed, upstream, upstream_f, fc1_bias_term, inner_grad, hidden)
    )
    fc1_bias_sum, bias_sum = (
        lax.psum_scatter(fc1_bias_term, ("dp", "ctx"), scatter_dimension=0, tiled=True),
        lax.psum_scatter(bias_term, ("dp", "ctx"), scatter_dimension=0, tiled=True),
    )
    dense_term = jnp.einsum("td,te->de", mixed, upstream, preferred_element_type=jnp.float32)
    dense_sum = lax.psum_scatter(dense_term, ("dp", "ctx"), scatter_dimension=0, tiled=True)
    dense_sum, upstream, dense_all = lax.optimization_barrier((dense_sum, upstream, dense_all))
    mixed_grad = (
        jnp.einsum("te,de->td", upstream, dense_all, preferred_element_type=jnp.float32)
        .astype(jnp.bfloat16)
        .reshape(stream_count, row_count, width)
    )
    delta = jnp.sum(
        (mixed_grad.astype(jnp.float32) * attended).reshape(
            stream_count, row_count, head_count, HEAD_DIM
        ),
        axis=3,
    )
    zero_block = jnp.zeros((stream_count, row_count, width), jnp.float32)
    query_key_part = lax.all_gather(keys_own, "ctx", axis=1, tiled=True)
    query_value_part = lax.all_gather(values_own, "ctx", axis=1, tiled=True)
    seg_part = lax.all_gather(own_seg, "ctx", axis=1, tiled=True)
    key_count = query_key_part.shape[1]
    query_allowed = visible(own_index, own_seg, jnp.arange(key_count, dtype=jnp.int32), seg_part)

    def query_compute(grad_in):
        step_list = []
        for group_index in range(group_count):
            low_col = group_index * group_cols
            high_col = low_col + group_cols
            low_head = group_index * group_heads
            high_head = low_head + group_heads
            scores = head_scores(
                split_cols(queries, low_col, high_col),
                split_cols(query_key_part, low_col, high_col),
                query_allowed,
            )
            lse_here = jnp.transpose(log_total[:, :, low_head:high_head], (0, 2, 1))[:, :, :, None]
            delta_here = jnp.transpose(delta[:, :, low_head:high_head], (0, 2, 1))[:, :, :, None]
            probs = jnp.where(query_allowed[:, None], jnp.exp(scores - lse_here), 0.0)
            prob_grad = jnp.einsum(
                "sqhd,skhd->shqk",
                split_cols(mixed_grad, low_col, high_col),
                split_cols(query_value_part, low_col, high_col),
                preferred_element_type=jnp.float32,
            )
            score_grad = (probs * (prob_grad - delta_here)).astype(jnp.bfloat16)
            query_step = (
                jnp.einsum(
                    "shqk,skhd->sqhd",
                    score_grad,
                    split_cols(query_key_part, low_col, high_col),
                    preferred_element_type=jnp.float32,
                )
                * SCALE
            )
            step_list.append(query_step.reshape(stream_count, row_count, group_cols))
        return grad_in + jnp.concatenate(step_list, 2)

    result_grad = lax.cond(
        jnp.int32(0) < row_start + row_count, query_compute, unchanged, zero_block
    )
    log_total_all, delta_all = (
        lax.all_gather(log_total, "ctx", axis=1, tiled=True),
        lax.all_gather(delta, "ctx", axis=1, tiled=True),
    )
    start = jnp.int32(0)
    query_part = lax.all_gather(queries, "ctx", axis=1, tiled=True)
    grad_part = lax.all_gather(mixed_grad, "ctx", axis=1, tiled=True)
    seg_part = lax.all_gather(own_seg, "ctx", axis=1, tiled=True)
    query_count = query_part.shape[1]
    query_index = jnp.arange(query_count, dtype=jnp.int32)
    key_allowed = visible(query_index, seg_part, own_index, own_seg)
    lse_part = lax.dynamic_slice_in_dim(log_total_all, start, query_count, 1)

    def key_compute(state):
        key_in, value_in = state
        key_list, value_list = ([], [])
        for group_index in range(group_count):
            low_col = group_index * group_cols
            high_col = low_col + group_cols
            low_head = group_index * group_heads
            high_head = low_head + group_heads
            scores = head_scores(
                split_cols(query_part, low_col, high_col),
                split_cols(keys_own, low_col, high_col),
                key_allowed,
            )
            lse_here = jnp.transpose(lse_part[:, :, low_head:high_head], (0, 2, 1))[:, :, :, None]
            delta_here = jnp.transpose(delta_all[:, :, low_head:high_head], (0, 2, 1))[
                :, :, :, None
            ]
            probs = jnp.where(key_allowed[:, None], jnp.exp(scores - lse_here), 0.0)
            grad_heads = split_cols(grad_part, low_col, high_col)
            value_step = jnp.einsum(
                "shqk,sqhd->skhd",
                probs.astype(jnp.bfloat16),
                grad_heads,
                preferred_element_type=jnp.float32,
            )
            prob_grad = jnp.einsum(
                "sqhd,skhd->shqk",
                grad_heads,
                split_cols(values_own, low_col, high_col),
                preferred_element_type=jnp.float32,
            )
            score_grad = (probs * (prob_grad - delta_here)).astype(jnp.bfloat16)
            key_step = (
                jnp.einsum(
                    "shqk,sqhd->skhd",
                    score_grad,
                    split_cols(query_part, low_col, high_col),
                    preferred_element_type=jnp.float32,
                )
                * SCALE
            )
            key_list.append(key_step.reshape(stream_count, row_count, group_cols))
            value_list.append(value_step.reshape(stream_count, row_count, group_cols))
        return (key_in + jnp.concatenate(key_list, 2), value_in + jnp.concatenate(value_list, 2))

    result_pair = lax.cond(
        start + query_count > row_start, key_compute, unchanged, (zero_block, zero_block)
    )
    key_grad, value_grad = result_pair
    joint_grad = jnp.concatenate(
        [
            rotate(result_grad.reshape(flat_rows, width), -angle_pos),
            rotate(key_grad.reshape(flat_rows, width), -angle_pos),
            value_grad.reshape(flat_rows, width),
        ],
        axis=1,
    ).astype(jnp.bfloat16)
    qkv_term = jnp.einsum("td,te->de", hidden, joint_grad, preferred_element_type=jnp.float32)
    qkv_bias_term = jnp.sum(joint_grad.astype(jnp.float32), axis=0)
    hidden_grad = jnp.einsum("te,de->td", joint_grad, qkv_all, preferred_element_type=jnp.float32)
    hidden_grad = hidden_grad + jnp.einsum(
        "tf,df->td", inner_grad, fc1_all, preferred_element_type=jnp.float32
    )
    resid_grad, gain_term, shift_term = norm_back(hidden_grad)
    input_grad = (
        (upstream_f + resid_grad).astype(jnp.bfloat16).reshape(stream_count, row_count, width)
    )
    gain_sum, shift_sum, qkv_sum, qkv_bias_sum = (
        lax.psum_scatter(gain_term, ("dp", "ctx"), scatter_dimension=0, tiled=True),
        lax.psum_scatter(shift_term, ("dp", "ctx"), scatter_dimension=0, tiled=True),
        lax.psum_scatter(qkv_term, ("dp", "ctx"), scatter_dimension=0, tiled=True),
        lax.psum_scatter(qkv_bias_term, ("dp", "ctx"), scatter_dimension=0, tiled=True),
    )
    return (
        outputs,
        input_grad,
        gain_sum,
        shift_sum,
        qkv_sum,
        qkv_bias_sum,
        dense_sum,
        bias_sum,
        fc1_sum,
        fc1_bias_sum,
        fc2_sum,
        bias_sum,
    )


BF = jnp.bfloat16
F32 = jnp.float32
BLK = 128
PAIR = 256
NC = 8
ND = 4
TOK = NC * BLK
HEADS_C = 4
MESH_ID = pl.DeviceIdType.MESH
GELU_A = 0.044715
GELU_K = math.sqrt(2.0 / math.pi)

R_N, R_G, R_M, R_V = 0, 16, 32, 40
R_WY, R_WC, R_WF = 44, 48, 52
R_X = (56, 64)
R_Z = (72, 82)
R_C, R_Y = 92, 100
R_A1, R_AQ, R_PC, R_PD = 104, 112, 120, 128
R_B = {R_N: 132, R_G: 133}
N_RECV = 134
N_SEND = 200
HALF = 1024
FREQS = [float(np.float32(BASE) ** np.float32(-2.0 * i / ROT)) for i in range(ROT // 2)]


def dot_nn(a, b):
    return lax.dot_general(a, b, (((1,), (0,)), ((), ())), preferred_element_type=F32)


def dot_nt(a, b):
    return lax.dot_general(a, b, (((1,), (1,)), ((), ())), preferred_element_type=F32)


def dot_tn(a, b):
    return lax.dot_general(a, b, (((0,), (0,)), ((), ())), preferred_element_type=F32)


def swap_turned(v):
    lane = lax.broadcasted_iota(jnp.int32, v.shape, 1) % HEAD_DIM
    return jnp.where(lane < 16, pltpu.roll(v, 112, 1), pltpu.roll(v, 16, 1))


def as_rows(v):
    return jnp.concatenate([v[:, i * 128 : (i + 1) * 128] for i in range(v.shape[1] // 128)], 0)


def as_row(v):
    return jnp.concatenate([v[i : i + 1] for i in range(v.shape[0])], 1)


def own_lanes(row, width, index, count):
    total = jnp.zeros((1, width), F32)
    for i in range(count):
        total = total + jnp.where(index == i, row[:, i * width : (i + 1) * width], 0.0)
    return total


def layer_kernel(
    x_ref,
    g_ref,
    seg_ref,
    pos_ref,
    gain_ref,
    shift_ref,
    bd_ref,
    b2_ref,
    bq_ref,
    b1_ref,
    wq_ref,
    w1_ref,
    w2_ref,
    wd_ref,
    out_ref,
    xgrad_ref,
    small_ref,
    w2s_ref,
    wds_ref,
    a1_ref,
    aq_ref,
    nb,
    gb,
    wq,
    w1,
    w2,
    wd,
    vbuf,
    mbuf,
    ctab,
    stab,
    qstart,
    qh,
    kh,
    vh,
    o_t,
    lse,
    delta,
    mixed,
    act,
    ig,
    d_out,
    jg,
    dkv,
    svec,
    outp,
    rx,
    rz,
    cw,
    cq,
    cd,
    a1,
    aq,
    pkc,
    pkd,
    w1s,
    ssem,
    rsem,
    lsem,
    xfree,
    zfree,
    cfree,
    yfree,
):
    dp = lax.axis_index("dp")
    c = lax.axis_index("ctx")
    core = dp % 2
    y = dp // 2
    xx = c % 2
    z = c // 2
    cx = z * 2 + (1 - xx)
    mid = (z == 1) | (z == 2)
    end = (z == 0) | (z == 3)
    far = jnp.where(z < 2, 1, 0)
    zp = [z, z + 1 - 2 * (z % 2), 1 + far, 3 * far]
    dp_core = y * 2 + (1 - core)
    dp_y = (1 - y) * 2 + core
    dp_diag = (1 - y) * 2 + (1 - core)
    to_x = (dp, cx)
    to_outer = (dp, zp[1] * 2 + xx)
    to_inner = (dp, jnp.where(mid, 3 - z, zp[1]) * 2 + xx)
    to_core = (dp_core, c)
    to_y = (dp_y, c)
    dp_peers = [dp_core, dp_y, dp_diag]
    ctx_peers = [(c + o) % NC for o in range(1, NC)]
    pending = []
    counter = [0]

    def rows_of(i, n):
        return pl.ds(pl.multiple_of(i * n, n), n)

    def send(src, dst, ridx, dev, sidx=None):
        if sidx is None:
            sidx = counter[0]
            counter[0] += 1
        copy = pltpu.make_async_remote_copy(
            src_ref=src,
            dst_ref=dst,
            send_sem=ssem.at[sidx],
            recv_sem=rsem.at[ridx],
            device_id=dev,
            device_id_type=MESH_ID,
        )
        copy.start()
        return copy

    def new_send():
        counter[0] += 1
        return counter[0] - 1

    def got(dst, ridx):
        pltpu.make_async_remote_copy(
            src_ref=dst,
            dst_ref=dst,
            send_sem=ssem.at[0],
            recv_sem=rsem.at[ridx],
            device_id=to_x,
            device_id_type=MESH_ID,
        ).wait_recv()

    def sent(src, sidx):
        pltpu.make_async_remote_copy(
            src_ref=src,
            dst_ref=src,
            send_sem=ssem.at[sidx],
            recv_sem=rsem.at[0],
            device_id=to_x,
            device_id_type=MESH_ID,
        ).wait_send()

    def signal(sem, dev):
        pl.semaphore_signal(sem, inc=1, device_id=dev, device_id_type=MESH_ID)

    barrier = pltpu.get_barrier_semaphore()
    for p in dp_peers:
        signal(barrier, (p, c))
    for p in ctx_peers:
        signal(barrier, (dp, p))
    pl.semaphore_wait(barrier, len(dp_peers) + len(ctx_peers))

    def blk(buf, cc):
        return buf.at[rows_of(cc, BLK)]

    relays = []

    def half(ref, h):
        return ref.at[:, pl.ds(h * HALF, HALF)]

    def send_block(src, buf, base, cc, dev):
        for h in range(2):
            pending.append(send(half(src, h), half(blk(buf, cc), h), base + 2 * cc + h, dev))

    def send_if(cond, kind, buf, base, cc, dev):
        ids = [new_send(), new_send()]

        @pl.when(cond)
        def _():
            for h in range(2):
                part = half(blk(buf, cc), h)
                send(part, part, base + 2 * cc + h, dev, ids[h])

        relays.extend((kind, half(blk(buf, cc), h), ids[h]) for h in range(2))

    def arrive(buf, base, k, who):
        cc = zp[k] * 2 + xx
        over_x = (1,) if k == 1 else (0, 1)
        ids = [(new_send(), new_send()) for _ in range(2)]

        @pl.when(mid if who else end)
        def _():
            for h in range(2):
                part = half(blk(buf, cc), h)
                got(part, base + 2 * cc + h)
                if who:
                    send(part, part, base + 2 * cc + h, to_inner if k == 1 else to_outer, ids[h][0])
                if h in over_x:
                    send(part, part, base + 2 * cc + h, to_x, ids[h][1])

        for h in range(2):
            part = half(blk(buf, cc), h)
            if who:
                relays.append((1, part, ids[h][0]))
            if h in over_x:
                relays.append((int(who), part, ids[h][1]))

    partner_here = set()

    def from_x(buf, base, k):
        cc = zp[k] * 2 + (1 - xx)
        if k == 0:
            if base in partner_here:
                return
            partner_here.add(base)
        for h in range(2):
            got(half(blk(buf, cc), h), R_B[base] if (k, h) == (1, 0) else base + 2 * cc + h)

    def partner_part(buf, base):
        from_x(buf, base, 0)
        part = half(blk(buf, cx), 0)
        pending.append(send(part, part, R_B[base], to_outer))

    gb[rows_of(c, BLK), :] = g_ref[...]
    send_block(g_ref, gb, R_G, c, to_x)
    send_block(g_ref, gb, R_G, c, to_outer)
    send_if(mid, 1, gb, R_G, c, to_inner)

    pair_cols = outp.at[pl.ds(0, 512)]
    for i in range(12):
        pltpu.make_async_copy(
            wq_ref.at[:, pl.ds(pl.multiple_of(i * 512 + z * 128, 128), 128)],
            pair_cols.at[:, pl.ds(i * 128, 128)],
            lsem.at[0],
        ).start()

    def row_of(ref):
        return ref[...].astype(F32).reshape(1, ref.shape[0])

    bq_all = row_of(bq_ref)
    bq_own = [own_lanes(bq_all[:, j * 512 : (j + 1) * 512], 64, c, NC) for j in range(3)]
    b1_own = own_lanes(row_of(b1_ref), 256, c, NC)
    wide = [row_of(r) for r in (gain_ref, shift_ref, bd_ref, b2_ref)]
    wide += [jnp.concatenate(bq_own + [jnp.zeros((1, 320), F32)], 1)]
    wide += [jnp.concatenate([b1_own, jnp.zeros((1, 256), F32)], 1)]
    vbuf[dp] = jnp.concatenate(wide + [jnp.zeros((10, 512), F32)], 0).astype(BF)
    mbuf[c] = jnp.concatenate([seg_ref[...], pos_ref[...], jnp.zeros((6, BLK), jnp.int32)], 0)
    for p in dp_peers:
        pending.append(send(vbuf.at[dp], vbuf.at[dp], R_V + dp, (p, c)))
    for p in ctx_peers:
        pending.append(send(mbuf.at[c], mbuf.at[c], R_M + c, (dp, p)))

    def pieces(t, slot):
        if t == 0:
            return [(wq.at[rows_of(slot, 512)], wq.at[rows_of(slot, 512)])]
        if t == 1:
            return [
                (
                    w1_ref.at[:, pl.ds(pl.multiple_of(q * 2048 + c * 256, 256), 256)],
                    w1.at[rows_of(slot, 512), pl.ds(q * 256, 256)],
                )
                for q in range(ND)
            ]
        if t == 2:
            return [
                (
                    w2_ref.at[rows_of(c, 256), pl.ds(half * 1024, 1024)],
                    w2.at[pl.ds(pl.multiple_of(half * 1024 + slot * 256, 256), 256)],
                )
                for half in range(2)
            ]
        return [(wd_ref.at[rows_of(c, 64)], wd.at[rows_of(slot, 64)])]

    def whole(t):
        return [wq.at[pl.ds(0, 512)], w1.at[pl.ds(0, 512)], w2.at[pl.ds(0, 512)], wd.at[pl.ds(0, 64)]][t]

    wsent = []

    def weight_send(t):
        sy, sc = new_send(), new_send()
        for src, dst in pieces(t, dp):
            send(src, dst, R_WY + t, to_y, sy)
        for src, dst in pieces(t, dp):
            send(src, dst, R_WC + t, to_core, sc)
        if t > 0:
            for src, dst in pieces(t, dp):
                pltpu.make_async_copy(src, dst, lsem.at[t]).start()
        wsent.extend([(t, sy), (t, sc)])

    def pick_heads():
        pltpu.make_async_copy(wq_ref.at[:, pl.ds(0, 1536)], pair_cols.at[:, pl.ds(0, 1536)], lsem.at[0]).wait()
        low_half = lax.broadcasted_iota(jnp.int32, (512, 128), 1) < 64
        for i in range(6):
            a = outp[0:512, i * 256 : i * 256 + 128].astype(F32)
            b = outp[0:512, i * 256 + 128 : i * 256 + 256].astype(F32)
            left = jnp.where(xx == 1, pltpu.roll(a, 64, 1), a)
            right = jnp.where(xx == 0, pltpu.roll(b, 64, 1), b)
            wq[rows_of(dp, 512), i * 128 : (i + 1) * 128] = jnp.where(low_half, left, right).astype(BF)

    pick_heads()
    for t in range(4):
        weight_send(t)

    def weight_forward(t):
        got(whole(t), R_WY + t)
        sf = new_send()
        for _, dst in pieces(t, dp_y):
            send(dst, dst, R_WF + t, to_core, sf)
        wsent.append((t, sf))

    def weight_ready(t):
        got(whole(t), R_WC + t)
        got(whole(t), R_WF + t)
        if t > 0:
            pltpu.make_async_copy(whole(t), whole(t), lsem.at[t]).wait()

    for p in dp_peers:
        got(vbuf.at[p], R_V + p)
    slots = [vbuf[s].astype(F32) for s in range(ND)]

    def vec_row(i):
        return jnp.concatenate([slots[s][i : i + 1] for s in range(ND)], 1)

    gain = vec_row(0)
    shift = vec_row(1)
    out_bias = vec_row(2) + vec_row(3)
    bias_q = jnp.concatenate([slots[i // 3][4:5, (i % 3) * 64 : (i % 3 + 1) * 64] for i in range(12)], 1)
    bias_1 = jnp.concatenate([slots[s][5:6, :256] for s in range(ND)], 1)

    def norm_parts():
        xv = x_ref[...].astype(F32)
        center = xv - jnp.mean(xv, axis=1, keepdims=True)
        inv = lax.rsqrt(jnp.mean(center * center, axis=1, keepdims=True) + EPS)
        return center * inv, inv

    xhat, _ = norm_parts()
    nb[rows_of(c, BLK), :] = (xhat * gain + shift).astype(BF)

    send_block(blk(nb, c), nb, R_N, c, to_x)
    send_block(blk(nb, c), nb, R_N, c, to_outer)
    send_if(mid, 1, nb, R_N, c, to_inner)

    for p in ctx_peers:
        got(mbuf.at[p], R_M + p)
    seg = jnp.concatenate([mbuf[i, 0:1, :] for i in range(NC)], 1)
    pos = jnp.concatenate([mbuf[i, 1:2, :] for i in range(NC)], 1).astype(F32)
    first_len = jnp.sum((seg == 0).astype(jnp.int32).astype(F32), axis=1, keepdims=True).astype(jnp.int32)
    last_start = jnp.sum((seg <= 1).astype(jnp.int32).astype(F32), axis=1, keepdims=True).astype(jnp.int32)
    qstart[...] = jnp.where(seg == 0, 0, jnp.where(seg == 1, first_len, last_start))
    lane = lax.broadcasted_iota(jnp.int32, (16, PAIR), 0)
    freqs = jnp.zeros((16, PAIR), F32)
    for i, value in enumerate(FREQS):
        freqs = jnp.where(lane == i, value, freqs)
    for i in range(4):
        angles = freqs * pos[:, i * PAIR : (i + 1) * PAIR]
        cos_h, sin_h = jnp.cos(angles), jnp.sin(angles)
        ones, zeros = jnp.ones((32, PAIR), F32), jnp.zeros((32, PAIR), F32)
        ctab[i * PAIR : (i + 1) * PAIR, :] = jnp.transpose(
            jnp.concatenate([cos_h, cos_h, ones, cos_h, cos_h, ones], 0)
        )
        stab[i * PAIR : (i + 1) * PAIR, :] = jnp.transpose(
            jnp.concatenate([-sin_h, sin_h, zeros, -sin_h, sin_h, zeros], 0)
        )

    def turn(v, rows, sign):
        cos_t, sin_t = ctab[rows, :], stab[rows, :]
        halves = []
        for i in range(v.shape[1] // 128):
            part = v[:, i * 128 : (i + 1) * 128]
            halves.append(part * cos_t + sign * (swap_turned(part) * sin_t))
        return jnp.concatenate(halves, 1) if len(halves) > 1 else halves[0]

    def project(pair):
        rows = rows_of(pair, PAIR)
        xv = nb[rows, :]
        for part in range(3):
            cols = slice(part * 256, (part + 1) * 256)
            val = dot_nn(xv, wq[:, cols]) + bias_q[:, cols]
            if part < 2:
                val = turn(val, rows, 1.0)
            low = val.astype(BF)
            dest = (qh, kh, vh)[part]
            for h in range(HEADS_C):
                dest[h, rows, :] = low[:, h * 64 : (h + 1) * 64]

    def project_ff(pair):
        rows = rows_of(pair, PAIR)
        xv = nb[rows, :]
        for f in range(4):
            cols = slice(f * 256, (f + 1) * 256)
            u = dot_nn(xv, w1[:, cols]) + bias_1[:, cols]
            uu = u * u
            th = jnp.tanh(GELU_K * (u + GELU_A * (uu * u)))
            half = 0.5 * (1.0 + th)
            act[rows, cols] = (u * half).astype(BF)
            slope = half + 0.5 * u * (1.0 - th * th) * (GELU_K * (1.0 + 3.0 * GELU_A * uu))
            ig[rows, cols] = slope.astype(BF)

    def masked(s, i, kv):
        ji = lax.broadcasted_iota(jnp.int32, (kv, PAIR), 0)
        qi = lax.broadcasted_iota(jnp.int32, (1, PAIR), 1) + i * PAIR
        ok = (ji <= qi) & (ji >= qstart[:, i * PAIR : (i + 1) * PAIR])
        return ok, jnp.where(ok, s * SCALE, MASKED)

    def head_rows(h):
        return pl.ds(pl.multiple_of(h * 64, 64), 64)

    def attend(h, carry):
        for i in range(4):
            kv = (i + 1) * PAIR
            cols = slice(i * PAIR, (i + 1) * PAIR)
            _, s = masked(dot_nt(kh[h, 0:kv, :], qh[h, cols, :]), i, kv)
            m = jnp.max(s, axis=0, keepdims=True)
            p = jnp.exp(s - m)
            total = jnp.sum(p, axis=0, keepdims=True)
            probs = (p * (1.0 / total)).astype(BF)
            o_t[head_rows(h), cols] = dot_tn(vh[h, 0:kv, :], probs)
            lse[h, :, cols] = m + jnp.log(total)
        return carry

    x_sent = [[None] * 4, [None] * 4]
    z_sent = [[None] * 4, [None] * 4]
    src_of = (outp, gb)

    def reduce_x(op, k):
        cc = zp[k] * 2 + (1 - xx)
        if op == 1:
            pl.semaphore_wait(xfree.at[k], 1)
        x_sent[op][k] = [
            send(half(blk(src_of[op], cc), h), half(rx.at[k], h), R_X[op] + 2 * k + h, to_x) for h in range(2)
        ]

    def z_send(op, k, h, slot, dev):
        if op == 1 and h == 0:
            pl.semaphore_wait(zfree.at[slot], 1)
        send(half(rx.at[k], h), half(rz.at[slot], h), R_Z[op] + 2 * slot + h, dev, z_sent[op][k][h])

    def reduce_z(op, k, middle, h):
        if z_sent[op][k] is None:
            z_sent[op][k] = [new_send(), new_send()]
        slot_in = {3: 0, 2: 1, 1: 3}[k]

        def step():
            cols = slice(h * HALF, (h + 1) * HALF)
            got(half(rx.at[k], h), R_X[op] + 2 * k + h)
            total = rx[k, :, cols].astype(F32) + src_of[op][rows_of(zp[k] * 2 + xx, BLK), cols].astype(F32)
            if middle:
                got(half(rz.at[slot_in], h), R_Z[op] + 2 * slot_in + h)
                total = total + rz[slot_in, :, cols].astype(F32)
            rx[k, :, cols] = total.astype(BF)
            if not middle:
                z_send(op, k, h, 3 - k, to_outer)
            elif k == 1:
                z_send(op, k, h, 0, to_outer)
            else:
                z_send(op, k, h, 6 - k, to_inner)

        @pl.when(mid if middle else end)
        def _():
            step()
            if middle and op == 0 and h == 1:
                signal(zfree.at[slot_in], to_inner if k == 1 else to_outer)

    def got_slot(op, slot):
        for h in range(2):
            got(half(rz.at[slot], h), R_Z[op] + 2 * slot + h)

    def keep(total):
        for j in range(16):
            dkv[j // 8, (j % 8) * 128 : (j % 8 + 1) * 128, :] = total[:, j * 128 : (j + 1) * 128]

    def reduced(op, total):
        @pl.when(end)
        def _():
            got_slot(op, 0)
            keep(total + rz[0].astype(F32))
            if op == 0:
                signal(zfree.at[0], to_outer)

        @pl.when(mid)
        def _():
            got_slot(op, 2)
            got_slot(op, 4)
            keep(total + rz[2].astype(F32) + rz[4].astype(F32))
            if op == 0:
                signal(zfree.at[2], to_outer)
                signal(zfree.at[4], to_inner)

        return jnp.concatenate([dkv[j // 8, (j % 8) * 128 : (j % 8 + 1) * 128, :] for j in range(16)], 1)

    def partial_out(pair):
        rows = rows_of(pair, PAIR)
        mv, av = mixed[rows, :], act[rows, :]
        for n in range(8):
            cols = slice(n * 256, (n + 1) * 256)
            half, off = n // 4, (n % 4) * 256
            val = dot_nn(mv, wd[:, cols]) + dot_nn(av, w2[half * 1024 : (half + 1) * 1024, off : off + 256])
            outp[rows, cols] = val.astype(BF)

    svec[...] = jnp.zeros_like(svec)

    def backward_in(pair):
        rows = rows_of(pair, PAIR)
        ga, gc = gb[rows, 0:1024], gb[rows, 1024:2048]
        svec[0:1, :] += jnp.sum(gb[rows, :].astype(F32), axis=0, keepdims=True)
        for f in range(4):
            cols = slice(f * 256, (f + 1) * 256)
            val = dot_nt(ga, w2[f * 256 : (f + 1) * 256, :]) + dot_nt(gc, w2[1024 + f * 256 : 1024 + (f + 1) * 256, :])
            low = (val * ig[rows, cols].astype(F32)).astype(BF)
            ig[rows, cols] = low
            svec[1:2, cols] += jnp.sum(low.astype(F32), axis=0, keepdims=True)
        mg = (dot_nt(ga, wd[:, 0:1024]) + dot_nt(gc, wd[:, 1024:2048])).astype(BF)
        for h in range(HEADS_C):
            d_out[h, rows, :] = mg[:, h * 64 : (h + 1) * 64]
        prod = jnp.transpose(mg.astype(F32)) * o_t[:, rows]
        for h in range(HEADS_C):
            delta[h, :, rows] = jnp.sum(prod[h * 64 : (h + 1) * 64], axis=0, keepdims=True)

    def mix():
        for i in range(4):
            cols = slice(i * PAIR, (i + 1) * PAIR)
            mixed[cols, :] = jnp.transpose(o_t[:, cols]).astype(BF)

    arrive(nb, R_N, 1, False)
    arrive(nb, R_N, 2, False)
    arrive(nb, R_N, 1, True)
    arrive(nb, R_N, 2, True)
    weight_forward(0)
    arrive(nb, R_N, 3, False)
    arrive(nb, R_N, 3, True)
    partner_part(nb, R_N)
    weight_ready(0)
    weight_forward(1)
    arrive(gb, R_G, 1, True)
    from_x(nb, R_N, 0)
    project(zp[0])
    weight_ready(1)
    from_x(nb, R_N, 2)
    project(zp[2])
    arrive(gb, R_G, 1, False)
    arrive(gb, R_G, 2, True)
    project_ff(zp[2])
    from_x(nb, R_N, 3)
    from_x(nb, R_N, 1)
    arrive(gb, R_G, 3, True)
    project(zp[1])
    project(zp[3])
    lax.fori_loop(0, 2, attend, 0)
    arrive(gb, R_G, 2, False)
    project_ff(zp[3])
    project_ff(zp[1])
    weight_forward(2)
    lax.fori_loop(2, 4, attend, 0)
    mix()
    partner_part(gb, R_G)
    arrive(gb, R_G, 3, False)
    weight_ready(2)
    weight_forward(3)
    project_ff(zp[0])
    from_x(gb, R_G, 0)
    from_x(gb, R_G, 2)
    weight_ready(3)
    partial_out(zp[3])
    reduce_x(0, 3)
    partial_out(zp[2])
    reduce_x(0, 2)
    partial_out(zp[1])
    reduce_x(0, 1)
    backward_in(zp[0])
    backward_in(zp[2])
    from_x(gb, R_G, 1)
    backward_in(zp[1])
    partial_out(zp[0])
    reduce_x(0, 0)
    from_x(gb, R_G, 3)
    backward_in(zp[3])

    def sends_done():
        for t, s in wsent:
            sent(whole(t), s)
        for s in pending:
            s.wait_send()
        pending.clear()
        for kind, cond in ((1, mid), (0, end)):

            @pl.when(cond)
            def _():
                for kk, src, s in relays:
                    if kk == kind:
                        sent(src, s)

    def grad_ff_in():
        for f in range(8):
            for n in range(2):
                rows, cols = slice(f * 256, (f + 1) * 256), slice(n * 512, (n + 1) * 512)
                w1s[rows, cols] = dot_tn(nb[:, rows], ig[:, cols]).astype(BF)

    def grad_ff_out():
        for f in range(4):
            for n in range(4):
                cols = slice((n % 2) * 512, (n % 2 + 1) * 512)
                first = (n // 2) * 1024 + f * 256
                w2[first : first + 256, cols] = dot_tn(
                    act[:, f * 256 : (f + 1) * 256], gb[:, n * 512 : (n + 1) * 512]
                ).astype(BF)

    def grad_dense():
        for n in range(4):
            cols = slice(n * 512, (n + 1) * 512)
            wd[:, cols] = dot_tn(mixed[...], gb[:, cols]).astype(BF)

    def grad_joint():
        for f in range(8):
            rows = slice(f * 256, (f + 1) * 256)
            for n in range(3):
                cols = slice(n * 256, (n + 1) * 256)
                wq[rows, cols] = dot_tn(nb[:, rows], jg[:, cols]).astype(BF)

    def quarter(t, q):
        if t == 2:
            return [w2.at[pl.ds(pl.multiple_of(half * 1024 + q * 256, 256), 256)] for half in range(2)]
        if t == 3:
            return [wd.at[rows_of(q, 64)]]
        return [(wq, w1s)[t].at[rows_of(q, 512)]]

    def core_slot(t, yy):
        if t == 0:
            return [cq.at[yy]]
        if t == 1:
            return [cw.at[yy]]
        if t == 2:
            return [cw.at[yy, pl.ds(half * 256, 256)] for half in range(2)]
        return [cd.at[yy]]

    core_sent, y_sent = {}, {}

    def core_send(t):
        ids = []
        for yy in range(2):
            s = new_send()
            for src, dst in zip(quarter(t, yy * 2 + (1 - core)), core_slot(t, yy)):
                send(src, dst, R_C + t * 2 + yy, to_core, s)
            ids.append(s)
        core_sent[t] = ids

    def slot_whole(t, yy):
        return (cq, cw, cw, cd)[t].at[yy]

    def landing(t):
        return quarter(t, 1 - core)

    def y_send(t):
        for s in core_sent[t]:
            sent(slot_whole(t, 0), s)
        signal(yfree.at[t], to_y)
        for yy in range(2):
            got(slot_whole(t, yy), R_C + t * 2 + yy)
            for own, other in zip(quarter(t, yy * 2 + core), core_slot(t, yy)):
                own[...] = (own[...].astype(F32) + other[...].astype(F32)).astype(BF)
        if t == 1:
            signal(cfree.at[0], to_core)
        pl.semaphore_wait(yfree.at[t], 1)
        s = new_send()
        for src, dst in zip(quarter(t, (1 - y) * 2 + core), landing(t)):
            send(src, dst, R_Y + t, to_y, s)
        y_sent[t] = s

    def total(t):
        got(whole(t), R_Y + t)
        for own, other in zip(quarter(t, y * 2 + core), landing(t)):
            own[...] = (own[...].astype(F32) + other[...].astype(F32)).astype(BF)

    totalled = set()

    def exchange(t, buf, base, other):
        src = (wq, w1s)[t]
        first = (y * 2 + core) * 8
        if t not in totalled:
            totalled.add(t)
            total(t)
            buf[c] = src[rows_of(first + c, 64), :]
        if other:
            peers = [zp[k] * 2 + (1 - xx) for k in range(4)]
        else:
            peers = [zp[k] * 2 + xx for k in (1, 2, 3)]
        for p in peers:
            pending.append(send(src.at[rows_of(first + p, 64)], buf.at[c], base + c, (dp, p)))

    def partial_ff(pair):
        rows = rows_of(pair, PAIR)
        iv = ig[rows, :]
        for n in range(8):
            cols = slice(n * 256, (n + 1) * 256)
            gb[rows, cols] = dot_nt(iv, w1[cols, :]).astype(BF)

    def partial_attn(pair):
        rows = rows_of(pair, PAIR)
        jv = jg[rows, :]
        svec[1:2, 1024:1792] += jnp.sum(jv.astype(F32), axis=0, keepdims=True)
        for n in range(8):
            cols = slice(n * 256, (n + 1) * 256)
            gb[rows, cols] = (dot_nt(jv, wq[cols, :]) + gb[rows, cols].astype(F32)).astype(BF)

    def attend_back(hp, carry):
        for j in range(2):
            h = hp * 2 + j
            for i in (3, 2, 1, 0):
                kv = (i + 1) * PAIR
                cols = slice(i * PAIR, (i + 1) * PAIR)
                ok, s = masked(dot_nt(kh[h, 0:kv, :], qh[h, cols, :]), i, kv)
                p = jnp.where(ok, jnp.exp(s - lse[h, :, cols]), 0.0)
                dp_t = dot_nt(vh[h, 0:kv, :], d_out[h, cols, :])
                ds = (p * (dp_t - delta[h, :, cols])).astype(BF)
                dv = dot_nn(p.astype(BF), d_out[h, cols, :])
                dk = dot_nn(ds, qh[h, cols, :])
                both = jnp.concatenate([dk, dv], 1)
                if i == 3:
                    dkv[j, 0:kv, :] = both
                else:
                    dkv[j, 0:kv, :] += both
                o_t[head_rows(h), cols] = dot_tn(kh[h, 0:kv, :], ds)
        for i in range(4):
            rows = slice(i * PAIR, (i + 1) * PAIR)
            kk = jnp.concatenate([dkv[0, rows, 0:64], dkv[1, rows, 0:64]], 1) * SCALE
            vv = jnp.concatenate([dkv[0, rows, 64:128], dkv[1, rows, 64:128]], 1)
            jg[rows, pl.ds(pl.multiple_of(256 + hp * 128, 128), 128)] = turn(kk, rows, -1.0).astype(BF)
            jg[rows, pl.ds(pl.multiple_of(512 + hp * 128, 128), 128)] = vv.astype(BF)
        return carry

    def next_x(k):
        for h in range(2):
            sent(half(rx.at[k], h), z_sent[0][k][h])
        signal(xfree.at[k], to_x)
        reduce_x(1, k)

    outs = []

    def out_copy(src, dst):
        copy = pltpu.make_async_copy(src, dst, lsem.at[4 + len(outs)])
        copy.start()
        outs.append(copy)

    def finish_out_weights():
        total(2)
        for half in range(2):
            out_copy(quarter(2, y * 2 + core)[half], w2s_ref.at[:, pl.ds(half * 1024, 1024)])
        total(3)
        out_copy(quarter(3, y * 2 + core)[0], wds_ref)

    reduce_z(0, 3, False, 0)
    grad_ff_in()
    core_send(1)
    reduce_z(0, 3, False, 1)
    reduce_z(0, 3, True, 0)
    lax.fori_loop(0, 1, attend_back, 0)
    y_send(1)
    reduce_z(0, 3, True, 1)
    reduce_z(0, 2, False, 0)
    reduce_z(0, 2, False, 1)
    sends_done()
    grad_ff_out()
    grad_dense()
    reduce_z(0, 1, False, 0)
    pl.semaphore_wait(cfree.at[0], 1)
    core_send(2)
    core_send(3)
    reduce_z(0, 1, False, 1)
    lax.fori_loop(1, 2, attend_back, 0)
    for i in range(4):
        rows = slice(i * PAIR, (i + 1) * PAIR)
        jg[rows, 0:256] = turn(jnp.transpose(o_t[:, rows]) * SCALE, rows, -1.0).astype(BF)

    reduce_z(0, 2, True, 0)
    reduce_z(0, 2, True, 1)
    reduce_z(0, 1, True, 0)
    y_send(2)
    y_send(3)
    exchange(1, a1, R_A1, True)
    exchange(1, a1, R_A1, False)
    reduce_z(0, 1, True, 1)
    for k in range(4):
        partial_ff(zp[k])
    for k in range(4):
        partial_attn(zp[k])
    next_x(3)
    next_x(2)
    next_x(1)
    for h in range(2):
        got(half(rx.at[0], h), R_X[0] + h)
        x_sent[0][0][h].wait_send()
    outp[rows_of(cx, BLK), :] = rx[0]
    signal(xfree.at[0], to_x)
    reduce_x(1, 0)
    total_o = outp[rows_of(cx, BLK), :].astype(F32) + outp[rows_of(c, BLK), :].astype(F32)
    out_ref[...] = (x_ref[...].astype(F32) + out_bias + reduced(0, total_o)).astype(BF)

    reduce_z(1, 3, False, 0)
    grad_joint()
    core_send(0)
    reduce_z(1, 3, False, 1)
    y_send(0)
    reduce_z(1, 3, True, 0)
    reduce_z(1, 2, False, 0)
    reduce_z(1, 2, False, 1)
    reduce_z(1, 1, False, 0)
    reduce_z(1, 1, False, 1)
    reduce_z(1, 3, True, 1)
    reduce_z(1, 2, True, 0)
    reduce_z(1, 2, True, 1)
    reduce_z(1, 1, True, 0)
    exchange(0, aq, R_AQ, True)
    exchange(0, aq, R_AQ, False)
    reduce_z(1, 1, True, 1)

    for h in range(2):
        got(half(rx.at[0], h), R_X[1] + h)
    ng = reduced(1, rx[0].astype(F32) + gb[rows_of(c, BLK), :].astype(F32))
    xhat, inv = norm_parts()
    e = ng * gain
    m1 = jnp.mean(e, axis=1, keepdims=True)
    m2 = jnp.mean(e * xhat, axis=1, keepdims=True)
    xgrad_ref[...] = (g_ref[...].astype(F32) + (e - m1 - xhat * m2) * inv).astype(BF)
    pkc[c, 0:16, :] = as_rows(jnp.sum(ng * xhat, axis=0, keepdims=True))
    pkc[c, 16:32, :] = as_rows(jnp.sum(ng, axis=0, keepdims=True))
    pkc[c, 32:40, :] = as_rows(svec[1:2, 1024:2048])
    for p in ctx_peers:
        pending.append(send(pkc.at[c], pkc.at[c], R_PC + c, (dp, p)))
    finish_out_weights()

    for p in ctx_peers:
        got(pkc.at[p], R_PC + p)
    norm_sum = pkc[0, 0:32, :]
    for i in range(1, NC):
        norm_sum = norm_sum + pkc[i, 0:32, :]
    pkd[dp, 0:32, :] = norm_sum
    for i in range(NC):
        pkd[dp, 32 + i * 8 : 40 + i * 8, :] = pkc[i, 32:40, :]
    pkd[dp, 96:112, :] = as_rows(svec[0:1, :])
    pkd[dp, 112:120, :] = as_rows(svec[1:2, 0:1024])
    for p in dp_peers:
        pending.append(send(pkd.at[dp], pkd.at[dp], R_PD + dp, (p, c)))

    for p in ctx_peers:
        got(a1.at[p], R_A1 + p)
    out_copy(a1, a1_ref)
    for p in dp_peers:
        got(pkd.at[p], R_PD + p)
    small_ref[...] = pkd[0] + pkd[1] + pkd[2] + pkd[3]
    for p in ctx_peers:
        got(aq.at[p], R_AQ + p)
    out_copy(aq, aq_ref)

    for s in pending:
        s.wait_send()
    for h in range(2):
        for k in (3, 2, 1):
            x_sent[0][k][h].wait_send()
            sent(half(rx.at[k], h), z_sent[1][k][h])
        for k in range(4):
            x_sent[1][k][h].wait_send()
    for t in range(4):
        sent(whole(t), y_sent[t])
    for copy in outs:
        copy.wait()


def finish_kernel(
    out_in,
    xgrad_in,
    small,
    w2s_in,
    wds_in,
    a1_in,
    aq_in,
    out_ref,
    xgrad_ref,
    gain_ref,
    shift_ref,
    wqg_ref,
    bqg_ref,
    wdg_ref,
    bd_ref,
    w1g_ref,
    b1_ref,
    w2g_ref,
    b2_ref,
    w2s,
    wds,
    a1,
    aq,
    w2w,
    wdw,
    w1w,
    wqw,
    rows_o,
    rows_x,
    sems,
):
    dp = lax.axis_index("dp")
    c = lax.axis_index("ctx")
    me = dp * NC + c
    used = []

    def move(src, dst):
        copy = pltpu.make_async_copy(src, dst, sems.at[len(used)])
        copy.start()
        used.append(copy)
        return copy

    pairs = ((wds_in, wds), (out_in, rows_o), (xgrad_in, rows_x), (w2s_in, w2s), (a1_in, a1), (aq_in, aq))
    loads = [move(*p) for p in pairs]
    stores = []
    loads[0].wait()
    wdw[...] = wds[...].astype(F32)
    stores.append(move(wdw, wdg_ref))
    loads[1].wait()
    stores.append(move(rows_o, out_ref))
    loads[2].wait()
    stores.append(move(rows_x, xgrad_ref))
    loads[3].wait()
    w2w[...] = w2s[...].astype(F32)
    stores.append(move(w2w, w2g_ref))
    loads[4].wait()
    for q in range(ND):
        for i in range(NC):
            w1w[:, q * 2048 + i * 256 : q * 2048 + (i + 1) * 256] = a1[i, :, q * 256 : (q + 1) * 256].astype(F32)
    stores.append(move(w1w, w1g_ref))
    loads[5].wait()
    for o in range(12):
        for i in range(NC // 2):
            both = [aq[2 * i + j, :, o * 64 : (o + 1) * 64].astype(F32) for j in range(2)]
            wqw[:, o * 512 + i * 128 : o * 512 + (i + 1) * 128] = jnp.concatenate(both, 1)
    stores.append(move(wqw, wqg_ref))

    def own_64(first):
        row = small[pl.ds(first + me // 2, 1), :]
        return jnp.where(me % 2 == 0, row[:, 0:64], row[:, 64:128]).reshape(64)

    gain_ref[...] = own_64(0)
    shift_ref[...] = own_64(16)
    summed = own_64(96)
    bd_ref[...] = summed
    b2_ref[...] = summed
    rows = small[pl.ds(112 + dp * 2, 2), :]
    b1_ref[...] = jnp.concatenate([rows[0:1], rows[1:2]], 1).reshape(256)

    picked = []
    for j in range(3):
        head = me * 3 + j
        o, i = head // NC, head % NC
        row = small[pl.ds(32 + i * 8 + o // 2, 1), :]
        picked.append(jnp.where(o % 2 == 0, row[:, 0:64], row[:, 64:128]))
    bqg_ref[...] = jnp.concatenate(picked, 1).reshape(192)
    for copy in stores:
        copy.wait()


def fast_device(inputs, positions, seq_ids, ln_gain, ln_bias, w_qkv, b_qkv, w_dense, b_dense, w_fc1, b_fc1, w_fc2, b_fc2, cotangent):
    width = inputs.shape[2]
    vm = pl.BlockSpec(memory_space=pltpu.VMEM)
    hbm = pl.BlockSpec(memory_space=pl.ANY)
    dma = pltpu.SemaphoreType.DMA
    reg = pltpu.SemaphoreType.REGULAR
    sd = jax.ShapeDtypeStruct
    parts = pl.pallas_call(
        layer_kernel,
        out_shape=(
            sd((BLK, width), BF),
            sd((BLK, width), BF),
            sd((120, 128), F32),
            sd((256, 2048), BF),
            sd((64, 2048), BF),
            sd((NC, 64, 1024), BF),
            sd((NC, 64, 768), BF),
        ),
        in_specs=[vm] * 10 + [hbm] * 4,
        out_specs=(vm, vm, vm, hbm, hbm, hbm, hbm),
        scratch_shapes=[
            pltpu.VMEM((TOK, 2048), BF),
            pltpu.VMEM((TOK, 2048), BF),
            pltpu.VMEM((2048, 768), BF),
            pltpu.VMEM((2048, 1024), BF),
            pltpu.VMEM((2048, 1024), BF),
            pltpu.VMEM((256, 2048), BF),
            pltpu.VMEM((ND, 16, 512), BF),
            pltpu.VMEM((NC, 8, BLK), jnp.int32),
            pltpu.VMEM((TOK, 128), F32),
            pltpu.VMEM((TOK, 128), F32),
            pltpu.VMEM((1, TOK), jnp.int32),
            pltpu.VMEM((4, TOK, 64), BF),
            pltpu.VMEM((4, TOK, 64), BF),
            pltpu.VMEM((4, TOK, 64), BF),
            pltpu.VMEM((256, TOK), F32),
            pltpu.VMEM((4, 1, TOK), F32),
            pltpu.VMEM((4, 1, TOK), F32),
            pltpu.VMEM((TOK, 256), BF),
            pltpu.VMEM((TOK, 1024), BF),
            pltpu.VMEM((TOK, 1024), BF),
            pltpu.VMEM((4, TOK, 64), BF),
            pltpu.VMEM((TOK, 768), BF),
            pltpu.VMEM((2, TOK, 128), F32),
            pltpu.VMEM((8, 2048), F32),
            pltpu.VMEM((TOK, 2048), BF),
            pltpu.VMEM((4, BLK, 2048), BF),
            pltpu.VMEM((5, BLK, 2048), BF),
            pltpu.VMEM((2, 512, 1024), BF),
            pltpu.VMEM((2, 512, 768), BF),
            pltpu.VMEM((2, 64, 2048), BF),
            pltpu.VMEM((NC, 64, 1024), BF),
            pltpu.VMEM((NC, 64, 768), BF),
            pltpu.VMEM((NC, 40, 128), F32),
            pltpu.VMEM((ND, 120, 128), F32),
            pltpu.VMEM((2048, 1024), BF),
            dma((N_SEND,)),
            dma((N_RECV,)),
            dma((9,)),
            reg((4,)),
            reg((5,)),
            reg((1,)),
            reg((4,)),
        ],
        compiler_params=pltpu.CompilerParams(
            collective_id=0, has_side_effects=True, vmem_limit_bytes=63 * 1024 * 1024
        ),
        name="layer",
    )(
        inputs[0], cotangent[0], seq_ids, positions, ln_gain, ln_bias, b_dense, b_fc2, b_qkv, b_fc1, w_qkv, w_fc1, w_fc2, w_dense
    )
    done = pl.pallas_call(
        finish_kernel,
        out_shape=(
            sd((BLK, width), BF),
            sd((BLK, width), BF),
            sd((64,), F32),
            sd((64,), F32),
            sd((64, 6144), F32),
            sd((192,), F32),
            sd((64, 2048), F32),
            sd((64,), F32),
            sd((64, 8192), F32),
            sd((256,), F32),
            sd((256, 2048), F32),
            sd((64,), F32),
        ),
        in_specs=[hbm, hbm, vm, hbm, hbm, hbm, hbm],
        out_specs=(hbm, hbm, vm, vm, hbm, vm, hbm, vm, hbm, vm, hbm, vm),
        scratch_shapes=[
            pltpu.VMEM((256, 2048), BF),
            pltpu.VMEM((64, 2048), BF),
            pltpu.VMEM((NC, 64, 1024), BF),
            pltpu.VMEM((NC, 64, 768), BF),
            pltpu.VMEM((256, 2048), F32),
            pltpu.VMEM((64, 2048), F32),
            pltpu.VMEM((64, 8192), F32),
            pltpu.VMEM((64, 6144), F32),
            pltpu.VMEM((BLK, 2048), BF),
            pltpu.VMEM((BLK, 2048), BF),
            dma((12,)),
        ],
        compiler_params=pltpu.CompilerParams(vmem_limit_bytes=62 * 1024 * 1024),
        name="finish",
    )(*parts)
    return (done[0][None], done[1][None]) + tuple(done[2:])


def solution(mesh):
    placed = (
        P("dp", "ctx", None),
        P("dp", "ctx"),
        P("dp", "ctx"),
        P("dp"),
        P("dp"),
        P("dp", None),
        P("dp"),
        P("dp", None),
        P("dp"),
        P("dp", None),
        P("dp"),
        P("dp", None),
        P("dp"),
        P("dp", "ctx", None),
    )
    fits = mesh.shape["dp"] == ND and mesh.shape["ctx"] == NC
    return jax.shard_map(
        fast_device if fits else per_device,
        mesh=mesh,
        in_specs=placed,
        out_specs=(
            P("dp", "ctx", None),
            P("dp", "ctx", None),
            P(("dp", "ctx")),
            P(("dp", "ctx")),
            P(("dp", "ctx"), None),
            P(("dp", "ctx")),
            P(("dp", "ctx"), None),
            P(("dp", "ctx")),
            P(("dp", "ctx"), None),
            P(("dp", "ctx")),
            P(("dp", "ctx"), None),
            P(("dp", "ctx")),
        ),
        check_vma=False,
    )
```
